256 devices in a mesh: ctx: 32 (over z_lo, y, core), head: 8 (over z_hi, x).
Axes of the slice: x: 4, y: 4, z: 8 (z_hi: 2, z_lo: 4; z = z_hi * 4 + z_lo), core: 2. Of those that a mesh axis runs over, the one named last changes fastest.
Arguments:
- queries: bfloat16 [16384, 4096], P('ctx', 'head'), may hold values from -6 to 6
- keys: bfloat16 [16384, 1024], P('ctx', 'head'), may hold values from -6 to 6
- values: bfloat16 [16384, 1024], P('ctx', 'head'), may hold values from -6 to 6
- out_weight: bfloat16 [4096, 8192], P(None, 'head'), may hold values from -0.375 to 0.375
Outputs:
- projected: bfloat16 [16384, 8192], P('ctx', 'head')
The draws below stay inside these ranges and needn't reach their ends.
All inputs are finite; a program needn't handle non-finite values.
Results may differ from the reference program's by a relative error of at most 0.0075.
Values may be sent and summed in bfloat16 or wider, within the bound.
No kernel may reach another device: no remote copies, remote signals or barrier semaphores. Data moves between devices by JAX's collectives and lax.ppermute only.
A program may use at most 64 MiB of HBM per device.

```python
import math
import jax
import jax.numpy as jnp
from jax import lax

DH = 128
QPK = 4
D = 8192
KV_HEADS = 8
HEADS = 32
SEQ = 16384


def row_scaled(key, shape, scale_low, scale_high):
    key_base, key_scale = jax.random.split(key)
    base_draw = jax.random.normal(key_base, shape, jnp.float32)
    log_scale = jax.random.uniform(key_scale, (shape[0], 1), jnp.float32, jnp.log(scale_low), jnp.log(scale_high))
    return jnp.clip(base_draw * jnp.exp(log_scale), -6.0, 6.0)


def draw_queries(key, part):
    key = jax.random.fold_in(key, 11)
    drawn = row_scaled(key, (SEQ, HEADS * DH), 0.4, 4.0)
    return drawn.astype(jnp.bfloat16)


def draw_keys(key, part):
    key = jax.random.fold_in(key, 23)
    drawn = row_scaled(key, (SEQ, KV_HEADS * DH), 0.3, 0.95)
    return drawn.astype(jnp.bfloat16)


def level_of(own_key, extent, pieces, least, largest):
    def one(dim, parts):
        steps = jax.random.uniform(jax.random.fold_in(jax.random.fold_in(own_key, 6), dim), (parts,), jnp.float32, least / len(pieces), largest / len(pieces))
        return jnp.repeat(jnp.exp(steps), extent[dim] // parts).reshape((-1,) + (1,) * (len(extent) - dim - 1))

    factor_of = one(*pieces[0])
    for cut in pieces[1:]:
        factor_of = factor_of * one(*cut)
    return factor_of


def centred(rng, shape, scale, limit, pieces=(), held_as=jnp.bfloat16):
    values = scale * jax.random.normal(rng, shape, jnp.float32)
    if pieces:
        values = values * level_of(rng, shape, pieces, -0.22, 0.18)
    return jnp.clip(values, -limit, limit).astype(held_as)


def setup_inputs(seed: int = 0) -> dict:
    arg_keys = jax.random.split(jax.random.key(seed), 5)
    return {
        "queries": draw_queries(jax.random.fold_in(arg_keys[4], 71), 0),
        "keys": draw_keys(jax.random.fold_in(arg_keys[4], 71), 0),
        "values": centred(arg_keys[2], (SEQ, KV_HEADS * DH), 1.0, 6.0, ((0, 32), (1, 8))),
        "out_weight": centred(arg_keys[3], (HEADS * DH, D), (HEADS * DH // 16) ** -0.5, 0.375, ((1, 8),)),
    }


def reference(queries, keys, values, out_weight):
    length_all = queries.shape[0]
    key_block = math.gcd(length_all, 512)
    score_scale = DH ** -0.5
    query_heads = queries.reshape(length_all, KV_HEADS, QPK, DH)
    key_pos = jnp.arange(length_all, dtype=jnp.int32)

    def one_block(block_index):
        offset = (block_index * key_block).astype(jnp.int32)
        query_rows = lax.dynamic_slice_in_dim(query_heads, offset, key_block, 0)
        query_pos = offset + jnp.arange(key_block, dtype=jnp.int32)
        allowed = (key_pos[None, :] <= query_pos[:, None])[:, None, :]
        head_outputs = []
        for group in range(KV_HEADS):
            key_rows = keys[:, group * DH:(group + 1) * DH].astype(jnp.float32)
            value_rows = values[:, group * DH:(group + 1) * DH].astype(jnp.float32)
            scores = jnp.einsum("rqd,nd->rqn", query_rows[:, group].astype(jnp.float32), key_rows) * score_scale
            scores = jnp.where(allowed, scores, -1e30)
            row_max = jnp.max(scores, axis=-1, keepdims=True)
            probs = jnp.where(allowed, jnp.exp(scores - row_max), 0.0)
            row_total = jnp.sum(probs, axis=-1, keepdims=True)
            rounded = lax.optimization_barrier(probs.astype(jnp.bfloat16))
            weighted = jnp.einsum("rqn,nd->rqd", rounded.astype(jnp.float32), value_rows) / row_total
            head_outputs.append(weighted.astype(jnp.bfloat16).reshape(key_block, QPK * DH))
        attended = jnp.concatenate(head_outputs, axis=1)
        return jnp.dot(attended, out_weight, preferred_element_type=jnp.float32).astype(jnp.bfloat16)

    projected = lax.map(one_block, jnp.arange(length_all // key_block, dtype=jnp.int32))
    return projected.reshape(length_all, out_weight.shape[1])
```

```python
import math

import jax
import jax.numpy as jnp
from jax import lax
from jax.experimental import pallas as pl
from jax.experimental.pallas import tpu as pltpu
from jax.sharding import PartitionSpec as P

DH = 128
QPK = 4
SCALE2 = math.log2(math.e) * DH ** (-0.5)
NEG = -1e30

NZ, NY, NC = 4, 4, 2
NH, NX = 2, 4
VMEM_LIMIT = 40 * 2**20


def ctx_id(z, y, c):
    return (z * NY + y) * NC + c


def ctx_permute(x, target):
    pairs = []
    for z in range(NZ):
        for y in range(NY):
            for c in range(NC):
                to = target(z, y, c)
                if to is not None:
                    pairs.append((ctx_id(z, y, c), ctx_id(*to)))
    return lax.ppermute(x, "ctx", pairs)


def head_permute(x, dz, dx):
    pairs = [
        (h * NX + i, (h + dz) % NH * NX + (i + dx) % NX) for h in range(NH) for i in range(NX)
    ]
    return lax.ppermute(x, "head", pairs)


def dot_nt(a, b):
    return lax.dot_general(a, b, (((1,), (1,)), ((), ())), preferred_element_type=jnp.float32)


def with_ones(values):
    return jnp.concatenate([values, jnp.ones_like(values)], axis=1)


TILE = 256


def own_kernel(info, q_own, q_oth, kv, m_out, acc_out):
    keys = kv[:, :DH]
    values = with_ones(kv[:, DH:])
    length = kv.shape[0]
    for h in range(QPK):
        for r in range(0, length, TILE):
            q = q_own[r : r + TILE, h * DH : (h + 1) * DH]
            s = dot_nt(q, keys) * SCALE2
            row = r + lax.broadcasted_iota(jnp.int32, s.shape, 0)
            col = lax.broadcasted_iota(jnp.int32, s.shape, 1)
            s = jnp.where(col <= row, s, NEG)
            m = jnp.broadcast_to(jnp.max(s, axis=1, keepdims=True), (TILE, DH))
            p = jnp.exp2(s - m[:, :1]).astype(jnp.bfloat16)
            m_out[h, r : r + TILE, :] = m
            acc_out[h, r : r + TILE, :] = jnp.dot(p, values, preferred_element_type=jnp.float32)

    @pl.when(info[0] == 0)
    def _():
        for h in range(QPK):
            for r in range(0, length, TILE):
                q = q_oth[r : r + TILE, h * DH : (h + 1) * DH]
                s = dot_nt(q, keys) * SCALE2
                m = jnp.broadcast_to(jnp.max(s, axis=1, keepdims=True), (TILE, DH))
                p = jnp.exp2(s - m[:, :1]).astype(jnp.bfloat16)
                m_out[QPK + h, r : r + TILE, :] = m
                acc_out[QPK + h, r : r + TILE, :] = jnp.dot(
                    p, values, preferred_element_type=jnp.float32
                )

    @pl.when(info[0] != 0)
    def _():
        m_out[QPK:] = jnp.full((QPK, length, DH), NEG, jnp.float32)
        acc_out[QPK:] = jnp.zeros((QPK, length, 2 * DH), jnp.float32)


def update(q, keys, values, m_out, acc_out, slot, r):
    rows = pl.ds(r, TILE)
    m_old = m_out[slot, rows, :]
    s = [dot_nt(q, k) * SCALE2 for k in keys]
    top = jnp.max(s[0], axis=1, keepdims=True)
    for one in s[1:]:
        top = jnp.maximum(top, jnp.max(one, axis=1, keepdims=True))
    m_new = jnp.maximum(m_old, top)
    lane = m_new[:, :1]
    added = None
    for one, v in zip(s, values):
        p = jnp.exp2(one - lane).astype(jnp.bfloat16)
        o = jnp.dot(p, v, preferred_element_type=jnp.float32)
        added = o if added is None else added + o
    shrink = jnp.exp2(m_old - m_new)
    shrink = jnp.concatenate([shrink, shrink], axis=1)
    m_out[slot, rows, :] = m_new
    acc_out[slot, rows, :] = acc_out[slot, rows, :] * shrink + added


def plane_kernel(info, q_own, q_oth, kv_own, kv_r, kv_l, kv_f1, kv_f2, m_in, acc_in, m_out, acc_out):
    m_out[...] = m_in[...]
    acc_out[...] = acc_in[...]

    @pl.when(info[0] != 0)
    def _():
        refs = (kv_own, kv_r, kv_l, kv_f1, kv_f2)
        keys = jnp.concatenate([ref[:, :DH] for ref in refs], axis=0)
        values = with_ones(jnp.concatenate([ref[:, DH:] for ref in refs], axis=0))
        for t, q_ref in enumerate((q_own, q_oth)):
            for h in range(QPK):
                for r in range(0, q_ref.shape[0], TILE):
                    q = q_ref[r : r + TILE, h * DH : (h + 1) * DH]
                    update(q, [keys], [values], m_out, acc_out, t * QPK + h, r)


def row_kernel(info, q_own, q_oth, kv_r, kv_l, kv_f1, kv_f2, m_in, acc_in, m_out, acc_out):
    m_out[...] = m_in[...]
    acc_out[...] = acc_in[...]
    for i, refs in enumerate(((kv_r,), (kv_l,), (kv_f1, kv_f2))):

        @pl.when(info[i] != 0)
        def _(refs=refs):
            keys = jnp.concatenate([ref[:, :DH] for ref in refs], axis=0)
            values = with_ones(jnp.concatenate([ref[:, DH:] for ref in refs], axis=0))
            for t, q_ref in enumerate((q_own, q_oth)):
                for h in range(QPK):
                    for r in range(0, q_ref.shape[0], TILE):
                        q = q_ref[r : r + TILE, h * DH : (h + 1) * DH]
                        update(q, [keys], [values], m_out, acc_out, t * QPK + h, r)


def part_kernel(m_in, acc_in, o_out, stat_out):
    stats = []
    for h in range(QPK):
        total = acc_in[QPK + h, :, DH:]
        some = total > 0.0
        o = acc_in[QPK + h, :, :DH] / jnp.where(some, total, 1.0)
        o_out[:, h * DH : (h + 1) * DH] = o.astype(jnp.bfloat16)
        log_total = m_in[QPK + h] + jnp.log2(jnp.where(some, total, 1.0))
        stats.append(jnp.where(some, log_total, NEG)[:, : DH // QPK])
    stat_out[...] = jnp.concatenate(stats, axis=1)


def join_kernel(m_in, acc_in, o_in, stat_in, out):
    for h in range(QPK):
        m = m_in[h]
        theirs = jnp.broadcast_to(stat_in[:, h * (DH // QPK) : h * (DH // QPK) + 1], m.shape)
        top = jnp.maximum(m, theirs)
        a = jnp.exp2(m - top)
        b = jnp.exp2(theirs - top)
        columns = slice(h * DH, (h + 1) * DH)
        o = acc_in[h, :, :DH] * a + o_in[:, columns].astype(jnp.float32) * b
        out[:, columns] = (o / (acc_in[h, :, DH:] * a + b)).astype(jnp.bfloat16)


VM = pl.BlockSpec(memory_space=pltpu.VMEM)
SM = pl.BlockSpec(memory_space=pltpu.SMEM)


def call(kernel, out_shape, *args, scalars=0, flops=0, aliases=None):
    size = sum(a.size * a.dtype.itemsize for a in args)
    many = isinstance(out_shape, tuple)
    return pl.pallas_call(
        kernel,
        out_shape=out_shape,
        in_specs=[SM] * scalars + [VM] * (len(args) - scalars),
        out_specs=tuple(VM for _ in out_shape) if many else VM,
        input_output_aliases=aliases or {},
        cost_estimate=pl.CostEstimate(flops=flops, bytes_accessed=size, transcendentals=0),
        compiler_params=pltpu.CompilerParams(vmem_limit_bytes=VMEM_LIMIT),
    )(*args)


def project(which, pieces, out_weight, so_far, out_type):
    refs = [block for piece in pieces for block in piece]
    counts = [len(piece) for piece in pieces]
    rows, depth = sum(b.shape[0] for b in pieces[0]), pieces[0][0].shape[1]
    columns = out_weight.shape[1]

    def kernel(which_ref, *args):
        parts = args[: len(refs)]
        w_ref = args[len(refs)]
        before = args[len(refs) + 1] if so_far is not None else None
        out, total = args[-2], args[-1]
        step = pl.program_id(0)
        first = 0
        for k, count in enumerate(counts):

            @pl.when(step == k)
            def _(k=k, blocks=parts[first : first + count]):
                start = 0
                for block in blocks:
                    at = slice(start, start + block.shape[0])
                    start += block.shape[0]
                    o = jnp.dot(block[...], w_ref[...], preferred_element_type=jnp.float32)
                    if k > 0:
                        o = total[at, :] + o
                    elif before is not None:
                        o = before[at, :] + o
                    if k == len(counts) - 1:
                        out[at, :] = o.astype(out_type)
                    else:
                        total[at, :] = o

            first += count

    whole = lambda a: pl.BlockSpec(a.shape, lambda k, which_ref: (0, 0))
    inputs = refs + [out_weight] + ([so_far] if so_far is not None else [])
    specs = [whole(a) for a in refs]
    specs.append(pl.BlockSpec((depth, columns), lambda k, which_ref: (which_ref[k], 0)))
    if so_far is not None:
        specs.append(whole(so_far))
    return pl.pallas_call(
        kernel,
        out_shape=jax.ShapeDtypeStruct((rows, columns), out_type),
        grid_spec=pltpu.PrefetchScalarGridSpec(
            num_scalar_prefetch=1,
            grid=(len(pieces),),
            in_specs=specs,
            out_specs=pl.BlockSpec((rows, columns), lambda k, which_ref: (0, 0)),
            scratch_shapes=[pltpu.VMEM((rows, columns), jnp.float32)],
        ),
        cost_estimate=pl.CostEstimate(
            flops=2 * rows * depth * columns * len(pieces),
            bytes_accessed=len(pieces) * depth * (columns + rows) * 2,
            transcendentals=0,
        ),
        compiler_params=pltpu.CompilerParams(vmem_limit_bytes=VMEM_LIMIT),
    )(which, *inputs)


def ring_y(x, low):
    half = x.shape[0] // 2
    up = lambda z, y, c: (z, (y + 1) % NY, c) if z >= low else None
    down = lambda z, y, c: (z, (y - 1) % NY, c) if z >= low else None
    r = ctx_permute(x, up)
    l = ctx_permute(x, down)
    return r, l, ctx_permute(r[:half], up), ctx_permute(l[half:], down)


def ring_x(x):
    half = x.shape[0] // 2
    r = head_permute(x, 0, 1)
    l = head_permute(x, 0, -1)
    return r, l, head_permute(r[:half], 0, 1), head_permute(l[half:], 0, -1)


def per_device(queries, keys, values, out_weight):
    rows = queries.shape[0]
    ctx = lax.axis_index("ctx")
    head = lax.axis_index("head")
    z, y, c = ctx // (NY * NC), ctx // NC % NY, ctx % NC
    i32 = lambda *v: jnp.stack([jnp.asarray(x, jnp.int32) for x in v])

    kv = jnp.concatenate([keys, values], axis=1)
    q_oth = ctx_permute(queries, lambda z, y, c: (z, y, 1 - c))
    lower = [
        ctx_permute(kv, lambda z, y, c, d=d: (z + d, y, c) if z + d < NZ else None)
        for d in range(1, NZ)
    ]
    state_shape = (
        jax.ShapeDtypeStruct((2 * QPK, rows, DH), jnp.float32),
        jax.ShapeDtypeStruct((2 * QPK, rows, 2 * DH), jnp.float32),
    )
    unit = 2 * 2 * 2 * QPK * rows * rows * DH
    r, l, f1, f2 = ring_y(kv, 0)
    m, acc = call(
        own_kernel, state_shape, i32(c), queries, q_oth, kv, scalars=1, flops=unit
    )
    m, acc = call(
        row_kernel,
        state_shape,
        i32(y >= 1, y >= 3, y >= 2),
        queries, q_oth, r, l, f1, f2, m, acc,
        scalars=1, flops=3 * unit, aliases={7: 0, 8: 1},
    )
    for d, piece in enumerate(lower, 1):
        r, l, f1, f2 = ring_y(piece, d)
        m, acc = call(
            plane_kernel,
            state_shape,
            i32(z >= d),
            queries, q_oth, piece, r, l, f1, f2, m, acc,
            scalars=1, flops=4 * unit, aliases={8: 0, 9: 1},
        )

    o_part, stat = call(
        part_kernel,
        (
            jax.ShapeDtypeStruct((rows, QPK * DH), jnp.bfloat16),
            jax.ShapeDtypeStruct((rows, DH), jnp.float32),
        ),
        m, acc,
    )
    swap = lambda z, y, c: (z, y, 1 - c)
    attended = call(
        join_kernel,
        jax.ShapeDtypeStruct((rows, QPK * DH), jnp.bfloat16),
        m, acc, ctx_permute(o_part, swap), ctx_permute(stat, swap),
    )

    far = head_permute(attended, 1, 0)
    hz, hx = head // NX, head % NX
    r, l, f1, f2 = ring_x(attended)
    order = lambda hz: i32(*[hz * NX + (hx + s) % NX for s in (0, -1, 1, 2)])
    total = project(order(hz), [[attended], [r], [l], [f1, f2]], out_weight, None, jnp.float32)
    r, l, f1, f2 = ring_x(far)
    return project(order(1 - hz), [[far], [r], [l], [f1, f2]], out_weight, total, jnp.bfloat16)


def solution(mesh):
    return jax.shard_map(
        per_device,
        mesh=mesh,
        in_specs=(P("ctx", "head"), P("ctx", "head"), P("ctx", "head"), P(None, "head")),
        out_specs=P("ctx", "head"),
        check_vma=False,
    )
```

```python
import math

import jax
import jax.numpy as jnp
from jax import lax
from jax.experimental import pallas as pl
from jax.experimental.pallas import tpu as pltpu
from jax.sharding import PartitionSpec as P

DH = 128
QPK = 4
SCALE2 = math.log2(math.e) * DH ** (-0.5)
NEG = -1e30

NZ, NY, NC = 4, 4, 2
NH, NX = 2, 4

TILE = 256
LANES = 128 // (2 * QPK)


def ctx_id(z, y, c):
    return (z * NY + y) * NC + c


def ctx_permute(x, target):
    pairs = []
    for z in range(NZ):
        for y in range(NY):
            for c in range(NC):
                to = target(z, y, c)
                if to is not None:
                    pairs.append((ctx_id(z, y, c), ctx_id(*to)))
    return lax.ppermute(x, "ctx", pairs)


def head_permute(x, dz, dx):
    pairs = [
        (h * NX + i, (h + dz) % NH * NX + (i + dx) % NX) for h in range(NH) for i in range(NX)
    ]
    return lax.ppermute(x, "head", pairs)


def dot_nt(a, b):
    return lax.dot_general(a, b, (((1,), (1,)), ((), ())), preferred_element_type=jnp.float32)


def split_kv(blocks):
    keys = jnp.concatenate([b[:, :DH] for b in blocks], axis=0)
    values = jnp.concatenate([b[:, DH:] for b in blocks], axis=0)
    return keys, jnp.concatenate([values, jnp.ones_like(values)], axis=1)


def update(q_refs, blocks, acc_in, st_in, acc_out, st_out, mask=None):
    keys, values = split_kv(blocks)
    for r in range(0, q_refs[0].shape[0], TILE):
        rows = slice(r, r + TILE)
        packed = st_in[rows, :] if st_in is not None else jnp.zeros((TILE, 128), jnp.float32)
        lane = lax.broadcasted_iota(jnp.int32, packed.shape, 1)
        for t, q_ref in enumerate(q_refs):
            for h in range(QPK):
                slot = t * QPK + h
                at = slot * LANES
                s = dot_nt(q_ref[rows, h * DH : (h + 1) * DH], keys) * SCALE2
                if mask is not None:
                    s = mask(s, t, r)
                m = jnp.max(s, axis=1, keepdims=True)
                if st_in is not None:
                    m_old = packed[:, at : at + 1]
                    m = jnp.maximum(m, m_old)
                p = jnp.exp2(s - m)
                if mask is not None:
                    p = jnp.where(m > 0.5 * NEG, p, 0.0)
                o = jnp.dot(p.astype(jnp.bfloat16), values, preferred_element_type=jnp.float32)
                total = o[:, DH : DH + 1]
                o = o[:, :DH]
                if st_in is not None:
                    shrink = jnp.exp2(m_old - m)
                    total = total + packed[:, at + LANES // 2 : at + LANES // 2 + 1] * shrink
                    o = o + acc_in[slot, rows, :] * shrink
                acc_out[slot, rows, :] = o
                packed = jnp.where((lane >= at) & (lane < at + LANES // 2), m, packed)
                packed = jnp.where((lane >= at + LANES // 2) & (lane < at + LANES), total, packed)
        st_out[rows, :] = packed


def near_kernel(info, q_own, q_oth, *refs):
    row, lower, (acc, st) = refs[:5], refs[5:10], refs[10:]
    c, y, z = info[0], info[1], info[2]
    length = row[0].shape[0]

    def mask(s, t, r):
        i = r + lax.broadcasted_iota(jnp.int32, (s.shape[0], length), 0)
        j = lax.broadcasted_iota(jnp.int32, (s.shape[0], length), 1)
        own = s[:, :length]
        own = jnp.where(j <= i, own, NEG) if t == 0 else jnp.where(c == 0, own, NEG)
        parts = [own]
        for k, low in enumerate((1, 3, 2)):
            part = s[:, (k + 1) * length : (k + 2) * length]
            parts.append(jnp.where(y >= low, part, NEG))
        return jnp.concatenate(parts, axis=1)

    update((q_own, q_oth), [b[...] for b in row], None, None, acc, st, mask)

    @pl.when(z >= 1)
    def _():
        update((q_own, q_oth), [b[...] for b in lower], acc, st, acc, st)


def far_kernel(info, q_own, q_oth, *refs):
    pieces, (acc_in, st_in, acc, st) = refs[:3], refs[3:]
    z = info[2]
    half = pieces[0].shape[0] // 2

    @pl.when(z < 2)
    def _():
        acc[...] = acc_in[...]
        st[...] = st_in[...]

    @pl.when(z == 2)
    def _():
        update((q_own, q_oth), [b[:half] for b in pieces], acc_in, st_in, acc, st)

    @pl.when(z == 3)
    def _():
        update((q_own, q_oth), [b[...] for b in pieces], acc_in, st_in, acc, st)


def last_kernel(info, q_own, q_oth, f2, f3, acc_in, st_in, own_out, own_log, send, acc, st):
    z = info[2]

    @pl.when(z < 2)
    def _():
        acc[...] = acc_in[...]
        st[...] = st_in[...]

    @pl.when(z == 2)
    def _():
        update((q_own, q_oth), [f2[...]], acc_in, st_in, acc, st)

    @pl.when(z == 3)
    def _():
        update((q_own, q_oth), [f2[...], f3[...]], acc_in, st_in, acc, st)

    rows = own_out.shape[0]
    lane = lax.broadcasted_iota(jnp.int32, (rows, 128), 1)
    logs = [jnp.zeros((rows, 128), jnp.float32), jnp.zeros((rows, 128), jnp.float32)]
    for slot in range(2 * QPK):
        at = slot * LANES
        t, h = slot // QPK, slot % QPK
        m, total = st[:, at : at + 1], st[:, at + LANES // 2 : at + LANES // 2 + 1]
        some = total > 0.0
        total = jnp.where(some, total, 1.0)
        o = acc[slot] / total
        log_total = jnp.where(some, m + jnp.log2(total), NEG)
        logs[t] = jnp.where(lane // (128 // QPK) == h, log_total, logs[t])
        if t == 0:
            own_out[:, h * DH : (h + 1) * DH] = o
        else:
            send[:, h * DH : (h + 1) * DH] = o.astype(jnp.bfloat16)
    own_log[...] = logs[0]
    first = logs[1].astype(jnp.bfloat16).astype(jnp.float32)
    second = (logs[1] - first).astype(jnp.bfloat16).astype(jnp.float32)
    third = logs[1] - first - second
    which = lane % (128 // QPK)
    parts = jnp.where(which == 0, first, jnp.where(which == 1, second, third))
    send[:, QPK * DH :] = parts.astype(jnp.bfloat16)


def join_kernel(own_in, own_log, got, out):
    theirs = got[:, QPK * DH :].astype(jnp.float32)
    for h in range(QPK):
        at = h * (128 // QPK)
        a = own_log[:, at : at + 1]
        b = theirs[:, at : at + 1] + theirs[:, at + 1 : at + 2] + theirs[:, at + 2 : at + 3]
        top = jnp.maximum(a, b)
        a, b = jnp.exp2(a - top), jnp.exp2(b - top)
        share = 1.0 / (a + b)
        a, b = a * share, b * share
        columns = slice(h * DH, (h + 1) * DH)
        o = own_in[:, columns] * a + got[:, columns].astype(jnp.float32) * b
        out[:, columns] = o.astype(jnp.bfloat16)


VM = pl.BlockSpec(memory_space=pltpu.VMEM)
SM = pl.BlockSpec(memory_space=pltpu.SMEM)


def call(kernel, out_shape, *args, info=None, flops=0, scratch=()):
    size = sum(a.size * a.dtype.itemsize for a in args)
    many = isinstance(out_shape, tuple)
    first = [] if info is None else [info]
    return pl.pallas_call(
        kernel,
        out_shape=out_shape,
        in_specs=[SM] * len(first) + [VM] * len(args),
        out_specs=tuple(VM for _ in out_shape) if many else VM,
        scratch_shapes=scratch,
        cost_estimate=pl.CostEstimate(flops=flops, bytes_accessed=size, transcendentals=0),
        compiler_params=pltpu.CompilerParams(vmem_limit_bytes=40 * 2**20),
    )(*first, *args)


def project(info, pieces, out_weight, so_far, out_type):
    refs = [block for piece in pieces for block in piece]
    counts = [len(piece) for piece in pieces]
    rows, depth = sum(b.shape[0] for b in pieces[0]), pieces[0][0].shape[1]
    columns = out_weight.shape[1]
    width = 256

    def kernel(info_ref, *args):
        parts = args[: len(refs)]
        w_ref = args[len(refs)]
        before = args[len(refs) + 1] if so_far is not None else None
        out = args[-1]
        weights = [
            w_ref[pl.ds(pl.multiple_of(info_ref[k + 1] * depth, depth), depth), :]
            for k in range(len(counts))
        ]
        half = rows // 2
        for i in range(2):
            o = before[i * half : (i + 1) * half, :] if before is not None else None
            first = 0
            for k, count in enumerate(counts):
                a = parts[first + i][...] if count == 2 else parts[first][i * half : (i + 1) * half, :]
                first += count
                new = jnp.dot(a, weights[k], preferred_element_type=jnp.float32)
                o = new if o is None else o + new
            out[i * half : (i + 1) * half, :] = o.astype(out_type)

    specs = [pl.BlockSpec(a.shape, lambda n, info_ref: (0, 0)) for a in refs]
    specs.append(pl.BlockSpec((depth * len(pieces), width), lambda n, info_ref: (info_ref[0], n)))
    inputs = refs + [out_weight]
    tile = pl.BlockSpec((rows, width), lambda n, info_ref: (0, n))
    if so_far is not None:
        inputs.append(so_far)
        specs.append(tile)
    return pl.pallas_call(
        kernel,
        out_shape=jax.ShapeDtypeStruct((rows, columns), out_type),
        grid_spec=pltpu.PrefetchScalarGridSpec(
            num_scalar_prefetch=1, grid=(columns // width,), in_specs=specs, out_specs=tile
        ),
        cost_estimate=pl.CostEstimate(
            flops=2 * rows * depth * columns * len(pieces),
            bytes_accessed=len(pieces) * depth * (columns + rows) * 2,
            transcendentals=0,
        ),
        compiler_params=pltpu.CompilerParams(vmem_limit_bytes=56 * 2**20),
    )(info, *inputs)


def ring_y(x, low):
    half = x.shape[0] // 2
    up = lambda z, y, c: (z, (y + 1) % NY, c) if z >= low else None
    down = lambda z, y, c: (z, (y - 1) % NY, c) if z >= low else None
    r = ctx_permute(x, up)
    l = ctx_permute(x, down)
    return r, l, ctx_permute(r[:half], up), ctx_permute(l[half:], down)


def ring_x(x):
    half = x.shape[0] // 2
    r = head_permute(x, 0, 1)
    l = head_permute(x, 0, -1)
    return r, l, head_permute(r[:half], 0, 1), head_permute(l[half:], 0, -1)


def per_device(queries, keys, values, out_weight):
    rows = queries.shape[0]
    ctx = lax.axis_index("ctx")
    head = lax.axis_index("head")
    z, y, c = ctx // (NY * NC), ctx // NC % NY, ctx % NC
    i32 = lambda *v: jnp.stack([jnp.asarray(x, jnp.int32) for x in v])
    info = i32(c, y, z)
    swap = lambda z, y, c: (z, y, 1 - c)

    kv = jnp.concatenate([keys, values], axis=1)
    lower = [
        ctx_permute(kv, lambda z, y, c, d=d: (z + d, y, c) if z + d < NZ else None)
        for d in range(1, NZ)
    ]
    q_oth = ctx_permute(queries, swap)
    unit = 2 * 2 * 2 * QPK * rows * rows * DH
    state = (
        jax.ShapeDtypeStruct((2 * QPK, rows, DH), jnp.float32),
        jax.ShapeDtypeStruct((rows, 128), jnp.float32),
    )
    near = [kv, *ring_y(kv, 0), lower[0], *ring_y(lower[0], 1)]
    both = jnp.concatenate(lower[1:], axis=0)
    r, l, f2, f3 = ring_y(both, 2)
    acc, st = call(near_kernel, state, queries, q_oth, *near, info=info, flops=8 * unit)
    acc, st = call(far_kernel, state, queries, q_oth, both, r, l, acc, st, info=info, flops=6 * unit)
    own, own_log, send = call(
        last_kernel,
        (
            jax.ShapeDtypeStruct((rows, QPK * DH), jnp.float32),
            jax.ShapeDtypeStruct((rows, 128), jnp.float32),
            jax.ShapeDtypeStruct((rows, QPK * DH + 128), jnp.bfloat16),
        ),
        queries, q_oth, f2, f3, acc, st,
        info=info, flops=2 * unit,
        scratch=(pltpu.VMEM(state[0].shape, jnp.float32), pltpu.VMEM(state[1].shape, jnp.float32)),
    )
    attended = call(
        join_kernel,
        jax.ShapeDtypeStruct((rows, QPK * DH), jnp.bfloat16),
        own, own_log, ctx_permute(send, swap),
    )

    far = head_permute(attended, 1, 0)
    hz, hx = head // NX, head % NX
    which = lambda hz: i32(hz, *[(hx + s) % NX for s in (0, -1, 1, 2)])
    r, l, f1, f2 = ring_x(attended)
    total = project(which(hz), [[attended], [r], [l], [f1, f2]], out_weight, None, jnp.float32)
    r, l, f1, f2 = ring_x(far)
    return project(which(1 - hz), [[far], [r], [l], [f1, f2]], out_weight, total, jnp.bfloat16)


def solution(mesh):
    return jax.shard_map(
        per_device,
        mesh=mesh,
        in_specs=(P("ctx", "head"), P("ctx", "head"), P("ctx", "head"), P(None, "head")),
        out_specs=P("ctx", "head"),
        check_vma=False,
    )
```

```python
import math

import jax
import jax.numpy as jnp
from jax import lax
from jax.experimental import pallas as pl
from jax.experimental.pallas import tpu as pltpu
from jax.sharding import PartitionSpec as P

DH = 128
QPK = 4
SCALE2 = math.log2(math.e) * DH ** (-0.5)
NEG = -1e30

NZ, NY, NC = 4, 4, 2
NH, NX = 2, 4

TILE = 256
BESIDE = 4


def ctx_id(z, y, c):
    return (z * NY + y) * NC + c


def ctx_permute(x, target):
    pairs = []
    for z in range(NZ):
        for y in range(NY):
            for c in range(NC):
                to = target(z, y, c)
                if to is not None:
                    pairs.append((ctx_id(z, y, c), ctx_id(*to)))
    return lax.ppermute(x, "ctx", pairs)


def head_permute(x, dz, dx):
    pairs = [
        (h * NX + i, (h + dz) % NH * NX + (i + dx) % NX) for h in range(NH) for i in range(NX)
    ]
    return lax.ppermute(x, "head", pairs)


def dot_nt(a, b):
    return lax.dot_general(a, b, (((1,), (1,)), ((), ())), preferred_element_type=jnp.float32)


def load_kv(blocks, keys, values):
    at = 0
    for block in blocks:
        n = block.shape[0]
        keys[at : at + n, :] = block[:, :DH]
        values[at : at + n, :DH] = block[:, DH:]
        at += n
    values[:at, DH:] = jnp.ones((at, DH), jnp.bfloat16)
    return at


def sweep(slots, length, scores, rest):
    per = length // TILE

    def turn(i, _):
        def place(u):
            j = i * BESIDE + u
            return slots[0] + j // per, pl.multiple_of(j % per * TILE, TILE)

        s = scores(*place(0))
        for u in range(BESIDE):
            after = scores(*place(u + 1)) if u + 1 < BESIDE else None
            rest(*place(u), s)
            s = after
        return 0

    lax.fori_loop(0, (slots[1] - slots[0]) * per // BESIDE, turn, 0)


def update(q, keys, values, count, m_in, acc_in, m_out, acc_out):
    def scores(slot, r):
        return dot_nt(q[slot, pl.ds(r, TILE), :], keys[:count, :]) * SCALE2

    def rest(slot, r, s):
        rows = pl.ds(r, TILE)
        m_old = m_in[slot, rows, :]
        m = jnp.maximum(m_old, jnp.max(s, axis=1, keepdims=True))
        p = jnp.exp2(s - m[:, :1]).astype(jnp.bfloat16)
        o = jnp.dot(p, values[:count, :], preferred_element_type=jnp.float32)
        shrink = jnp.exp2(m_old - m)
        m_out[slot, rows, :] = m
        acc_out[slot, rows, :] = acc_in[slot, rows, :] * jnp.concatenate([shrink, shrink], axis=1) + o

    sweep((0, 2 * QPK), q.shape[1], scores, rest)


def row_kernel(info, q, own, r_ref, l_ref, f_ref, m_out, acc_out, keys, values, bias):
    c, y = info[0], info[1]
    n = own.shape[0]
    count = load_kv((own, r_ref, l_ref, f_ref), keys, values)
    for t in range(2):
        bias[t, :, :n] = jnp.full((8, n), jnp.where((t == 0) | (c == 0), 0.0, NEG), jnp.float32)
        for k, low in enumerate((1, 3, 2), 1):
            bias[t, :, k * n : (k + 1) * n] = jnp.full((8, n), jnp.where(y >= low, 0.0, NEG), jnp.float32)

        def scores(slot, r, t=t):
            s = dot_nt(q[slot, pl.ds(r, TILE), :], keys[:count, :]) * SCALE2 + bias[t, :1, :]
            if t == 0:
                i = r + lax.broadcasted_iota(jnp.int32, (TILE, n), 0)
                j = lax.broadcasted_iota(jnp.int32, (TILE, n), 1)
                s = jnp.concatenate([jnp.where(j <= i, s[:, :n], NEG), s[:, n:]], axis=1)
            return s

        def rest(slot, r, s):
            rows = pl.ds(r, TILE)
            m = jnp.broadcast_to(jnp.max(s, axis=1, keepdims=True), (TILE, DH))
            p = jnp.exp2(s - m[:, :1]).astype(jnp.bfloat16)
            o = jnp.dot(p, values[:count, :], preferred_element_type=jnp.float32)
            some = jnp.concatenate([m, m], axis=1) > 0.5 * NEG
            m_out[slot, rows, :] = m
            acc_out[slot, rows, :] = jnp.where(some, o, 0.0)

        sweep((t * QPK, (t + 1) * QPK), q.shape[1], scores, rest)


def plane_kernel(counts, info, q, *refs):
    blocks, (m_in, acc_in, m_out, acc_out, keys, values) = refs[:-6], refs[-6:]
    z = info[2]
    for kind in sorted(set(counts)):
        of = [k for k in range(NZ) if counts[k] == kind]

        @pl.when((z >= of[0]) & (z <= of[-1]))
        def _(kind=kind):
            if kind == 0:
                m_out[...] = m_in[...]
                acc_out[...] = acc_in[...]
            else:
                count = load_kv([b.at[: b.shape[0] * kind // 2] for b in blocks], keys, values)
                update(q, keys, values, count, m_in, acc_in, m_out, acc_out)


def share_kernel(m, acc, own_out, own_log, send):
    rows = own_out.shape[0]
    lane = lax.broadcasted_iota(jnp.int32, (rows, 128), 1)
    logs = [jnp.zeros((rows, 128), jnp.float32), jnp.zeros((rows, 128), jnp.float32)]
    for slot in range(2 * QPK):
        t, h = slot // QPK, slot % QPK
        total = acc[slot, :, DH:]
        some = total > 0.0
        total = jnp.where(some, total, 1.0)
        o = acc[slot, :, :DH] / total
        log_total = jnp.where(some, m[slot] + jnp.log2(total), NEG)
        logs[t] = jnp.where(lane // (128 // QPK) == h, log_total, logs[t])
        if t == 0:
            own_out[:, h * DH : (h + 1) * DH] = o
        else:
            send[:, h * DH : (h + 1) * DH] = o.astype(jnp.bfloat16)
    own_log[...] = logs[0]
    first = logs[1].astype(jnp.bfloat16).astype(jnp.float32)
    second = (logs[1] - first).astype(jnp.bfloat16).astype(jnp.float32)
    third = logs[1] - first - second
    which = lane % (128 // QPK)
    parts = jnp.where(which == 0, first, jnp.where(which == 1, second, third))
    send[:, QPK * DH :] = parts.astype(jnp.bfloat16)


def join_kernel(own_in, own_log, got, out):
    theirs = got[:, QPK * DH :].astype(jnp.float32)
    for h in range(QPK):
        at = h * (128 // QPK)
        a = own_log[:, at : at + 1]
        b = theirs[:, at : at + 1] + theirs[:, at + 1 : at + 2] + theirs[:, at + 2 : at + 3]
        top = jnp.maximum(a, b)
        a, b = jnp.exp2(a - top), jnp.exp2(b - top)
        share = 1.0 / (a + b)
        a, b = a * share, b * share
        columns = slice(h * DH, (h + 1) * DH)
        o = own_in[:, columns] * a + got[:, columns].astype(jnp.float32) * b
        out[:, columns] = o.astype(jnp.bfloat16)


VM = pl.BlockSpec(memory_space=pltpu.VMEM)
SM = pl.BlockSpec(memory_space=pltpu.SMEM)


def call(kernel, out_shape, *args, info=None, flops=0, scratch=()):
    size = sum(a.size * a.dtype.itemsize for a in args)
    many = isinstance(out_shape, tuple)
    first = [] if info is None else [info]
    return pl.pallas_call(
        kernel,
        out_shape=out_shape,
        in_specs=[SM] * len(first) + [VM] * len(args),
        out_specs=tuple(VM for _ in out_shape) if many else VM,
        scratch_shapes=scratch,
        cost_estimate=pl.CostEstimate(flops=flops, bytes_accessed=size, transcendentals=0),
        compiler_params=pltpu.CompilerParams(vmem_limit_bytes=32 * 2**20),
    )(*first, *args)


def project(info, pieces, out_weight, so_far, out_type):
    refs = [block for piece in pieces for block in piece]
    counts = [len(piece) for piece in pieces]
    rows, depth = sum(b.shape[0] for b in pieces[0]), pieces[0][0].shape[1]
    columns = out_weight.shape[1]

    def kernel(info_ref, *args):
        parts, w_ref = args[: len(refs)], args[len(refs)]
        before = args[len(refs) + 1] if so_far is not None else None
        out, total = args[-2], args[-1]
        step = pl.program_id(0)
        first = 0
        for k, count in enumerate(counts):

            @pl.when(step == k)
            def _(k=k, blocks=parts[first : first + count]):
                start = 0
                for block in blocks:
                    at = slice(start, start + block.shape[0])
                    start += block.shape[0]
                    o = jnp.dot(block[...], w_ref[...], preferred_element_type=jnp.float32)
                    if k > 0:
                        o = total[at, :] + o
                    elif before is not None:
                        o = before[at, :] + o
                    if k == len(counts) - 1:
                        out[at, :] = o.astype(out_type)
                    else:
                        total[at, :] = o

            first += count

    whole = lambda a: pl.BlockSpec(a.shape, lambda k, info_ref: (0, 0))
    inputs = refs + [out_weight] + ([so_far] if so_far is not None else [])
    specs = [whole(a) for a in refs]
    specs.append(pl.BlockSpec((depth, columns), lambda k, info_ref: (info_ref[k], 0)))
    if so_far is not None:
        specs.append(whole(so_far))
    return pl.pallas_call(
        kernel,
        out_shape=jax.ShapeDtypeStruct((rows, columns), out_type),
        grid_spec=pltpu.PrefetchScalarGridSpec(
            num_scalar_prefetch=1,
            grid=(len(pieces),),
            in_specs=specs,
            out_specs=pl.BlockSpec((rows, columns), lambda k, info_ref: (0, 0)),
            scratch_shapes=[pltpu.VMEM((rows, columns), jnp.float32)],
        ),
        cost_estimate=pl.CostEstimate(
            flops=2 * rows * depth * columns * len(pieces),
            bytes_accessed=len(pieces) * depth * (columns + rows) * 2,
            transcendentals=0,
        ),
        compiler_params=pltpu.CompilerParams(vmem_limit_bytes=32 * 2**20),
    )(info, *inputs)


def ring_y(x, low):
    shift = lambda d: ctx_permute(x, lambda z, y, c: (z, (y + d) % NY, c) if z >= low else None)
    return shift(1), shift(-1), shift(2)


def per_device(queries, keys, values, out_weight):
    rows = queries.shape[0]
    ctx = lax.axis_index("ctx")
    head = lax.axis_index("head")
    z, y, c = ctx // (NY * NC), ctx // NC % NY, ctx % NC
    i32 = lambda *v: jnp.stack([jnp.asarray(x, jnp.int32) for x in v])
    info = i32(c, y, z)
    swap = lambda z, y, c: (z, y, 1 - c)

    kv = jnp.concatenate([keys, values], axis=1)
    lower = [
        ctx_permute(kv, lambda z, y, c, d=d: (z + d, y, c) if z + d < NZ else None)
        for d in range(1, NZ)
    ]
    q_own = queries.reshape(rows, QPK, DH).transpose(1, 0, 2)
    q = jnp.concatenate([q_own, ctx_permute(q_own, swap)], axis=0)
    unit = 2 * 2 * 2 * QPK * rows * rows * DH
    state = (
        jax.ShapeDtypeStruct((2 * QPK, rows, DH), jnp.float32),
        jax.ShapeDtypeStruct((2 * QPK, rows, 2 * DH), jnp.float32),
    )

    def scratch(chunks):
        return [
            pltpu.VMEM((chunks * rows, DH), jnp.bfloat16),
            pltpu.VMEM((chunks * rows, 2 * DH), jnp.bfloat16),
        ]

    def planes(counts, q, blocks, m, acc):
        chunks = sum(b.shape[0] for b in blocks) // rows
        return call(
            lambda *refs: plane_kernel(counts, *refs),
            state, q, *blocks, m, acc, info=info, flops=chunks * unit, scratch=scratch(chunks),
        )

    m, acc = call(
        row_kernel,
        state,
        q, kv, *ring_y(kv, 0),
        info=info, flops=4 * unit, scratch=[*scratch(4), pltpu.VMEM((2, 8, 4 * rows), jnp.float32)],
    )
    near = [lower[0], *ring_y(lower[0], 1)]
    both = jnp.concatenate(lower[1:], axis=0)
    r, l, f = ring_y(both, 2)
    near[0], both = lax.optimization_barrier((near[0], both))
    m, acc = planes((0, 2, 2, 2), q, near, m, acc)
    m, acc = planes((0, 0, 1, 2), q, [both, r, l], m, acc)
    m, acc = planes((0, 0, 1, 2), q, [f], m, acc)
    own, own_log, send = call(
        share_kernel,
        (
            jax.ShapeDtypeStruct((rows, QPK * DH), jnp.float32),
            jax.ShapeDtypeStruct((rows, 128), jnp.float32),
            jax.ShapeDtypeStruct((rows, QPK * DH + 128), jnp.bfloat16),
        ),
        m, acc,
    )
    attended = call(
        join_kernel,
        jax.ShapeDtypeStruct((rows, QPK * DH), jnp.bfloat16),
        own, own_log, ctx_permute(send, swap),
    )

    hz, hx = head // NX, head % NX
    which = lambda hz, *shifts: i32(*[hz * NX + (hx + s) % NX for s in shifts])
    half = rows // 2
    far = head_permute(attended, 1, 0)
    r, l = head_permute(attended, 0, 1), head_permute(attended, 0, -1)
    f1, f2 = head_permute(r[:half], 0, 1), head_permute(l[half:], 0, -1)
    far_r, far_l = head_permute(far, 0, 1), head_permute(far, 0, -1)
    total = project(
        which(hz, 0, -1, 1, 2), [[attended], [r], [l], [f1, f2]], out_weight, None, jnp.float32
    )
    far_r, far_l, total = lax.optimization_barrier((far_r, far_l, total))
    f1, f2 = head_permute(far_r[:half], 0, 1), head_permute(far_l[half:], 0, -1)
    total = project(which(1 - hz, 0, -1, 1), [[far], [far_r], [far_l]], out_weight, total, jnp.float32)
    return project(which(1 - hz, 2), [[f1, f2]], out_weight, total, jnp.bfloat16)


def solution(mesh):
    return jax.shard_map(
        per_device,
        mesh=mesh,
        in_specs=(P("ctx", "head"), P("ctx", "head"), P("ctx", "head"), P(None, "head")),
        out_specs=P("ctx", "head"),
        check_vma=False,
    )
```

```python
import math

import jax
import jax.numpy as jnp
from jax import lax
from jax.experimental import pallas as pl
from jax.experimental.pallas import tpu as pltpu
from jax.sharding import PartitionSpec as P

DH = 128
QPK = 4
SCALE2 = math.log2(math.e) * DH ** (-0.5)
NEG = -1e30

NZ, NY, NC = 4, 4, 2
NH, NX = 2, 4

TILE = 256
BESIDE = 4


def ctx_id(z, y, c):
    return (z * NY + y) * NC + c


def ctx_permute(x, target):
    pairs = []
    for z in range(NZ):
        for y in range(NY):
            for c in range(NC):
                to = target(z, y, c)
                if to is not None:
                    pairs.append((ctx_id(z, y, c), ctx_id(*to)))
    return lax.ppermute(x, "ctx", pairs)


def head_permute(x, dz, dx):
    pairs = [
        (h * NX + i, (h + dz) % NH * NX + (i + dx) % NX) for h in range(NH) for i in range(NX)
    ]
    return lax.ppermute(x, "head", pairs)


def dot_nt(a, b):
    return lax.dot_general(a, b, (((1,), (1,)), ((), ())), preferred_element_type=jnp.float32)


def load_kv(blocks, keys, values):
    at = 0
    for block in blocks:
        n = block.shape[0]
        keys[at : at + n, :] = block[:, :DH]
        values[at : at + n, :DH] = block[:, DH:]
        at += n
    values[:at, DH:] = jnp.ones((at, DH), jnp.bfloat16)
    return at


def sweep(slots, length, scores, rest):
    per = length // TILE

    def turn(i, _):
        def place(u):
            j = i * BESIDE + u
            return slots[0] + j // per, pl.multiple_of(j % per * TILE, TILE)

        s = scores(*place(0))
        for u in range(BESIDE):
            after = scores(*place(u + 1)) if u + 1 < BESIDE else None
            rest(*place(u), s)
            s = after
        return 0

    lax.fori_loop(0, (slots[1] - slots[0]) * per // BESIDE, turn, 0)


def update(q, keys, values, count, m_in, acc_in, m_out, acc_out):
    def scores(slot, r):
        return dot_nt(q[slot, pl.ds(r, TILE), :], keys[:count, :]) * SCALE2

    def rest(slot, r, s):
        rows = pl.ds(r, TILE)
        m_old = m_in[slot, rows, :]
        m = jnp.maximum(m_old, jnp.max(s, axis=1, keepdims=True))
        p = jnp.exp2(s - m[:, :1]).astype(jnp.bfloat16)
        o = jnp.dot(p, values[:count, :], preferred_element_type=jnp.float32)
        shrink = jnp.exp2(m_old - m)
        m_out[slot, rows, :] = m
        acc_out[slot, rows, :] = acc_in[slot, rows, :] * jnp.concatenate([shrink, shrink], axis=1) + o

    sweep((0, 2 * QPK), q.shape[1], scores, rest)


def row_kernel(info, q, own, r_ref, l_ref, f_ref, m_out, acc_out, keys, values, bias):
    c, y = info[0], info[1]
    n = own.shape[0]
    count = load_kv((own, r_ref, l_ref, f_ref), keys, values)
    for t in range(2):
        bias[t, :, :n] = jnp.full((8, n), jnp.where((t == 0) | (c == 0), 0.0, NEG), jnp.float32)
        for k, low in enumerate((1, 3, 2), 1):
            bias[t, :, k * n : (k + 1) * n] = jnp.full((8, n), jnp.where(y >= low, 0.0, NEG), jnp.float32)

        def scores(slot, r, t=t):
            s = dot_nt(q[slot, pl.ds(r, TILE), :], keys[:count, :]) * SCALE2 + bias[t, :1, :]
            if t == 0:
                i = r + lax.broadcasted_iota(jnp.int32, (TILE, n), 0)
                j = lax.broadcasted_iota(jnp.int32, (TILE, n), 1)
                s = jnp.concatenate([jnp.where(j <= i, s[:, :n], NEG), s[:, n:]], axis=1)
            return s

        def rest(slot, r, s):
            rows = pl.ds(r, TILE)
            m = jnp.broadcast_to(jnp.max(s, axis=1, keepdims=True), (TILE, DH))
            p = jnp.exp2(s - m[:, :1]).astype(jnp.bfloat16)
            o = jnp.dot(p, values[:count, :], preferred_element_type=jnp.float32)
            some = jnp.concatenate([m, m], axis=1) > 0.5 * NEG
            m_out[slot, rows, :] = m
            acc_out[slot, rows, :] = jnp.where(some, o, 0.0)

        sweep((t * QPK, (t + 1) * QPK), q.shape[1], scores, rest)


def plane_kernel(counts, info, q, *refs):
    blocks, (m_in, acc_in, m_out, acc_out, keys, values) = refs[:-6], refs[-6:]
    z = info[2]
    for kind in sorted(set(counts)):
        of = [k for k in range(NZ) if counts[k] == kind]

        @pl.when((z >= of[0]) & (z <= of[-1]))
        def _(kind=kind):
            if kind == 0:
                m_out[...] = m_in[...]
                acc_out[...] = acc_in[...]
            else:
                count = load_kv([b.at[: b.shape[0] * kind // 2] for b in blocks], keys, values)
                update(q, keys, values, count, m_in, acc_in, m_out, acc_out)


def share_kernel(m, acc, own_out, own_log, send):
    rows = own_out.shape[0]
    lane = lax.broadcasted_iota(jnp.int32, (rows, 128), 1)
    logs = [jnp.zeros((rows, 128), jnp.float32), jnp.zeros((rows, 128), jnp.float32)]
    for slot in range(2 * QPK):
        t, h = slot // QPK, slot % QPK
        total = acc[slot, :, DH:]
        some = total > 0.0
        total = jnp.where(some, total, 1.0)
        o = acc[slot, :, :DH] / total
        log_total = jnp.where(some, m[slot] + jnp.log2(total), NEG)
        logs[t] = jnp.where(lane // (128 // QPK) == h, log_total, logs[t])
        if t == 0:
            own_out[:, h * DH : (h + 1) * DH] = o
        else:
            send[:, h * DH : (h + 1) * DH] = o.astype(jnp.bfloat16)
    own_log[...] = logs[0]
    first = logs[1].astype(jnp.bfloat16).astype(jnp.float32)
    second = (logs[1] - first).astype(jnp.bfloat16).astype(jnp.float32)
    third = logs[1] - first - second
    which = lane % (128 // QPK)
    parts = jnp.where(which == 0, first, jnp.where(which == 1, second, third))
    send[:, QPK * DH :] = parts.astype(jnp.bfloat16)


def join_kernel(own_in, own_log, got, out):
    theirs = got[:, QPK * DH :].astype(jnp.float32)
    for h in range(QPK):
        at = h * (128 // QPK)
        a = own_log[:, at : at + 1]
        b = theirs[:, at : at + 1] + theirs[:, at + 1 : at + 2] + theirs[:, at + 2 : at + 3]
        top = jnp.maximum(a, b)
        a, b = jnp.exp2(a - top), jnp.exp2(b - top)
        share = 1.0 / (a + b)
        a, b = a * share, b * share
        columns = slice(h * DH, (h + 1) * DH)
        o = own_in[:, columns] * a + got[:, columns].astype(jnp.float32) * b
        out[:, columns] = o.astype(jnp.bfloat16)


VM = pl.BlockSpec(memory_space=pltpu.VMEM)
SM = pl.BlockSpec(memory_space=pltpu.SMEM)


def call(kernel, out_shape, *args, info=None, flops=0, scratch=()):
    size = sum(a.size * a.dtype.itemsize for a in args)
    many = isinstance(out_shape, tuple)
    first = [] if info is None else [info]
    return pl.pallas_call(
        kernel,
        out_shape=out_shape,
        in_specs=[SM] * len(first) + [VM] * len(args),
        out_specs=tuple(VM for _ in out_shape) if many else VM,
        scratch_shapes=scratch,
        cost_estimate=pl.CostEstimate(flops=flops, bytes_accessed=size, transcendentals=0),
        compiler_params=pltpu.CompilerParams(vmem_limit_bytes=32 * 2**20),
    )(*first, *args)


def project(info, pieces, out_weight, so_far, out_type):
    refs = [block for piece in pieces for block in piece]
    counts = [len(piece) for piece in pieces]
    rows, depth = sum(b.shape[0] for b in pieces[0]), pieces[0][0].shape[1]
    columns = out_weight.shape[1]

    def kernel(info_ref, *args):
        parts, w_ref = args[: len(refs)], args[len(refs)]
        before = args[len(refs) + 1] if so_far is not None else None
        out, total, weights, sems = args[-4:]
        copies = []
        for k in range(len(counts)):
            start = pl.multiple_of(info_ref[k] * depth, depth)
            copies.append(pltpu.make_async_copy(w_ref.at[pl.ds(start, depth), :], weights.at[k], sems.at[k]))
            copies[-1].start()
        first = 0
        for k, count in enumerate(counts):
            copies[k].wait()
            start = 0
            for block in parts[first : first + count]:
                at = slice(start, start + block.shape[0])
                start += block.shape[0]
                o = jnp.dot(block[...], weights[k], preferred_element_type=jnp.float32)
                if k > 0:
                    o = total[at, :] + o
                elif before is not None:
                    o = before[at, :] + o
                if k == len(counts) - 1:
                    out[at, :] = o.astype(out_type)
                else:
                    total[at, :] = o
            first += count

    inputs = refs + [out_weight] + ([so_far] if so_far is not None else [])
    specs = [VM] * len(refs) + [pl.BlockSpec(memory_space=pltpu.HBM)]
    if so_far is not None:
        specs.append(VM)
    return pl.pallas_call(
        kernel,
        out_shape=jax.ShapeDtypeStruct((rows, columns), out_type),
        in_specs=[SM] + specs,
        out_specs=VM,
        scratch_shapes=[
            pltpu.VMEM((rows, columns), jnp.float32),
            pltpu.VMEM((len(pieces), depth, columns), out_weight.dtype),
            pltpu.SemaphoreType.DMA((len(pieces),)),
        ],
        cost_estimate=pl.CostEstimate(
            flops=2 * rows * depth * columns * len(pieces),
            bytes_accessed=len(pieces) * depth * (columns + rows) * 2,
            transcendentals=0,
        ),
        compiler_params=pltpu.CompilerParams(vmem_limit_bytes=32 * 2**20),
    )(info, *inputs)


def ring_y(x, low):
    shift = lambda d: ctx_permute(x, lambda z, y, c: (z, (y + d) % NY, c) if z >= low else None)
    return shift(1), shift(-1), shift(2)


def per_device(queries, keys, values, out_weight):
    rows = queries.shape[0]
    ctx = lax.axis_index("ctx")
    head = lax.axis_index("head")
    z, y, c = ctx // (NY * NC), ctx // NC % NY, ctx % NC
    i32 = lambda *v: jnp.stack([jnp.asarray(x, jnp.int32) for x in v])
    info = i32(c, y, z)
    swap = lambda z, y, c: (z, y, 1 - c)

    kv = jnp.concatenate([keys, values], axis=1)
    q_own = queries.reshape(rows, QPK, DH).transpose(1, 0, 2)
    q_oth = ctx_permute(q_own, swap)
    lift = lambda x, d: ctx_permute(x, lambda z, y, c: (z + d, y, c) if z + d < NZ else None)
    row = ring_y(kv, 0)
    kv_late, q_oth = lax.optimization_barrier((kv, q_oth))
    lower = [lift(kv, 1), lift(kv_late, 2), lift(kv_late, 3)]
    q = jnp.concatenate([q_own, q_oth], axis=0)
    unit = 2 * 2 * 2 * QPK * rows * rows * DH
    state = (
        jax.ShapeDtypeStruct((2 * QPK, rows, DH), jnp.float32),
        jax.ShapeDtypeStruct((2 * QPK, rows, 2 * DH), jnp.float32),
    )

    def scratch(chunks):
        return [
            pltpu.VMEM((chunks * rows, DH), jnp.bfloat16),
            pltpu.VMEM((chunks * rows, 2 * DH), jnp.bfloat16),
        ]

    def planes(counts, q, blocks, m, acc):
        chunks = sum(b.shape[0] for b in blocks) // rows
        return call(
            lambda *refs: plane_kernel(counts, *refs),
            state, q, *blocks, m, acc, info=info, flops=chunks * unit, scratch=scratch(chunks),
        )

    row_kv, lower[0] = lax.optimization_barrier((kv, lower[0]))
    near = [lower[0], *ring_y(lower[0], 1)]
    m, acc = call(
        row_kernel,
        state,
        q, row_kv, *row,
        info=info, flops=4 * unit, scratch=[*scratch(4), pltpu.VMEM((2, 8, 4 * rows), jnp.float32)],
    )
    m, *lower[1:] = lax.optimization_barrier((m, *lower[1:]))
    both = jnp.concatenate(lower[1:], axis=0)
    r, l, f = ring_y(both, 2)
    near[0], both = lax.optimization_barrier((near[0], both))
    m, acc = planes((0, 2, 2, 2), q, near, m, acc)
    m, acc = planes((0, 0, 1, 2), q, [both, r, l], m, acc)
    m, acc = planes((0, 0, 1, 2), q, [f], m, acc)
    own, own_log, send = call(
        share_kernel,
        (
            jax.ShapeDtypeStruct((rows, QPK * DH), jnp.float32),
            jax.ShapeDtypeStruct((rows, 128), jnp.float32),
            jax.ShapeDtypeStruct((rows, QPK * DH + 128), jnp.bfloat16),
        ),
        m, acc,
    )
    attended = call(
        join_kernel,
        jax.ShapeDtypeStruct((rows, QPK * DH), jnp.bfloat16),
        own, own_log, ctx_permute(send, swap),
    )

    hz, hx = head // NX, head % NX
    which = lambda hz, *shifts: i32(*[hz * NX + (hx + s) % NX for s in shifts])
    half = rows // 2
    far = head_permute(attended, 1, 0)
    r, l = head_permute(attended, 0, 1), head_permute(attended, 0, -1)
    f1, f2 = head_permute(r[:half], 0, 1), head_permute(l[half:], 0, -1)
    far_r, far_l = head_permute(far, 0, 1), head_permute(far, 0, -1)
    total = project(
        which(hz, 0, -1, 1, 2), [[attended], [r], [l], [f1, f2]], out_weight, None, jnp.float32
    )
    f1, f2 = head_permute(far_r[:half], 0, 1), head_permute(far_l[half:], 0, -1)
    total = project(which(1 - hz, 0, -1, 1), [[far], [far_r], [far_l]], out_weight, total, jnp.float32)
    return project(which(1 - hz, 2), [[f1, f2]], out_weight, total, jnp.bfloat16)


def solution(mesh):
    return jax.shard_map(
        per_device,
        mesh=mesh,
        in_specs=(P("ctx", "head"), P("ctx", "head"), P("ctx", "head"), P(None, "head")),
        out_specs=P("ctx", "head"),
        check_vma=False,
    )
```

```python
import math

import jax
import jax.numpy as jnp
from jax import lax
from jax.experimental import pallas as pl
from jax.experimental.pallas import tpu as pltpu
from jax.sharding import PartitionSpec as P

DH = 128
QPK = 4
SCALE2 = math.log2(math.e) * DH ** (-0.5)
NEG = -1e30

NZ, NY, NC = 4, 4, 2
NH, NX = 2, 4

TILE = 256
BESIDE = 4
PIECE = 512
ONES = 16
ROOM = 100.0


def ctx_id(z, y, c):
    return (z * NY + y) * NC + c


def ctx_permute(x, target):
    pairs = []
    for z in range(NZ):
        for y in range(NY):
            for c in range(NC):
                to = target(z, y, c)
                if to is not None:
                    pairs.append((ctx_id(z, y, c), ctx_id(*to)))
    return lax.ppermute(x, "ctx", pairs)


def head_permute(x, dz, dx):
    pairs = [
        (h * NX + i, (h + dz) % NH * NX + (i + dx) % NX) for h in range(NH) for i in range(NX)
    ]
    return lax.ppermute(x, "head", pairs)


def load_kv(blocks, keys, values):
    at = 0
    for block in blocks:
        for i in range(0, block.shape[0], DH):
            keys[at : at + DH, :] = block[i : i + DH, :DH]
            values[:DH, at : at + DH] = block[i : i + DH, DH:]
            at += DH
    values[DH:, :at] = jnp.ones((ONES, at), jnp.bfloat16)
    return at


def sweep(slots, length, scores, rest):
    per = length // TILE

    def turn(i, _):
        def place(u):
            j = i * BESIDE + u
            return slots[0] + j // per, pl.multiple_of(j % per * TILE, TILE)

        s = scores(*place(0))
        for u in range(BESIDE):
            after = scores(*place(u + 1)) if u + 1 < BESIDE else None
            rest(*place(u), s)
            s = after
        return 0

    lax.fori_loop(0, (slots[1] - slots[0]) * per // BESIDE, turn, 0)


def scores_of(q, keys, count):
    def scores(slot, r):
        rows = q[slot, :, pl.ds(r, TILE)]
        return [
            jnp.dot(keys[k : k + PIECE, :], rows, preferred_element_type=jnp.float32) * SCALE2
            for k in range(0, count, PIECE)
        ]

    return scores


def weigh(values, s, m):
    return [
        jnp.dot(
            values[:, k * PIECE : (k + 1) * PIECE],
            jnp.exp2(one - m[:1]).astype(jnp.bfloat16),
            preferred_element_type=jnp.float32,
        )
        for k, one in enumerate(s)
    ]


def update(q, keys, values, count, m_in, acc_in, m_out, acc_out):
    scores = scores_of(q, keys, count)
    squares = keys[:count, :].astype(jnp.float32)
    longest = jnp.sqrt(jnp.max(jnp.sum(squares * squares, axis=1, keepdims=True), axis=0, keepdims=True))
    for t in range(2):
        slots = (t * QPK, (t + 1) * QPK)
        over = None
        for slot in range(*slots):
            rows = q[slot].astype(jnp.float32)
            reach = jnp.sqrt(jnp.sum(rows * rows, axis=0, keepdims=True)) * (1.01 * SCALE2) * longest
            reach = reach - m_in[slot, :1, :]
            over = reach if over is None else jnp.maximum(over, reach)
        near = jnp.max(over) < ROOM

        @pl.when(near)
        def _(slots=slots):
            def rest(slot, r, s):
                rows = pl.ds(r, TILE)
                m = m_in[slot, :, rows]
                m_out[slot, :, rows] = m
                acc_out[slot, :, rows] = acc_in[slot, :, rows] + sum(weigh(values, s, m))

            sweep(slots, q.shape[2], scores, rest)

        @pl.when(jnp.logical_not(near))
        def _(slots=slots):
            def rest(slot, r, s):
                rows = pl.ds(r, TILE)
                m_old = m_in[slot, :, rows]
                m = m_old
                for one in s:
                    m = jnp.maximum(m, jnp.max(one, axis=0, keepdims=True))
                shrink = jnp.exp2(m_old - m)
                m_out[slot, :, rows] = m
                acc_out[slot, :, rows] = acc_in[slot, :, rows] * shrink[:1] + sum(weigh(values, s, m))

            sweep(slots, q.shape[2], scores, rest)


def row_kernel(info, q, own, r_ref, l_ref, f_ref, m_out, acc_out, keys, values):
    c, y = info[0], info[1]
    n = own.shape[0]
    count = load_kv((own, r_ref, l_ref, f_ref), keys, values)
    plain = scores_of(q, keys, count)
    for t in range(2):
        kept = [(c == 0) | (t == 0), y >= 1, y >= 3, y >= 2]
        kept = [kept[k * PIECE // n] for k in range(count // PIECE)]

        def scores(slot, r, t=t):
            s = plain(slot, r)
            if t == 0:
                i = r + lax.broadcasted_iota(jnp.int32, (PIECE, TILE), 1)
                j = lax.broadcasted_iota(jnp.int32, (PIECE, TILE), 0)
                for k in range(n // PIECE):
                    s[k] = jnp.where(j + k * PIECE <= i, s[k], NEG)
            return s

        def rest(slot, r, s, kept=kept):
            rows = pl.ds(r, TILE)
            m = jnp.full((8, TILE), NEG, jnp.float32)
            for one, keep in zip(s, kept):
                m = jnp.maximum(m, jnp.where(keep, jnp.max(one, axis=0, keepdims=True), NEG))
            m_out[slot, :, rows] = m
            acc_out[slot, :, rows] = sum(
                jnp.where(keep, o, 0.0) for o, keep in zip(weigh(values, s, m), kept)
            )

        sweep((t * QPK, (t + 1) * QPK), q.shape[2], scores, rest)


def plane_kernel(counts, info, q, *refs):
    blocks, (m_in, acc_in, m_out, acc_out, keys, values) = refs[:-6], refs[-6:]
    z = info[2]
    for kind in sorted(set(counts)):
        of = [k for k in range(NZ) if counts[k] == kind]

        @pl.when((z >= of[0]) & (z <= of[-1]))
        def _(kind=kind):
            if kind == 0:
                m_out[...] = m_in[...]
                acc_out[...] = acc_in[...]
            else:
                count = load_kv([b.at[: b.shape[0] * kind // 2] for b in blocks], keys, values)
                update(q, keys, values, count, m_in, acc_in, m_out, acc_out)


def share_kernel(m, acc, own_out, own_log, send):
    rows = own_out.shape[1]
    parts = []
    for slot in range(2 * QPK):
        t, h = slot // QPK, slot % QPK
        total = acc[slot, DH : DH + 1, :]
        some = total > 0.0
        total = jnp.where(some, total, 1.0)
        o = acc[slot, :DH, :] / total
        log_total = jnp.where(some, m[slot, :1, :] + jnp.log2(total), NEG)
        columns = slice(h * DH, (h + 1) * DH)
        if t == 0:
            own_out[columns, :] = o
            own_log[h : h + 1, :] = log_total
        else:
            send[columns, :] = o.astype(jnp.bfloat16)
            for _ in range(3):
                parts.append(log_total.astype(jnp.bfloat16).astype(jnp.float32))
                log_total = log_total - parts[-1]
    parts += [jnp.zeros((1, rows), jnp.float32)] * (ONES - len(parts))
    send[QPK * DH :, :] = jnp.concatenate(parts, axis=0).astype(jnp.bfloat16)


def join_kernel(own_in, own_log, got, out):
    theirs = got[QPK * DH :, :].astype(jnp.float32)
    for h in range(QPK):
        a = own_log[h : h + 1, :]
        b = theirs[3 * h : 3 * h + 1, :] + theirs[3 * h + 1 : 3 * h + 2, :] + theirs[3 * h + 2 : 3 * h + 3, :]
        top = jnp.maximum(a, b)
        a, b = jnp.exp2(a - top), jnp.exp2(b - top)
        share = 1.0 / (a + b)
        columns = slice(h * DH, (h + 1) * DH)
        o = own_in[columns, :] * (a * share) + got[columns, :].astype(jnp.float32) * (b * share)
        out[:, columns] = o.T.astype(jnp.bfloat16)


VM = pl.BlockSpec(memory_space=pltpu.VMEM)
SM = pl.BlockSpec(memory_space=pltpu.SMEM)


def call(kernel, out_shape, *args, info=None, flops=0, scratch=()):
    size = sum(a.size * a.dtype.itemsize for a in args)
    many = isinstance(out_shape, tuple)
    first = [] if info is None else [info]
    return pl.pallas_call(
        kernel,
        out_shape=out_shape,
        in_specs=[SM] * len(first) + [VM] * len(args),
        out_specs=tuple(VM for _ in out_shape) if many else VM,
        scratch_shapes=scratch,
        cost_estimate=pl.CostEstimate(flops=flops, bytes_accessed=size, transcendentals=0),
        compiler_params=pltpu.CompilerParams(vmem_limit_bytes=32 * 2**20),
    )(*first, *args)


def project(info, pieces, out_weight, so_far, out_type):
    refs = [block for piece in pieces for block in piece]
    counts = [len(piece) for piece in pieces]
    rows, depth = sum(b.shape[0] for b in pieces[0]), pieces[0][0].shape[1]
    columns = out_weight.shape[1]

    def kernel(info_ref, *args):
        parts, w_ref = args[: len(refs)], args[len(refs)]
        before = args[len(refs) + 1] if so_far is not None else None
        out, total, weights, sems = args[-4:]
        copies = []
        for k in range(len(counts)):
            start = pl.multiple_of(info_ref[k] * depth, depth)
            copies.append(pltpu.make_async_copy(w_ref.at[pl.ds(start, depth), :], weights.at[k], sems.at[k]))
            copies[-1].start()
        first = 0
        for k, count in enumerate(counts):
            copies[k].wait()
            start = 0
            for block in parts[first : first + count]:
                at = slice(start, start + block.shape[0])
                start += block.shape[0]
                o = jnp.dot(block[...], weights[k], preferred_element_type=jnp.float32)
                if k > 0:
                    o = total[at, :] + o
                elif before is not None:
                    o = before[at, :] + o
                if k == len(counts) - 1:
                    out[at, :] = o.astype(out_type)
                else:
                    total[at, :] = o
            first += count

    inputs = refs + [out_weight] + ([so_far] if so_far is not None else [])
    specs = [VM] * len(refs) + [pl.BlockSpec(memory_space=pltpu.HBM)]
    if so_far is not None:
        specs.append(VM)
    return pl.pallas_call(
        kernel,
        out_shape=jax.ShapeDtypeStruct((rows, columns), out_type),
        in_specs=[SM] + specs,
        out_specs=VM,
        scratch_shapes=[
            pltpu.VMEM((rows, columns), jnp.float32),
            pltpu.VMEM((len(pieces), depth, columns), out_weight.dtype),
            pltpu.SemaphoreType.DMA((len(pieces),)),
        ],
        cost_estimate=pl.CostEstimate(
            flops=2 * rows * depth * columns * len(pieces),
            bytes_accessed=len(pieces) * depth * (columns + rows) * 2,
            transcendentals=0,
        ),
        compiler_params=pltpu.CompilerParams(vmem_limit_bytes=55 * 2**20),
    )(info, *inputs)


def ring_y(x, low):
    shift = lambda d: ctx_permute(x, lambda z, y, c: (z, (y + d) % NY, c) if z >= low else None)
    return [shift(1), shift(-1), shift(2)]


def per_device(queries, keys, values, out_weight):
    rows = queries.shape[0]
    ctx = lax.axis_index("ctx")
    head = lax.axis_index("head")
    z, y, c = ctx // (NY * NC), ctx // NC % NY, ctx % NC
    i32 = lambda *v: jnp.stack([jnp.asarray(x, jnp.int32) for x in v])
    info = i32(c, y, z)
    swap = lambda z, y, c: (z, y, 1 - c)

    squares = values.reshape(rows // DH, DH, DH).transpose(0, 2, 1).reshape(rows, DH)
    kv = jnp.concatenate([keys, squares], axis=1)
    q_own = queries.T.reshape(QPK, DH, rows)
    q_oth = ctx_permute(q_own, swap)
    lift = lambda x, d: ctx_permute(x, lambda z, y, c: (z + d, y, c) if z + d < NZ else None)
    row = ring_y(kv, 0)
    below, q_oth, *row[:2] = lax.optimization_barrier((lift(kv, 1), q_oth, *row[:2]))
    both = jnp.concatenate([lift(below, 1), lift(below, 2)], axis=0)
    near = [below, *ring_y(below, 1)]
    r, l, f = ring_y(both, 2)
    q = jnp.concatenate([q_own, q_oth], axis=0)
    unit = 2 * 2 * 2 * QPK * rows * rows * DH
    state = (
        jax.ShapeDtypeStruct((2 * QPK, 8, rows), jnp.float32),
        jax.ShapeDtypeStruct((2 * QPK, DH + ONES, rows), jnp.float32),
    )

    def scratch(chunks):
        return [
            pltpu.VMEM((chunks * rows, DH), jnp.bfloat16),
            pltpu.VMEM((DH + ONES, chunks * rows), jnp.bfloat16),
        ]

    def planes(counts, q, blocks, m, acc):
        chunks = sum(b.shape[0] for b in blocks) // rows
        return call(
            lambda *refs: plane_kernel(counts, *refs),
            state, q, *blocks, m, acc, info=info, flops=chunks * unit, scratch=scratch(chunks),
        )

    row_kv, both = lax.optimization_barrier((kv, both))
    m, acc = call(
        row_kernel, state, q, row_kv, *row, info=info, flops=4 * unit, scratch=scratch(4)
    )
    m, acc = planes((0, 2, 2, 2), q, near, m, acc)
    m, acc = planes((0, 0, 1, 2), q, [both, r, l], m, acc)
    m, acc = planes((0, 0, 1, 2), q, [f], m, acc)
    own, own_log, send = call(
        share_kernel,
        (
            jax.ShapeDtypeStruct((QPK * DH, rows), jnp.float32),
            jax.ShapeDtypeStruct((8, rows), jnp.float32),
            jax.ShapeDtypeStruct((QPK * DH + ONES, rows), jnp.bfloat16),
        ),
        m, acc,
    )
    attended = call(
        join_kernel,
        jax.ShapeDtypeStruct((rows, QPK * DH), jnp.bfloat16),
        own, own_log, ctx_permute(send, swap),
    )

    hz, hx = head // NX, head % NX
    which = lambda hz, *shifts: [hz * NX + (hx + s) % NX for s in shifts]
    half = rows // 2
    far = head_permute(attended, 1, 0)
    r, l = head_permute(attended, 0, 1), head_permute(attended, 0, -1)
    f = [head_permute(r[:half], 0, 1), head_permute(l[half:], 0, -1)]
    far_r, far_l = head_permute(far, 0, 1), head_permute(far, 0, -1)
    total = project(
        i32(*which(hz, 0, -1, 1)), [[attended], [r], [l]], out_weight, None, jnp.float32
    )
    far_r, far_l, total = lax.optimization_barrier((far_r, far_l, total))
    far_f = [head_permute(far_r[:half], 0, 1), head_permute(far_l[half:], 0, -1)]
    total = project(
        i32(*which(hz, 2), *which(1 - hz, 0, -1, 1)),
        [f, [far], [far_r], [far_l]],
        out_weight, total, jnp.float32,
    )
    return project(i32(*which(1 - hz, 2)), [far_f], out_weight, total, jnp.bfloat16)


def solution(mesh):
    return jax.shard_map(
        per_device,
        mesh=mesh,
        in_specs=(P("ctx", "head"), P("ctx", "head"), P("ctx", "head"), P(None, "head")),
        out_specs=P("ctx", "head"),
        check_vma=False,
    )
```

```python
import math

import jax
import jax.numpy as jnp
from jax import lax
from jax.experimental import pallas as pl
from jax.experimental.pallas import tpu as pltpu
from jax.sharding import PartitionSpec as P

DH = 128
QPK = 4
SCALE2 = math.log2(math.e) * DH ** (-0.5)
NEG = -1e30

NZ, NY, NC = 4, 4, 2
NH, NX = 2, 4

TILE = 256
BESIDE = 4
PIECE = 512
ONES = 16
ROOM = 100.0


def ctx_id(z, y, c):
    return (z * NY + y) * NC + c


def ctx_permute(x, target):
    pairs = []
    for z in range(NZ):
        for y in range(NY):
            for c in range(NC):
                to = target(z, y, c)
                if to is not None:
                    pairs.append((ctx_id(z, y, c), ctx_id(*to)))
    return lax.ppermute(x, "ctx", pairs)


def head_permute(x, dz, dx):
    pairs = [
        (h * NX + i, (h + dz) % NH * NX + (i + dx) % NX) for h in range(NH) for i in range(NX)
    ]
    return lax.ppermute(x, "head", pairs)


def load_kv(blocks, keys, values):
    at = 0
    for block in blocks:
        for i in range(0, block.shape[0], DH):
            keys[at : at + DH, :] = block[i : i + DH, :DH]
            values[:DH, at : at + DH] = block[i : i + DH, DH:]
            at += DH
    values[DH:, :at] = jnp.ones((ONES, at), jnp.bfloat16)
    return at


def sweep(slots, length, scores, rest):
    per = length // TILE

    def turn(i, _):
        def place(u):
            j = i * BESIDE + u
            return slots[0] + j // per, pl.multiple_of(j % per * TILE, TILE)

        s = scores(*place(0))
        for u in range(BESIDE):
            after = scores(*place(u + 1)) if u + 1 < BESIDE else None
            rest(*place(u), s)
            s = after
        return 0

    lax.fori_loop(0, (slots[1] - slots[0]) * per // BESIDE, turn, 0)


def scores_of(q, keys, count):
    def scores(slot, r):
        rows = q[slot, :, pl.ds(r, TILE)]
        return [
            jnp.dot(keys[k : k + PIECE, :], rows, preferred_element_type=jnp.float32) * SCALE2
            for k in range(0, count, PIECE)
        ]

    return scores


def weigh(values, s, m, kept=None):
    total = None
    for k, one in enumerate(s):
        p = jnp.exp2(one - m[:1]).astype(jnp.bfloat16)
        o = jnp.dot(
            values[:, k * PIECE : (k + 1) * PIECE], p, preferred_element_type=jnp.float32
        )
        if kept is not None:
            o = jnp.where(kept[k], o, 0.0)
        total = o if total is None else total + o
    return total


def update(q, keys, values, count, m_in, acc_in, m_out, acc_out, kept=None):
    scores = scores_of(q, keys, count)
    squares = jnp.dot(
        keys[:count, :] * keys[:count, :], jnp.ones((DH, DH), jnp.bfloat16), preferred_element_type=jnp.float32
    )
    longest = jnp.sqrt(jnp.max(squares, axis=0, keepdims=True))[:, :1]
    for t in range(2):
        slots = (t * QPK, (t + 1) * QPK)
        over = None
        for slot in range(*slots):
            rows = q[slot].astype(jnp.float32)
            reach = jnp.sqrt(jnp.sum(rows * rows, axis=0, keepdims=True)) * (1.02 * SCALE2) * longest
            reach = reach - m_in[slot, :1, :]
            over = reach if over is None else jnp.maximum(over, reach)
        near = jnp.max(over) < ROOM

        @pl.when(near)
        def _(slots=slots):
            def rest(slot, r, s):
                rows = pl.ds(r, TILE)
                m = m_in[slot, :, rows]
                m_out[slot, :, rows] = m
                acc_out[slot, :, rows] = acc_in[slot, :, rows] + weigh(values, s, m, kept)

            sweep(slots, q.shape[2], scores, rest)

        @pl.when(jnp.logical_not(near))
        def _(slots=slots):
            def rest(slot, r, s):
                rows = pl.ds(r, TILE)
                m_old = m_in[slot, :, rows]
                m = m_old
                for k, one in enumerate(s):
                    top = jnp.max(one, axis=0, keepdims=True)
                    m = jnp.maximum(m, top if kept is None else jnp.where(kept[k], top, NEG))
                shrink = jnp.exp2(m_old - m)
                m_out[slot, :, rows] = m
                acc_out[slot, :, rows] = acc_in[slot, :, rows] * shrink[:1] + weigh(values, s, m, kept)

            sweep(slots, q.shape[2], scores, rest)


def own_kernel(info, q, own, m_out, acc_out, keys, values):
    n = own.shape[0]
    count = load_kv((own,), keys, values)
    plain = scores_of(q, keys, count)

    def masked(slot, r):
        s = plain(slot, r)
        i = r + lax.broadcasted_iota(jnp.int32, (PIECE, TILE), 1)
        j = lax.broadcasted_iota(jnp.int32, (PIECE, TILE), 0)
        return [jnp.where(j + k * PIECE <= i, one, NEG) for k, one in enumerate(s)]

    def rest(slot, r, s):
        rows = pl.ds(r, TILE)
        m = jnp.full((8, TILE), NEG, jnp.float32)
        for one in s:
            m = jnp.maximum(m, jnp.max(one, axis=0, keepdims=True))
        m_out[slot, :, rows] = m
        acc_out[slot, :, rows] = weigh(values, s, m)

    sweep((0, QPK), n, masked, rest)

    @pl.when(info[0] == 0)
    def _():
        sweep((QPK, 2 * QPK), n, plain, rest)

    @pl.when(info[0] != 0)
    def _():
        m_out[QPK:] = jnp.full((QPK, 8, n), NEG, jnp.float32)
        acc_out[QPK:] = jnp.zeros((QPK, DH + ONES, n), jnp.float32)


def row_kernel(info, q, r_ref, l_ref, f_ref, m_in, acc_in, m_out, acc_out, keys, values):
    y = info[1]
    n = r_ref.shape[0]

    @pl.when(y == 0)
    def _():
        m_out[...] = m_in[...]
        acc_out[...] = acc_in[...]

    @pl.when(y != 0)
    def _():
        count = load_kv((r_ref, f_ref, l_ref), keys, values)
        kept = [y >= 1 + k * PIECE // n for k in range(count // PIECE)]
        update(q, keys, values, count, m_in, acc_in, m_out, acc_out, kept)


def plane_kernel(counts, info, q, *refs):
    blocks, (m_in, acc_in, m_out, acc_out, keys, values) = refs[:-6], refs[-6:]
    z = info[2]
    for kind in sorted(set(counts)):
        of = [k for k in range(NZ) if counts[k] == kind]

        @pl.when((z >= of[0]) & (z <= of[-1]))
        def _(kind=kind):
            if kind == 0:
                m_out[...] = m_in[...]
                acc_out[...] = acc_in[...]
            else:
                count = load_kv([b.at[: b.shape[0] * kind // 2] for b in blocks], keys, values)
                update(q, keys, values, count, m_in, acc_in, m_out, acc_out)


def share_kernel(m, acc, own_out, own_log, send):
    rows = own_out.shape[1]
    parts = []
    for slot in range(2 * QPK):
        t, h = slot // QPK, slot % QPK
        total = acc[slot, DH : DH + 1, :]
        some = total > 0.0
        total = jnp.where(some, total, 1.0)
        o = acc[slot, :DH, :] / total
        log_total = jnp.where(some, m[slot, :1, :] + jnp.log2(total), NEG)
        columns = slice(h * DH, (h + 1) * DH)
        if t == 0:
            own_out[columns, :] = o
            own_log[h : h + 1, :] = log_total
        else:
            send[columns, :] = o.astype(jnp.bfloat16)
            for _ in range(3):
                parts.append(log_total.astype(jnp.bfloat16).astype(jnp.float32))
                log_total = log_total - parts[-1]
    parts += [jnp.zeros((1, rows), jnp.float32)] * (ONES - len(parts))
    send[QPK * DH :, :] = jnp.concatenate(parts, axis=0).astype(jnp.bfloat16)


def join_kernel(own_in, own_log, got, out):
    theirs = got[QPK * DH :, :].astype(jnp.float32)
    for h in range(QPK):
        a = own_log[h : h + 1, :]
        b = theirs[3 * h : 3 * h + 1, :] + theirs[3 * h + 1 : 3 * h + 2, :] + theirs[3 * h + 2 : 3 * h + 3, :]
        top = jnp.maximum(a, b)
        a, b = jnp.exp2(a - top), jnp.exp2(b - top)
        share = 1.0 / (a + b)
        columns = slice(h * DH, (h + 1) * DH)
        o = own_in[columns, :] * (a * share) + got[columns, :].astype(jnp.float32) * (b * share)
        out[:, columns] = o.T.astype(jnp.bfloat16)


VM = pl.BlockSpec(memory_space=pltpu.VMEM)
SM = pl.BlockSpec(memory_space=pltpu.SMEM)


def call(kernel, out_shape, *args, info=None, flops=0, scratch=()):
    size = sum(a.size * a.dtype.itemsize for a in args)
    many = isinstance(out_shape, tuple)
    first = [] if info is None else [info]
    return pl.pallas_call(
        kernel,
        out_shape=out_shape,
        in_specs=[SM] * len(first) + [VM] * len(args),
        out_specs=tuple(VM for _ in out_shape) if many else VM,
        scratch_shapes=scratch,
        cost_estimate=pl.CostEstimate(flops=flops, bytes_accessed=size, transcendentals=0),
        compiler_params=pltpu.CompilerParams(vmem_limit_bytes=32 * 2**20),
    )(*first, *args)


def arrange(order, out_weight, depth):
    count = out_weight.shape[0] // depth

    def kernel(order_ref, w_ref, out, sems):
        copies = []
        for k in range(count):
            start = pl.multiple_of(order_ref[k] * depth, depth)
            copies.append(
                pltpu.make_async_copy(
                    w_ref.at[pl.ds(start, depth), :], out.at[pl.ds(k * depth, depth), :], sems.at[k]
                )
            )
            copies[-1].start()
        for copy in copies:
            copy.wait()

    return pl.pallas_call(
        kernel,
        out_shape=jax.ShapeDtypeStruct(out_weight.shape, out_weight.dtype),
        in_specs=[SM, pl.BlockSpec(memory_space=pltpu.HBM)],
        out_specs=VM,
        scratch_shapes=[pltpu.SemaphoreType.DMA((count,))],
        compiler_params=pltpu.CompilerParams(vmem_limit_bytes=32 * 2**20),
    )(order, out_weight)


def project(first, pieces, weights, so_far, out_type):
    refs = [block for piece in pieces for block in piece]
    counts = [len(piece) for piece in pieces]
    rows, depth = sum(b.shape[0] for b in pieces[0]), pieces[0][0].shape[1]
    columns = weights.shape[1]

    def kernel(*args):
        parts, w_ref = args[: len(refs)], args[len(refs)]
        before = args[len(refs) + 1] if so_far is not None else None
        out, total = args[-2:]
        at_ref = 0
        for k, count in enumerate(counts):
            start = 0
            for block in parts[at_ref : at_ref + count]:
                at = slice(start, start + block.shape[0])
                start += block.shape[0]
                w = w_ref[(first + k) * depth : (first + k + 1) * depth, :]
                o = jnp.dot(block[...], w, preferred_element_type=jnp.float32)
                if k > 0:
                    o = total[at, :] + o
                elif before is not None:
                    o = before[at, :] + o
                if k == len(counts) - 1:
                    out[at, :] = o.astype(out_type)
                else:
                    total[at, :] = o
            at_ref += count

    inputs = refs + [weights] + ([so_far] if so_far is not None else [])
    return pl.pallas_call(
        kernel,
        out_shape=jax.ShapeDtypeStruct((rows, columns), out_type),
        in_specs=[VM] * len(inputs),
        out_specs=VM,
        scratch_shapes=[pltpu.VMEM((rows, columns), jnp.float32)],
        cost_estimate=pl.CostEstimate(
            flops=2 * rows * depth * columns * len(pieces),
            bytes_accessed=len(pieces) * depth * (columns + rows) * 2,
            transcendentals=0,
        ),
        compiler_params=pltpu.CompilerParams(vmem_limit_bytes=32 * 2**20),
    )(*inputs)


def shift_y(x, d, low=0):
    return ctx_permute(x, lambda z, y, c: (z, (y + d) % NY, c) if z >= low else None)


def ring_y(x, low):
    return [shift_y(x, d, low) for d in (1, -1, 2)]


def per_device(queries, keys, values, out_weight):
    rows = queries.shape[0]
    ctx = lax.axis_index("ctx")
    head = lax.axis_index("head")
    z, y, c = ctx // (NY * NC), ctx // NC % NY, ctx % NC
    i32 = lambda *v: jnp.stack([jnp.asarray(x, jnp.int32) for x in v])
    info = i32(c, y, z)
    swap = lambda z, y, c: (z, y, 1 - c)

    squares = values.reshape(rows // DH, DH, DH).transpose(0, 2, 1).reshape(rows, DH)
    kv, queries = lax.optimization_barrier((jnp.concatenate([keys, squares], axis=1), queries))
    q_own = queries.T.reshape(QPK, DH, rows)
    q = jnp.concatenate([q_own, ctx_permute(q_own, swap)], axis=0)
    lift = lambda x, d: ctx_permute(x, lambda z, y, c: (z + d, y, c) if z + d < NZ else None)
    unit = 2 * 2 * 2 * QPK * rows * rows * DH
    state = (
        jax.ShapeDtypeStruct((2 * QPK, 8, rows), jnp.float32),
        jax.ShapeDtypeStruct((2 * QPK, DH + ONES, rows), jnp.float32),
    )

    def attend(kernel, chunks, *args):
        return call(
            kernel,
            state,
            *args,
            info=info,
            flops=chunks * unit,
            scratch=[
                pltpu.VMEM((chunks * rows, DH), jnp.bfloat16),
                pltpu.VMEM((DH + ONES, chunks * rows), jnp.bfloat16),
            ],
        )

    def planes(counts, blocks, m, acc):
        chunks = sum(b.shape[0] for b in blocks) // rows
        return attend(lambda *refs: plane_kernel(counts, *refs), chunks, q, *blocks, m, acc)

    hz, hx = head // NX, head % NX
    order = [h * NX + (hx + s) % NX for h, s in ((hz, 0), (hz, -1), (hz, 1), (hz, 2))]
    order += [(1 - hz) * NX + (hx + s) % NX for s in (0, -1, 1, 2)]
    below = lift(kv, 1)
    row = [shift_y(kv, d) for d in (1, -1)]
    m, acc = attend(own_kernel, 1, q, kv)
    lower = [lift(below, 1), lift(below, 2)]
    near, kv_late, m, *row = lax.optimization_barrier((below, kv, m, *row))
    row.append(shift_y(kv_late, 2))
    near = [near, *ring_y(near, 1)]
    m, acc = attend(row_kernel, 3, q, *row, m, acc)
    m, *lower = lax.optimization_barrier((m, *lower))
    both = jnp.concatenate(lower, axis=0)
    r, l, f = ring_y(both, 2)
    near[0], both = lax.optimization_barrier((near[0], both))
    m, acc = planes((0, 2, 2, 2), near, m, acc)
    m, acc = planes((0, 0, 1, 2), [both], m, acc)
    m, order = lax.optimization_barrier((m, i32(*order)))
    weights = arrange(order, out_weight, QPK * DH)
    m, weights = lax.optimization_barrier((m, weights))
    m, acc = planes((0, 0, 1, 2), [r, l], m, acc)
    m, acc = planes((0, 0, 1, 2), [f], m, acc)
    own, own_log, send = call(
        share_kernel,
        (
            jax.ShapeDtypeStruct((QPK * DH, rows), jnp.float32),
            jax.ShapeDtypeStruct((8, rows), jnp.float32),
            jax.ShapeDtypeStruct((QPK * DH + ONES, rows), jnp.bfloat16),
        ),
        m, acc,
    )
    attended = call(
        join_kernel,
        jax.ShapeDtypeStruct((rows, QPK * DH), jnp.bfloat16),
        own, own_log, ctx_permute(send, swap),
    )

    half = rows // 2
    far = head_permute(attended, 1, 0)
    r, l = head_permute(attended, 0, 1), head_permute(attended, 0, -1)
    f = [head_permute(r[:half], 0, 1), head_permute(l[half:], 0, -1)]
    far_r, far_l = head_permute(far, 0, 1), head_permute(far, 0, -1)
    total = project(0, [[attended], [r], [l]], weights, None, jnp.float32)
    far_r, far_l, total = lax.optimization_barrier((far_r, far_l, total))
    far_f = [head_permute(far_r[:half], 0, 1), head_permute(far_l[half:], 0, -1)]
    total = project(3, [f, [far], [far_r], [far_l]], weights, total, jnp.float32)
    return project(7, [far_f], weights, total, jnp.bfloat16)


def solution(mesh):
    return jax.shard_map(
        per_device,
        mesh=mesh,
        in_specs=(P("ctx", "head"), P("ctx", "head"), P("ctx", "head"), P(None, "head")),
        out_specs=P("ctx", "head"),
        check_vma=False,
    )
```

```python
import math

import jax
import jax.numpy as jnp
from jax import lax
from jax.experimental import pallas as pl
from jax.experimental.pallas import tpu as pltpu
from jax.sharding import PartitionSpec as P

DH = 128
QPK = 4
SCALE2 = math.log2(math.e) * DH ** (-0.5)
NEG = -1e30

NZ, NY, NC = 4, 4, 2
NH, NX = 2, 4

TILE = 256
BESIDE = 4
PIECE = 512
ONES = 16
ROOM = 100.0


def ctx_id(z, y, c):
    return (z * NY + y) * NC + c


def ctx_permute(x, target):
    pairs = []
    for z in range(NZ):
        for y in range(NY):
            for c in range(NC):
                to = target(z, y, c)
                if to is not None:
                    pairs.append((ctx_id(z, y, c), ctx_id(*to)))
    return lax.ppermute(x, "ctx", pairs)


def head_permute(x, dz, dx):
    pairs = [
        (h * NX + i, (h + dz) % NH * NX + (i + dx) % NX) for h in range(NH) for i in range(NX)
    ]
    return lax.ppermute(x, "head", pairs)


def load_kv(blocks, keys, values):
    at = 0
    for block in blocks:
        for i in range(0, block.shape[0], DH):
            keys[at : at + DH, :] = block[i : i + DH, :DH]
            values[:DH, at : at + DH] = block[i : i + DH, DH:]
            at += DH
    values[DH:, :at] = jnp.ones((ONES, at), jnp.bfloat16)
    return at


def sweep(slots, length, scores, *ways):
    per = length // TILE

    def turn(i, _):
        def place(u):
            j = i * BESIDE + u
            return slots[0] + j // per, pl.multiple_of(j % per * TILE, TILE)

        def go(rest):
            s = scores(*place(0))
            for u in range(BESIDE):
                after = scores(*place(u + 1)) if u + 1 < BESIDE else None
                rest(*place(u), s)
                s = after

        for way in ways:
            if isinstance(way, tuple):
                pl.when(way[0](place(0)[0]))(lambda rest=way[1]: go(rest))
            else:
                go(way)
        return 0

    lax.fori_loop(0, (slots[1] - slots[0]) * per // BESIDE, turn, 0)


def scores_of(q, keys, count):
    def scores(slot, r):
        rows = q[slot, :, pl.ds(r, TILE)]
        return [
            jnp.dot(keys[k : k + PIECE, :], rows, preferred_element_type=jnp.float32) * SCALE2
            for k in range(0, count, PIECE)
        ]

    return scores


def weigh(values, s, m, kept=None):
    total = None
    for k, one in enumerate(s):
        p = jnp.exp2(one - m[:1]).astype(jnp.bfloat16)
        o = jnp.dot(
            values[:, k * PIECE : (k + 1) * PIECE], p, preferred_element_type=jnp.float32
        )
        if kept is not None:
            o = jnp.where(kept[k], o, 0.0)
        total = o if total is None else total + o
    return total


def update(q, keys, values, count, m_in, acc_in, m_out, acc_out, kept):
    scores = scores_of(q, keys, count)
    squares = jnp.dot(
        keys[:count, :] * keys[:count, :], jnp.ones((DH, DH), jnp.bfloat16), preferred_element_type=jnp.float32
    )
    longest = jnp.sqrt(jnp.max(squares, axis=0, keepdims=True))[:, :1] * (1.02 * SCALE2)
    near = []
    for t in range(2):
        over = None
        for slot in range(t * QPK, (t + 1) * QPK):
            reach = m_in[slot, 1:2, :] * longest - m_in[slot, :1, :]
            over = reach if over is None else jnp.maximum(over, reach)
        near.append(jnp.max(over) < ROOM)
    near_at = lambda slot: jnp.where(slot < QPK, near[0], near[1])

    def stay(slot, r, s):
        rows = pl.ds(r, TILE)
        m = m_in[slot, :, rows]
        m_out[slot, :, rows] = m
        acc_out[slot, :, rows] = acc_in[slot, :, rows] + weigh(values, s, m, kept)

    def move(slot, r, s):
        rows = pl.ds(r, TILE)
        m_old = m_in[slot, :, rows]
        m = m_old[:1]
        for one, keep in zip(s, kept):
            m = jnp.maximum(m, jnp.where(keep, jnp.max(one, axis=0, keepdims=True), NEG))
        shrink = jnp.exp2(m_old[:1] - m)
        m_out[slot, :, rows] = jnp.concatenate([m, m_old[1:]], axis=0)
        acc_out[slot, :, rows] = acc_in[slot, :, rows] * shrink + weigh(values, s, m, kept)

    sweep(
        (0, 2 * QPK), q.shape[2], scores, (near_at, stay), (lambda slot: jnp.logical_not(near_at(slot)), move)
    )


def own_kernel(info, q, own, m_out, acc_out, keys, values):
    n = own.shape[0]
    count = load_kv((own,), keys, values)
    plain = scores_of(q, keys, count)

    def masked(slot, r):
        s = plain(slot, r)
        i = r + lax.broadcasted_iota(jnp.int32, (PIECE, TILE), 1)
        j = lax.broadcasted_iota(jnp.int32, (PIECE, TILE), 0)
        return [jnp.where(j + k * PIECE <= i, one, NEG) for k, one in enumerate(s)]

    def rest(slot, r, s):
        rows = pl.ds(r, TILE)
        m = jnp.max(s[0], axis=0, keepdims=True)
        for one in s[1:]:
            m = jnp.maximum(m, jnp.max(one, axis=0, keepdims=True))
        m_out[slot, :1, rows] = m
        acc_out[slot, :, rows] = weigh(values, s, m)

    sweep((0, QPK), n, masked, rest)

    @pl.when(info[0] == 0)
    def _():
        sweep((QPK, 2 * QPK), n, plain, rest)

    @pl.when(info[0] != 0)
    def _():
        m_out[QPK:, :1, :] = jnp.full((QPK, 1, n), NEG, jnp.float32)
        acc_out[QPK:] = jnp.zeros((QPK, DH + ONES, n), jnp.float32)

    for slot in range(2 * QPK):
        rows = q[slot].astype(jnp.float32)
        length = jnp.sqrt(jnp.sum(rows * rows, axis=0, keepdims=True))
        m_out[slot, 1:, :] = jnp.broadcast_to(length, (7, n))


def row_kernel(info, q, r_ref, l_ref, f_ref, m_in, acc_in, m_out, acc_out, keys, values):
    y = info[1]
    n = r_ref.shape[0]

    @pl.when(y == 0)
    def _():
        m_out[...] = m_in[...]
        acc_out[...] = acc_in[...]

    @pl.when(y != 0)
    def _():
        count = load_kv((r_ref, f_ref, l_ref), keys, values)
        kept = [y >= 1 + k * PIECE // n for k in range(count // PIECE)]
        update(q, keys, values, count, m_in, acc_in, m_out, acc_out, kept)


def plane_kernel(lowest, info, q, *refs):
    blocks, (m_in, acc_in, m_out, acc_out, keys, values) = refs[:-6], refs[-6:]
    z = info[2]

    @pl.when(z < min(lowest))
    def _():
        m_out[...] = m_in[...]
        acc_out[...] = acc_in[...]

    @pl.when(z >= min(lowest))
    def _():
        count = load_kv(blocks, keys, values)
        n = blocks[0].shape[0] // len(lowest)
        kept = [z >= lowest[k * PIECE // n % len(lowest)] for k in range(count // PIECE)]
        update(q, keys, values, count, m_in, acc_in, m_out, acc_out, kept)


def share_kernel(m, acc, own_out, own_log, send):
    rows = own_out.shape[1]
    parts = []
    for slot in range(2 * QPK):
        t, h = slot // QPK, slot % QPK
        total = acc[slot, DH : DH + 1, :]
        some = total > 0.0
        total = jnp.where(some, total, 1.0)
        o = acc[slot, :DH, :] / total
        log_total = jnp.where(some, m[slot, :1, :] + jnp.log2(total), NEG)
        columns = slice(h * DH, (h + 1) * DH)
        if t == 0:
            own_out[columns, :] = o
            own_log[h : h + 1, :] = log_total
        else:
            send[columns, :] = o.astype(jnp.bfloat16)
            for _ in range(3):
                parts.append(log_total.astype(jnp.bfloat16).astype(jnp.float32))
                log_total = log_total - parts[-1]
    parts += [jnp.zeros((1, rows), jnp.float32)] * (ONES - len(parts))
    send[QPK * DH :, :] = jnp.concatenate(parts, axis=0).astype(jnp.bfloat16)


def join_kernel(own_in, own_log, got, top_out, low_out):
    theirs = got[QPK * DH :, :].astype(jnp.float32)
    for h in range(QPK):
        a = own_log[h : h + 1, :]
        b = theirs[3 * h : 3 * h + 1, :] + theirs[3 * h + 1 : 3 * h + 2, :] + theirs[3 * h + 2 : 3 * h + 3, :]
        top = jnp.maximum(a, b)
        a, b = jnp.exp2(a - top), jnp.exp2(b - top)
        share = 1.0 / (a + b)
        columns = slice(h * DH, (h + 1) * DH)
        o = own_in[columns, :] * (a * share) + got[columns, :].astype(jnp.float32) * (b * share)
        o = o.T.astype(jnp.bfloat16)
        half = top_out.shape[0]
        top_out[:, columns] = o[:half]
        low_out[:, columns] = o[half:]


VM = pl.BlockSpec(memory_space=pltpu.VMEM)
SM = pl.BlockSpec(memory_space=pltpu.SMEM)


def call(kernel, out_shape, *args, info=None, flops=0, scratch=()):
    size = sum(a.size * a.dtype.itemsize for a in args)
    many = isinstance(out_shape, tuple)
    first = [] if info is None else [info]
    return pl.pallas_call(
        kernel,
        out_shape=out_shape,
        in_specs=[SM] * len(first) + [VM] * len(args),
        out_specs=tuple(VM for _ in out_shape) if many else VM,
        scratch_shapes=scratch,
        cost_estimate=pl.CostEstimate(flops=flops, bytes_accessed=size, transcendentals=0),
        compiler_params=pltpu.CompilerParams(vmem_limit_bytes=32 * 2**20),
    )(*first, *args)


def arrange(order, out_weight, depth):
    count = out_weight.shape[0] // depth

    def kernel(order_ref, w_ref, out, sems):
        copies = []
        for k in range(count):
            start = pl.multiple_of(order_ref[k] * depth, depth)
            copies.append(
                pltpu.make_async_copy(
                    w_ref.at[pl.ds(start, depth), :], out.at[pl.ds(k * depth, depth), :], sems.at[k]
                )
            )
            copies[-1].start()
        for copy in copies:
            copy.wait()

    return pl.pallas_call(
        kernel,
        out_shape=jax.ShapeDtypeStruct(out_weight.shape, out_weight.dtype),
        in_specs=[SM, pl.BlockSpec(memory_space=pltpu.HBM)],
        out_specs=VM,
        scratch_shapes=[pltpu.SemaphoreType.DMA((count,))],
        compiler_params=pltpu.CompilerParams(vmem_limit_bytes=32 * 2**20),
    )(order, out_weight)


def project(first, pieces, weights, so_far, out_type):
    refs = [block for piece in pieces for block in piece]
    counts = [len(piece) for piece in pieces]
    rows, depth = sum(b.shape[0] for b in pieces[0]), pieces[0][0].shape[1]
    columns = weights.shape[1]

    def kernel(*args):
        parts, w_ref = args[: len(refs)], args[len(refs)]
        before = args[len(refs) + 1] if so_far is not None else None
        out, total = args[-2:]
        at_ref = 0
        for k, count in enumerate(counts):
            start = 0
            for block in parts[at_ref : at_ref + count]:
                at = slice(start, start + block.shape[0])
                start += block.shape[0]
                w = w_ref[(first + k) * depth : (first + k + 1) * depth, :]
                o = jnp.dot(block[...], w, preferred_element_type=jnp.float32)
                if k > 0:
                    o = total[at, :] + o
                elif before is not None:
                    o = before[at, :] + o
                if k == len(counts) - 1:
                    out[at, :] = o.astype(out_type)
                else:
                    total[at, :] = o
            at_ref += count

    inputs = refs + [weights] + ([so_far] if so_far is not None else [])
    return pl.pallas_call(
        kernel,
        out_shape=jax.ShapeDtypeStruct((rows, columns), out_type),
        in_specs=[VM] * len(inputs),
        out_specs=VM,
        scratch_shapes=[pltpu.VMEM((rows, columns), jnp.float32)],
        cost_estimate=pl.CostEstimate(
            flops=2 * rows * depth * columns * len(pieces),
            bytes_accessed=len(pieces) * depth * (columns + rows) * 2,
            transcendentals=0,
        ),
        compiler_params=pltpu.CompilerParams(vmem_limit_bytes=32 * 2**20),
    )(*inputs)


def shift_y(x, d, low=0):
    return ctx_permute(x, lambda z, y, c: (z, (y + d) % NY, c) if z >= low else None)


def ring_y(x, low):
    return [shift_y(x, d, low) for d in (1, -1, 2)]


def per_device(queries, keys, values, out_weight):
    rows = queries.shape[0]
    ctx = lax.axis_index("ctx")
    head = lax.axis_index("head")
    z, y, c = ctx // (NY * NC), ctx // NC % NY, ctx % NC
    i32 = lambda *v: jnp.stack([jnp.asarray(x, jnp.int32) for x in v])
    info = i32(c, y, z)
    swap = lambda z, y, c: (z, y, 1 - c)

    squares = values.reshape(rows // DH, DH, DH).transpose(0, 2, 1).reshape(rows, DH)
    kv, queries = lax.optimization_barrier((jnp.concatenate([keys, squares], axis=1), queries))
    q_own = queries.T.reshape(QPK, DH, rows)
    q = jnp.concatenate([q_own, ctx_permute(q_own, swap)], axis=0)
    lift = lambda x, d: ctx_permute(x, lambda z, y, c: (z + d, y, c) if z + d < NZ else None)
    unit = 2 * 2 * 2 * QPK * rows * rows * DH
    state = (
        jax.ShapeDtypeStruct((2 * QPK, 8, rows), jnp.float32),
        jax.ShapeDtypeStruct((2 * QPK, DH + ONES, rows), jnp.float32),
    )

    def attend(kernel, chunks, *args):
        return call(
            kernel,
            state,
            *args,
            info=info,
            flops=chunks * unit,
            scratch=[
                pltpu.VMEM((chunks * rows, DH), jnp.bfloat16),
                pltpu.VMEM((DH + ONES, chunks * rows), jnp.bfloat16),
            ],
        )

    def planes(lowest, blocks, m, acc):
        chunks = sum(b.shape[0] for b in blocks) // rows
        return attend(lambda *refs: plane_kernel(lowest, *refs), chunks, q, *blocks, m, acc)

    hz, hx = head // NX, head % NX
    order = [h * NX + (hx + s) % NX for h, s in ((hz, 0), (hz, -1), (hz, 1), (hz, 2))]
    order += [(1 - hz) * NX + (hx + s) % NX for s in (0, -1, 1, 2)]
    below = lift(kv, 1)
    row = [shift_y(kv, d) for d in (1, -1)]
    m, acc = attend(own_kernel, 1, q, kv)
    lower = [lift(below, 1), lift(below, 2)]
    near, kv_late, m, *row = lax.optimization_barrier((below, kv, m, *row))
    row.append(shift_y(kv_late, 2))
    near = [near, *ring_y(near, 1)]
    m, acc = attend(row_kernel, 3, q, *row, m, acc)
    m, *lower = lax.optimization_barrier((m, *lower))
    both = jnp.concatenate(lower, axis=0)
    r, l, f = ring_y(both, 2)
    near[0], both = lax.optimization_barrier((near[0], both))
    m, acc = planes((1,), near, m, acc)
    m, acc = planes((2, 3), [both], m, acc)
    m, order = lax.optimization_barrier((m, i32(*order)))
    weights = arrange(order, out_weight, QPK * DH)
    m, weights = lax.optimization_barrier((m, weights))
    m, acc = planes((2, 3), [r, l], m, acc)
    m, acc = planes((2, 3), [f], m, acc)
    own, own_log, send = call(
        share_kernel,
        (
            jax.ShapeDtypeStruct((QPK * DH, rows), jnp.float32),
            jax.ShapeDtypeStruct((8, rows), jnp.float32),
            jax.ShapeDtypeStruct((QPK * DH + ONES, rows), jnp.bfloat16),
        ),
        m, acc,
    )
    attended = call(
        join_kernel,
        (jax.ShapeDtypeStruct((rows // 2, QPK * DH), jnp.bfloat16),) * 2,
        own, own_log, ctx_permute(send, swap),
    )

    far = [head_permute(a, 1, 0) for a in attended]

    def ring_x(halves):
        r = [head_permute(a, 0, 1) for a in halves]
        l = [head_permute(a, 0, -1) for a in halves]
        return r, l, [head_permute(r[0], 0, 1), head_permute(l[1], 0, -1)]

    r, l, f = ring_x(attended)
    far_r, far_l, far_f = ring_x(far)
    total = project(0, [attended, r, l], weights, None, jnp.float32)
    far_r[1], far_l[0], total = lax.optimization_barrier((far_r[1], far_l[0], total))
    total = project(3, [f, far, far_r, far_l], weights, total, jnp.float32)
    return project(7, [far_f], weights, total, jnp.bfloat16)


def solution(mesh):
    return jax.shard_map(
        per_device,
        mesh=mesh,
        in_specs=(P("ctx", "head"), P("ctx", "head"), P("ctx", "head"), P(None, "head")),
        out_specs=P("ctx", "head"),
        check_vma=False,
    )
```

```python
import math

import jax
import jax.numpy as jnp
from jax import lax
from jax.experimental import pallas as pl
from jax.experimental.pallas import tpu as pltpu
from jax.sharding import PartitionSpec as P

DH = 128
QPK = 4
SCALE2 = math.log2(math.e) * DH ** (-0.5)
NEG = -1e30

NZ, NY, NC = 4, 4, 2
NH, NX = 2, 4

TILE = 256
BESIDE = 4
PIECE = 512
ONES = 16
ROOM = 100.0


def ctx_id(z, y, c):
    return (z * NY + y) * NC + c


def ctx_permute(x, target):
    pairs = []
    for z in range(NZ):
        for y in range(NY):
            for c in range(NC):
                to = target(z, y, c)
                if to is not None:
                    pairs.append((ctx_id(z, y, c), ctx_id(*to)))
    return lax.ppermute(x, "ctx", pairs)


def head_permute(x, dz, partner):
    pairs = [(h * NX + i, (h + dz) % NH * NX + partner(i)) for h in range(NH) for i in range(NX)]
    return lax.ppermute(x, "head", pairs)


ONE = lambda i: i ^ 1
OTHER = lambda i: 3 - i
ACROSS = lambda i: (i + 2) % 4


def load_kv(blocks, keys, values):
    at = 0
    for block in blocks:
        for i in range(0, block.shape[0], DH):
            keys[at : at + DH, :] = block[i : i + DH, :DH]
            values[:DH, at : at + DH] = block[i : i + DH, DH:]
            at += DH
    values[DH:, :at] = jnp.ones((ONES, at), jnp.bfloat16)
    return at


def sweep(slots, length, scores, *ways):
    per = length // TILE

    def turn(i, _):
        def place(u):
            j = i * BESIDE + u
            return slots[0] + j // per, pl.multiple_of(j % per * TILE, TILE)

        def go(rest):
            s = scores(*place(0))
            for u in range(BESIDE):
                after = scores(*place(u + 1)) if u + 1 < BESIDE else None
                rest(*place(u), s)
                s = after

        for way in ways:
            if isinstance(way, tuple):
                pl.when(way[0](place(0)[0]))(lambda rest=way[1]: go(rest))
            else:
                go(way)
        return 0

    lax.fori_loop(0, (slots[1] - slots[0]) * per // BESIDE, turn, 0)


def scores_of(q, keys, count):
    def scores(slot, r):
        rows = q[slot, :, pl.ds(r, TILE)]
        return [
            jnp.dot(keys[k : k + PIECE, :], rows, preferred_element_type=jnp.float32) * SCALE2
            for k in range(0, count, PIECE)
        ]

    return scores


def weigh(values, s, m, kept=None):
    total = None
    for k, one in enumerate(s):
        p = jnp.exp2(one - m[:1]).astype(jnp.bfloat16)
        o = jnp.dot(
            values[:, k * PIECE : (k + 1) * PIECE], p, preferred_element_type=jnp.float32
        )
        if kept is not None:
            o = jnp.where(kept[k], o, 0.0)
        total = o if total is None else total + o
    return total


def update(q, keys, values, count, m_in, acc_in, m_out, acc_out, kept):
    scores = scores_of(q, keys, count)
    squares = jnp.dot(
        keys[:count, :] * keys[:count, :], jnp.ones((DH, DH), jnp.bfloat16), preferred_element_type=jnp.float32
    )
    longest = jnp.sqrt(jnp.max(squares, axis=0, keepdims=True))[:, :1] * (1.02 * SCALE2)
    near = []
    for t in range(2):
        over = None
        for slot in range(t * QPK, (t + 1) * QPK):
            reach = m_in[slot, 1:2, :] * longest - m_in[slot, :1, :]
            over = reach if over is None else jnp.maximum(over, reach)
        near.append(jnp.max(over) < ROOM)
    near_at = lambda slot: jnp.where(slot < QPK, near[0], near[1])

    def stay(slot, r, s):
        rows = pl.ds(r, TILE)
        m = m_in[slot, :, rows]
        m_out[slot, :, rows] = m
        acc_out[slot, :, rows] = acc_in[slot, :, rows] + weigh(values, s, m, kept)

    def move(slot, r, s):
        rows = pl.ds(r, TILE)
        m_old = m_in[slot, :, rows]
        m = m_old[:1]
        for one, keep in zip(s, kept):
            m = jnp.maximum(m, jnp.where(keep, jnp.max(one, axis=0, keepdims=True), NEG))
        shrink = jnp.exp2(m_old[:1] - m)
        m_out[slot, :, rows] = jnp.concatenate([m, m_old[1:]], axis=0)
        acc_out[slot, :, rows] = acc_in[slot, :, rows] * shrink + weigh(values, s, m, kept)

    sweep(
        (0, 2 * QPK), q.shape[2], scores, (near_at, stay), (lambda slot: jnp.logical_not(near_at(slot)), move)
    )


def own_kernel(info, q, own, m_out, acc_out, keys, values):
    n = own.shape[0]
    count = load_kv((own,), keys, values)
    plain = scores_of(q, keys, count)

    def masked(slot, r):
        s = plain(slot, r)
        i = r + lax.broadcasted_iota(jnp.int32, (PIECE, TILE), 1)
        j = lax.broadcasted_iota(jnp.int32, (PIECE, TILE), 0)
        return [jnp.where(j + k * PIECE <= i, one, NEG) for k, one in enumerate(s)]

    def rest(slot, r, s):
        rows = pl.ds(r, TILE)
        m = jnp.max(s[0], axis=0, keepdims=True)
        for one in s[1:]:
            m = jnp.maximum(m, jnp.max(one, axis=0, keepdims=True))
        m_out[slot, :1, rows] = m
        acc_out[slot, :, rows] = weigh(values, s, m)

    sweep((0, QPK), n, masked, rest)

    @pl.when(info[0] == 0)
    def _():
        sweep((QPK, 2 * QPK), n, plain, rest)

    @pl.when(info[0] != 0)
    def _():
        m_out[QPK:, :1, :] = jnp.full((QPK, 1, n), NEG, jnp.float32)
        acc_out[QPK:] = jnp.zeros((QPK, DH + ONES, n), jnp.float32)

    for slot in range(2 * QPK):
        rows = q[slot].astype(jnp.float32)
        length = jnp.sqrt(jnp.sum(rows * rows, axis=0, keepdims=True))
        m_out[slot, 1:, :] = jnp.broadcast_to(length, (7, n))


def row_kernel(info, q, one_ref, other_ref, across_ref, m_in, acc_in, m_out, acc_out, keys, values):
    y = info[1]
    n = one_ref.shape[0]

    @pl.when(y == 0)
    def _():
        m_out[...] = m_in[...]
        acc_out[...] = acc_in[...]

    @pl.when(y != 0)
    def _():
        count = load_kv((one_ref, other_ref, across_ref), keys, values)
        before = ((y == 1) | (y == 3), y >= 2, y >= 2)
        kept = [before[k * PIECE // n] for k in range(count // PIECE)]
        update(q, keys, values, count, m_in, acc_in, m_out, acc_out, kept)


def plane_kernel(lowest, info, q, *refs):
    blocks, (m_in, acc_in, m_out, acc_out, keys, values) = refs[:-6], refs[-6:]
    z = info[2]

    @pl.when(z < min(lowest))
    def _():
        m_out[...] = m_in[...]
        acc_out[...] = acc_in[...]

    @pl.when(z >= min(lowest))
    def _():
        count = load_kv(blocks, keys, values)
        n = blocks[0].shape[0] // len(lowest)
        kept = [z >= lowest[k * PIECE // n % len(lowest)] for k in range(count // PIECE)]
        update(q, keys, values, count, m_in, acc_in, m_out, acc_out, kept)


def share_kernel(m, acc, own_out, own_log, send):
    rows = own_out.shape[1]
    parts = []
    for slot in range(2 * QPK):
        t, h = slot // QPK, slot % QPK
        total = acc[slot, DH : DH + 1, :]
        some = total > 0.0
        total = jnp.where(some, total, 1.0)
        o = acc[slot, :DH, :] / total
        log_total = jnp.where(some, m[slot, :1, :] + jnp.log2(total), NEG)
        columns = slice(h * DH, (h + 1) * DH)
        if t == 0:
            own_out[columns, :] = o
            own_log[h : h + 1, :] = log_total
        else:
            send[columns, :] = o.astype(jnp.bfloat16)
            for _ in range(3):
                parts.append(log_total.astype(jnp.bfloat16).astype(jnp.float32))
                log_total = log_total - parts[-1]
    parts += [jnp.zeros((1, rows), jnp.float32)] * (ONES - len(parts))
    send[QPK * DH :, :] = jnp.concatenate(parts, axis=0).astype(jnp.bfloat16)


def join_kernel(own_in, own_log, got, top_out, low_out):
    theirs = got[QPK * DH :, :].astype(jnp.float32)
    for h in range(QPK):
        a = own_log[h : h + 1, :]
        b = theirs[3 * h : 3 * h + 1, :] + theirs[3 * h + 1 : 3 * h + 2, :] + theirs[3 * h + 2 : 3 * h + 3, :]
        top = jnp.maximum(a, b)
        a, b = jnp.exp2(a - top), jnp.exp2(b - top)
        share = 1.0 / (a + b)
        columns = slice(h * DH, (h + 1) * DH)
        o = own_in[columns, :] * (a * share) + got[columns, :].astype(jnp.float32) * (b * share)
        o = o.T.astype(jnp.bfloat16)
        half = top_out.shape[0]
        top_out[:, columns] = o[:half]
        low_out[:, columns] = o[half:]


VM = pl.BlockSpec(memory_space=pltpu.VMEM)
SM = pl.BlockSpec(memory_space=pltpu.SMEM)


def call(kernel, out_shape, *args, info=None, flops=0, scratch=()):
    size = sum(a.size * a.dtype.itemsize for a in args)
    many = isinstance(out_shape, tuple)
    first = [] if info is None else [info]
    return pl.pallas_call(
        kernel,
        out_shape=out_shape,
        in_specs=[SM] * len(first) + [VM] * len(args),
        out_specs=tuple(VM for _ in out_shape) if many else VM,
        scratch_shapes=scratch,
        cost_estimate=pl.CostEstimate(flops=flops, bytes_accessed=size, transcendentals=0),
        compiler_params=pltpu.CompilerParams(vmem_limit_bytes=22 * 2**20),
    )(*first, *args)


def arrange(order, out_weight, depth):
    count = out_weight.shape[0] // depth

    def kernel(order_ref, w_ref, out, sems):
        copies = []
        for k in range(count):
            start = pl.multiple_of(order_ref[k] * depth, depth)
            copies.append(
                pltpu.make_async_copy(
                    w_ref.at[pl.ds(start, depth), :], out.at[pl.ds(k * depth, depth), :], sems.at[k]
                )
            )
            copies[-1].start()
        for copy in copies:
            copy.wait()

    return pl.pallas_call(
        kernel,
        out_shape=jax.ShapeDtypeStruct(out_weight.shape, out_weight.dtype),
        in_specs=[SM, pl.BlockSpec(memory_space=pltpu.HBM)],
        out_specs=VM,
        scratch_shapes=[pltpu.SemaphoreType.DMA((count,))],
        compiler_params=pltpu.CompilerParams(vmem_limit_bytes=22 * 2**20),
    )(order, out_weight)


def project(first, pieces, weights, so_far, out_type):
    refs = [block for piece in pieces for block in piece]
    counts = [len(piece) for piece in pieces]
    rows, depth = sum(b.shape[0] for b in pieces[0]), pieces[0][0].shape[1]
    columns = weights.shape[1]

    def kernel(*args):
        parts, w_ref = args[: len(refs)], args[len(refs)]
        before = args[len(refs) + 1] if so_far is not None else None
        out, total = args[-2:]
        at_ref = 0
        for k, count in enumerate(counts):
            start = 0
            for block in parts[at_ref : at_ref + count]:
                at = slice(start, start + block.shape[0])
                start += block.shape[0]
                w = w_ref[(first + k) * depth : (first + k + 1) * depth, :]
                o = jnp.dot(block[...], w, preferred_element_type=jnp.float32)
                if k > 0:
                    o = total[at, :] + o
                elif before is not None:
                    o = before[at, :] + o
                if k == len(counts) - 1:
                    out[at, :] = o.astype(out_type)
                else:
                    total[at, :] = o
            at_ref += count

    inputs = refs + [weights] + ([so_far] if so_far is not None else [])
    return pl.pallas_call(
        kernel,
        out_shape=jax.ShapeDtypeStruct((rows, columns), out_type),
        in_specs=[VM] * len(inputs),
        out_specs=VM,
        scratch_shapes=[pltpu.VMEM((rows, columns), jnp.float32)],
        cost_estimate=pl.CostEstimate(
            flops=2 * rows * depth * columns * len(pieces),
            bytes_accessed=len(pieces) * depth * (columns + rows) * 2,
            transcendentals=0,
        ),
        compiler_params=pltpu.CompilerParams(vmem_limit_bytes=22 * 2**20),
    )(*inputs)


def swap_y(x, partner, low=0):
    return ctx_permute(x, lambda z, y, c: (z, partner(y), c) if z >= low else None)


def ring_y(x, low):
    return [swap_y(x, partner, low) for partner in (ONE, OTHER, ACROSS)]


def per_device(queries, keys, values, out_weight):
    rows = queries.shape[0]
    ctx = lax.axis_index("ctx")
    head = lax.axis_index("head")
    z, y, c = ctx // (NY * NC), ctx // NC % NY, ctx % NC
    i32 = lambda *v: jnp.stack([jnp.asarray(x, jnp.int32) for x in v])
    info = i32(c, y, z)
    swap = lambda z, y, c: (z, y, 1 - c)

    squares = values.reshape(rows // DH, DH, DH).transpose(0, 2, 1).reshape(rows, DH)
    kv, queries = lax.optimization_barrier((jnp.concatenate([keys, squares], axis=1), queries))
    q_own = queries.T.reshape(QPK, DH, rows)
    q = jnp.concatenate([q_own, ctx_permute(q_own, swap)], axis=0)
    lift = lambda x, d: ctx_permute(x, lambda z, y, c: (z + d, y, c) if z + d < NZ else None)
    unit = 2 * 2 * 2 * QPK * rows * rows * DH
    state = (
        jax.ShapeDtypeStruct((2 * QPK, 8, rows), jnp.float32),
        jax.ShapeDtypeStruct((2 * QPK, DH + ONES, rows), jnp.float32),
    )

    def attend(kernel, chunks, *args):
        return call(
            kernel,
            state,
            *args,
            info=info,
            flops=chunks * unit,
            scratch=[
                pltpu.VMEM((chunks * rows, DH), jnp.bfloat16),
                pltpu.VMEM((DH + ONES, chunks * rows), jnp.bfloat16),
            ],
        )

    def planes(lowest, blocks, m, acc):
        chunks = sum(b.shape[0] for b in blocks) // rows
        return attend(lambda *refs: plane_kernel(lowest, *refs), chunks, q, *blocks, m, acc)

    hz, hx = head // NX, head % NX
    along = (hx, hx + 1 - hx % 2 * 2, 3 - hx, (hx + 2) % NX)
    order = [h * NX + i for h in (hz, 1 - hz) for i in along]
    below = lift(kv, 1)
    row = [swap_y(kv, partner) for partner in (ONE, OTHER)]
    m, acc = attend(own_kernel, 1, q, kv)
    lower = [lift(below, 1), lift(below, 2)]
    near, kv_late, m, *row = lax.optimization_barrier((below, kv, m, *row))
    row.append(swap_y(kv_late, ACROSS))
    near = [near, *ring_y(near, 1)]
    m, acc = attend(row_kernel, 3, q, *row, m, acc)
    m, *lower = lax.optimization_barrier((m, *lower))
    both = jnp.concatenate(lower, axis=0)
    one, other, across = ring_y(both, 2)
    near[0], both = lax.optimization_barrier((near[0], both))
    m, acc = planes((1,), near, m, acc)
    m, acc = planes((2, 3), [both], m, acc)
    m, order = lax.optimization_barrier((m, i32(*order)))
    weights = arrange(order, out_weight, QPK * DH)
    m, weights = lax.optimization_barrier((m, weights))
    m, acc = planes((2, 3), [one, other], m, acc)
    m, acc = planes((2, 3), [across], m, acc)
    own, own_log, send = call(
        share_kernel,
        (
            jax.ShapeDtypeStruct((QPK * DH, rows), jnp.float32),
            jax.ShapeDtypeStruct((8, rows), jnp.float32),
            jax.ShapeDtypeStruct((QPK * DH + ONES, rows), jnp.bfloat16),
        ),
        m, acc,
    )
    attended = call(
        join_kernel,
        (jax.ShapeDtypeStruct((rows // 2, QPK * DH), jnp.bfloat16),) * 2,
        own, own_log, ctx_permute(send, swap),
    )

    far = [head_permute(a, 1, lambda i: i) for a in attended]

    def ring_x(halves):
        one = [head_permute(a, 0, ONE) for a in halves]
        other = [head_permute(a, 0, OTHER) for a in halves]
        return one, other, [head_permute(one[0], 0, OTHER), head_permute(other[1], 0, ONE)]

    one, other, across = ring_x(attended)
    far_one, far_other, far_across = ring_x(far)
    total = project(0, [attended, one, other], weights, None, jnp.float32)
    far_one[1], far_other[0], total = lax.optimization_barrier((far_one[1], far_other[0], total))
    total = project(3, [across, far, far_one, far_other], weights, total, jnp.float32)
    return project(7, [far_across], weights, total, jnp.bfloat16)


def solution(mesh):
    return jax.shard_map(
        per_device,
        mesh=mesh,
        in_specs=(P("ctx", "head"), P("ctx", "head"), P("ctx", "head"), P(None, "head")),
        out_specs=P("ctx", "head"),
        check_vma=False,
    )
```

```python
import math

import jax
import jax.numpy as jnp
from jax import lax
from jax.experimental import pallas as pl
from jax.experimental.pallas import tpu as pltpu
from jax.sharding import Mesh
from jax.sharding import PartitionSpec as P

DH = 128
QPK = 4
SCALE2 = math.log2(math.e) * DH ** (-0.5)
NEG = -1e30

NZ, NY, NC = 4, 4, 2
CTX = ("z", "y", "c")
NH, NX = 2, 4

TILE = 256
BESIDE = 4
PIECE = 512
ONES = 16
ROOM = 100.0


def ctx_id(z, y, c):
    return (z * NY + y) * NC + c


def ctx_permute(x, target):
    pairs = []
    for z in range(NZ):
        for y in range(NY):
            for c in range(NC):
                to = target(z, y, c)
                if to is not None:
                    pairs.append((ctx_id(z, y, c), ctx_id(*to)))
    return lax.ppermute(x, CTX, pairs)


def head_permute(x, dz, partner):
    pairs = [(h * NX + i, (h + dz) % NH * NX + partner(i)) for h in range(NH) for i in range(NX)]
    return lax.ppermute(x, "head", pairs)


ONE = lambda i: i ^ 1
OTHER = lambda i: 3 - i
ACROSS = lambda i: (i + 2) % 4


def load_kv(blocks, keys, values):
    at = 0
    for block in blocks:
        for i in range(0, block.shape[0], DH):
            keys[at : at + DH, :] = block[i : i + DH, :DH]
            values[:DH, at : at + DH] = block[i : i + DH, DH:]
            at += DH
    values[DH:, :at] = jnp.ones((ONES, at), jnp.bfloat16)
    return at


def sweep(slots, length, scores, *ways):
    per = length // TILE

    def turn(i, _):
        def place(u):
            j = i * BESIDE + u
            return slots[0] + j // per, pl.multiple_of(j % per * TILE, TILE)

        def go(rest):
            s = scores(*place(0))
            for u in range(BESIDE):
                after = scores(*place(u + 1)) if u + 1 < BESIDE else None
                rest(*place(u), s)
                s = after

        for way in ways:
            if isinstance(way, tuple):
                pl.when(way[0](place(0)[0]))(lambda rest=way[1]: go(rest))
            else:
                go(way)
        return 0

    lax.fori_loop(0, (slots[1] - slots[0]) * per // BESIDE, turn, 0)


def scores_of(q, keys, count):
    def scores(slot, r):
        rows = q[slot, :, pl.ds(r, TILE)]
        return [
            jnp.dot(keys[k : k + PIECE, :], rows, preferred_element_type=jnp.float32) * SCALE2
            for k in range(0, count, PIECE)
        ]

    return scores


def weigh(values, s, m, kept=None):
    total = None
    for k, one in enumerate(s):
        p = jnp.exp2(one - m[:1]).astype(jnp.bfloat16)
        o = jnp.dot(
            values[:, k * PIECE : (k + 1) * PIECE], p, preferred_element_type=jnp.float32
        )
        if kept is not None:
            o = jnp.where(kept[k], o, 0.0)
        total = o if total is None else total + o
    return total


def update(q, keys, values, count, m_in, acc_in, m_out, acc_out, kept):
    scores = scores_of(q, keys, count)
    squares = jnp.dot(
        keys[:count, :] * keys[:count, :], jnp.ones((DH, DH), jnp.bfloat16), preferred_element_type=jnp.float32
    )
    longest = jnp.sqrt(jnp.max(squares, axis=0, keepdims=True))[:, :1] * (1.02 * SCALE2)
    near = []
    for t in range(2):
        over = None
        for slot in range(t * QPK, (t + 1) * QPK):
            reach = m_in[slot, 1:2, :] * longest - m_in[slot, :1, :]
            over = reach if over is None else jnp.maximum(over, reach)
        near.append(jnp.max(over) < ROOM)
    near_at = lambda slot: jnp.where(slot < QPK, near[0], near[1])

    def stay(slot, r, s):
        rows = pl.ds(r, TILE)
        m = m_in[slot, :, rows]
        m_out[slot, :, rows] = m
        acc_out[slot, :, rows] = acc_in[slot, :, rows] + weigh(values, s, m, kept)

    def move(slot, r, s):
        rows = pl.ds(r, TILE)
        m_old = m_in[slot, :, rows]
        m = m_old[:1]
        for one, keep in zip(s, kept):
            m = jnp.maximum(m, jnp.where(keep, jnp.max(one, axis=0, keepdims=True), NEG))
        shrink = jnp.exp2(m_old[:1] - m)
        m_out[slot, :, rows] = jnp.concatenate([m, m_old[1:]], axis=0)
        acc_out[slot, :, rows] = acc_in[slot, :, rows] * shrink + weigh(values, s, m, kept)

    sweep(
        (0, 2 * QPK), q.shape[2], scores, (near_at, stay), (lambda slot: jnp.logical_not(near_at(slot)), move)
    )


def own_kernel(info, q, own, m_out, acc_out, keys, values):
    n = own.shape[0]
    count = load_kv((own,), keys, values)
    plain = scores_of(q, keys, count)

    def masked(slot, r):
        s = plain(slot, r)
        i = r + lax.broadcasted_iota(jnp.int32, (PIECE, TILE), 1)
        j = lax.broadcasted_iota(jnp.int32, (PIECE, TILE), 0)
        return [jnp.where(j + k * PIECE <= i, one, NEG) for k, one in enumerate(s)]

    def rest(slot, r, s):
        rows = pl.ds(r, TILE)
        m = jnp.max(s[0], axis=0, keepdims=True)
        for one in s[1:]:
            m = jnp.maximum(m, jnp.max(one, axis=0, keepdims=True))
        m_out[slot, :1, rows] = m
        acc_out[slot, :, rows] = weigh(values, s, m)

    sweep((0, QPK), n, masked, rest)

    @pl.when(info[0] == 0)
    def _():
        sweep((QPK, 2 * QPK), n, plain, rest)

    @pl.when(info[0] != 0)
    def _():
        m_out[QPK:, :1, :] = jnp.full((QPK, 1, n), NEG, jnp.float32)
        acc_out[QPK:] = jnp.zeros((QPK, DH + ONES, n), jnp.float32)

    for slot in range(2 * QPK):
        rows = q[slot].astype(jnp.float32)
        length = jnp.sqrt(jnp.sum(rows * rows, axis=0, keepdims=True))
        m_out[slot, 1:, :] = jnp.broadcast_to(length, (7, n))


def row_kernel(info, q, row, m_in, acc_in, m_out, acc_out, keys, values):
    y = info[1]
    n = row.shape[0] // NY

    @pl.when(y == 0)
    def _():
        m_out[...] = m_in[...]
        acc_out[...] = acc_in[...]

    @pl.when(y != 0)
    def _():
        count = load_kv((row.at[: (NY - 1) * n],), keys, values)
        kept = [y > k * PIECE // n for k in range(count // PIECE)]
        update(q, keys, values, count, m_in, acc_in, m_out, acc_out, kept)


def plane_kernel(lowest, info, q, *refs):
    blocks, (m_in, acc_in, m_out, acc_out, keys, values) = refs[:-6], refs[-6:]
    z = info[2]

    @pl.when(z < min(lowest))
    def _():
        m_out[...] = m_in[...]
        acc_out[...] = acc_in[...]

    @pl.when(z >= min(lowest))
    def _():
        count = load_kv(blocks, keys, values)
        n = blocks[0].shape[0] // len(lowest)
        kept = [z >= lowest[k * PIECE // n % len(lowest)] for k in range(count // PIECE)]
        update(q, keys, values, count, m_in, acc_in, m_out, acc_out, kept)


def share_kernel(m, acc, own_out, own_log, send):
    rows = own_out.shape[1]
    parts = []
    for slot in range(2 * QPK):
        t, h = slot // QPK, slot % QPK
        total = acc[slot, DH : DH + 1, :]
        some = total > 0.0
        total = jnp.where(some, total, 1.0)
        o = acc[slot, :DH, :] / total
        log_total = jnp.where(some, m[slot, :1, :] + jnp.log2(total), NEG)
        columns = slice(h * DH, (h + 1) * DH)
        if t == 0:
            own_out[columns, :] = o
            own_log[h : h + 1, :] = log_total
        else:
            send[columns, :] = o.astype(jnp.bfloat16)
            for _ in range(3):
                parts.append(log_total.astype(jnp.bfloat16).astype(jnp.float32))
                log_total = log_total - parts[-1]
    parts += [jnp.zeros((1, rows), jnp.float32)] * (ONES - len(parts))
    send[QPK * DH :, :] = jnp.concatenate(parts, axis=0).astype(jnp.bfloat16)


def join_kernel(own_in, own_log, got, top_out, low_out):
    theirs = got[QPK * DH :, :].astype(jnp.float32)
    for h in range(QPK):
        a = own_log[h : h + 1, :]
        b = theirs[3 * h : 3 * h + 1, :] + theirs[3 * h + 1 : 3 * h + 2, :] + theirs[3 * h + 2 : 3 * h + 3, :]
        top = jnp.maximum(a, b)
        a, b = jnp.exp2(a - top), jnp.exp2(b - top)
        share = 1.0 / (a + b)
        columns = slice(h * DH, (h + 1) * DH)
        o = own_in[columns, :] * (a * share) + got[columns, :].astype(jnp.float32) * (b * share)
        o = o.T.astype(jnp.bfloat16)
        half = top_out.shape[0]
        top_out[:, columns] = o[:half]
        low_out[:, columns] = o[half:]


VM = pl.BlockSpec(memory_space=pltpu.VMEM)
SM = pl.BlockSpec(memory_space=pltpu.SMEM)


def call(kernel, out_shape, *args, info=None, flops=0, scratch=()):
    size = sum(a.size * a.dtype.itemsize for a in args)
    many = isinstance(out_shape, tuple)
    first = [] if info is None else [info]
    return pl.pallas_call(
        kernel,
        out_shape=out_shape,
        in_specs=[SM] * len(first) + [VM] * len(args),
        out_specs=tuple(VM for _ in out_shape) if many else VM,
        scratch_shapes=scratch,
        cost_estimate=pl.CostEstimate(flops=flops, bytes_accessed=size, transcendentals=0),
        compiler_params=pltpu.CompilerParams(vmem_limit_bytes=22 * 2**20),
    )(*first, *args)


def arrange(order, out_weight, depth):
    count = out_weight.shape[0] // depth

    def kernel(order_ref, w_ref, out, sems):
        copies = []
        for k in range(count):
            start = pl.multiple_of(order_ref[k] * depth, depth)
            copies.append(
                pltpu.make_async_copy(
                    w_ref.at[pl.ds(start, depth), :], out.at[pl.ds(k * depth, depth), :], sems.at[k]
                )
            )
            copies[-1].start()
        for copy in copies:
            copy.wait()

    return pl.pallas_call(
        kernel,
        out_shape=jax.ShapeDtypeStruct(out_weight.shape, out_weight.dtype),
        in_specs=[SM, pl.BlockSpec(memory_space=pltpu.HBM)],
        out_specs=VM,
        scratch_shapes=[pltpu.SemaphoreType.DMA((count,))],
        compiler_params=pltpu.CompilerParams(vmem_limit_bytes=22 * 2**20),
    )(order, out_weight)


def project(first, pieces, weights, so_far, out_type):
    refs = [block for piece in pieces for block in piece]
    counts = [len(piece) for piece in pieces]
    rows, depth = sum(b.shape[0] for b in pieces[0]), pieces[0][0].shape[1]
    columns = weights.shape[1]

    def kernel(*args):
        parts, w_ref = args[: len(refs)], args[len(refs)]
        before = args[len(refs) + 1] if so_far is not None else None
        out, total = args[-2:]
        at_ref = 0
        for k, count in enumerate(counts):
            start = 0
            for block in parts[at_ref : at_ref + count]:
                at = slice(start, start + block.shape[0])
                start += block.shape[0]
                w = w_ref[(first + k) * depth : (first + k + 1) * depth, :]
                o = jnp.dot(block[...], w, preferred_element_type=jnp.float32)
                if k > 0:
                    o = total[at, :] + o
                elif before is not None:
                    o = before[at, :] + o
                if k == len(counts) - 1:
                    out[at, :] = o.astype(out_type)
                else:
                    total[at, :] = o
            at_ref += count

    inputs = refs + [weights] + ([so_far] if so_far is not None else [])
    return pl.pallas_call(
        kernel,
        out_shape=jax.ShapeDtypeStruct((rows, columns), out_type),
        in_specs=[VM] * len(inputs),
        out_specs=VM,
        scratch_shapes=[pltpu.VMEM((rows, columns), jnp.float32)],
        cost_estimate=pl.CostEstimate(
            flops=2 * rows * depth * columns * len(pieces),
            bytes_accessed=len(pieces) * depth * (columns + rows) * 2,
            transcendentals=0,
        ),
        compiler_params=pltpu.CompilerParams(vmem_limit_bytes=22 * 2**20),
    )(*inputs)


def swap_y(x, partner, low=0):
    return ctx_permute(x, lambda z, y, c: (z, partner(y), c) if z >= low else None)


def ring_y(x, low):
    return [swap_y(x, partner, low) for partner in (ONE, OTHER, ACROSS)]


def per_device(queries, keys, values, out_weight):
    rows = queries.shape[0]
    head = lax.axis_index("head")
    z, y, c = (lax.axis_index(axis) for axis in CTX)
    i32 = lambda *v: jnp.stack([jnp.asarray(x, jnp.int32) for x in v])
    info = i32(c, y, z)
    swap = lambda z, y, c: (z, y, 1 - c)

    squares = values.reshape(rows // DH, DH, DH).transpose(0, 2, 1).reshape(rows, DH)
    kv, queries = lax.optimization_barrier((jnp.concatenate([keys, squares], axis=1), queries))
    q_own = queries.T.reshape(QPK, DH, rows)
    q = jnp.concatenate([q_own, ctx_permute(q_own, swap)], axis=0)
    lift = lambda x, d: ctx_permute(x, lambda z, y, c: (z + d, y, c) if z + d < NZ else None)
    unit = 2 * 2 * 2 * QPK * rows * rows * DH
    state = (
        jax.ShapeDtypeStruct((2 * QPK, 8, rows), jnp.float32),
        jax.ShapeDtypeStruct((2 * QPK, DH + ONES, rows), jnp.float32),
    )

    def attend(kernel, chunks, *args):
        return call(
            kernel,
            state,
            *args,
            info=info,
            flops=chunks * unit,
            scratch=[
                pltpu.VMEM((chunks * rows, DH), jnp.bfloat16),
                pltpu.VMEM((DH + ONES, chunks * rows), jnp.bfloat16),
            ],
        )

    def planes(lowest, blocks, m, acc):
        chunks = sum(b.shape[0] for b in blocks) // rows
        return attend(lambda *refs: plane_kernel(lowest, *refs), chunks, q, *blocks, m, acc)

    hz, hx = head // NX, head % NX
    along = (hx, hx + 1 - hx % 2 * 2, 3 - hx, (hx + 2) % NX)
    order = [h * NX + i for h in (hz, 1 - hz) for i in along]
    row = lax.all_gather(kv, "y", axis=0, tiled=True)
    below = lift(kv, 1)
    m, acc = attend(own_kernel, 1, q, kv)
    lower = [lift(below, 1), lift(below, 2)]
    near = [below, *ring_y(below, 1)]
    m, *lower = lax.optimization_barrier((m, *lower))
    both = jnp.concatenate(lower, axis=0)
    one, other, across = ring_y(both, 2)
    near[0], both = lax.optimization_barrier((near[0], both))
    m, acc = planes((1,), near, m, acc)
    m, row = lax.optimization_barrier((m, row))
    m, acc = attend(row_kernel, 3, q, row, m, acc)
    m, acc = planes((2, 3), [both], m, acc)
    m, order = lax.optimization_barrier((m, i32(*order)))
    weights = arrange(order, out_weight, QPK * DH)
    m, weights = lax.optimization_barrier((m, weights))
    m, acc = planes((2, 3), [one, other], m, acc)
    m, acc = planes((2, 3), [across], m, acc)
    own, own_log, send = call(
        share_kernel,
        (
            jax.ShapeDtypeStruct((QPK * DH, rows), jnp.float32),
            jax.ShapeDtypeStruct((8, rows), jnp.float32),
            jax.ShapeDtypeStruct((QPK * DH + ONES, rows), jnp.bfloat16),
        ),
        m, acc,
    )
    attended = call(
        join_kernel,
        (jax.ShapeDtypeStruct((rows // 2, QPK * DH), jnp.bfloat16),) * 2,
        own, own_log, ctx_permute(send, swap),
    )

    far = [head_permute(a, 1, lambda i: i) for a in attended]

    def ring_x(halves):
        one = [head_permute(a, 0, ONE) for a in halves]
        other = [head_permute(a, 0, OTHER) for a in halves]
        return one, other, [head_permute(one[0], 0, OTHER), head_permute(other[1], 0, ONE)]

    one, other, across = ring_x(attended)
    far_one, far_other, far_across = ring_x(far)
    total = project(0, [attended, one, other], weights, None, jnp.float32)
    far_one[1], far_other[0], total = lax.optimization_barrier((far_one[1], far_other[0], total))
    total = project(3, [across, far, far_one, far_other], weights, total, jnp.float32)
    return project(7, [far_across], weights, total, jnp.bfloat16)


def solution(mesh):
    parts = Mesh(mesh.devices.reshape(NZ, NY, NC, NH * NX), (*CTX, "head"))
    return jax.shard_map(
        per_device,
        mesh=parts,
        in_specs=(P(CTX, "head"), P(CTX, "head"), P(CTX, "head"), P(None, "head")),
        out_specs=P(CTX, "head"),
        check_vma=False,
    )
```

```python
import math

import jax
import jax.numpy as jnp
from jax import lax
from jax.experimental import pallas as pl
from jax.experimental.pallas import tpu as pltpu
from jax.sharding import PartitionSpec as P

DH = 128
QPK = 4
SCALE2 = math.log2(math.e) * DH ** (-0.5)
NEG = -1e30

NZ, NY, NC = 4, 4, 2
NH, NX = 2, 4

TILE = 256
BESIDE = 4
PIECE = 512
ONES = 16
ROOM = 100.0


def ctx_id(z, y, c):
    return (z * NY + y) * NC + c


def ctx_permute(x, target):
    pairs = []
    for z in range(NZ):
        for y in range(NY):
            for c in range(NC):
                to = target(z, y, c)
                if to is not None:
                    pairs.append((ctx_id(z, y, c), ctx_id(*to)))
    return lax.ppermute(x, "ctx", pairs)


def head_permute(x, dz, partner):
    pairs = [(h * NX + i, (h + dz) % NH * NX + partner(i)) for h in range(NH) for i in range(NX)]
    return lax.ppermute(x, "head", pairs)


ONE = lambda i: i ^ 1
OTHER = lambda i: 3 - i
ACROSS = lambda i: (i + 2) % 4


def load_kv(blocks, keys, values):
    at = 0
    for block in blocks:
        for i in range(0, block.shape[0], DH):
            keys[at : at + DH, :] = block[i : i + DH, :DH]
            values[:DH, at : at + DH] = block[i : i + DH, DH:]
            at += DH
    values[DH:, :at] = jnp.ones((ONES, at), jnp.bfloat16)
    return at


def sweep(slots, length, scores, *ways):
    per = length // TILE

    def turn(i, _):
        def place(u):
            j = i * BESIDE + u
            return slots[0] + j // per, pl.multiple_of(j % per * TILE, TILE)

        def go(rest):
            s = scores(*place(0))
            for u in range(BESIDE):
                after = scores(*place(u + 1)) if u + 1 < BESIDE else None
                rest(*place(u), s)
                s = after

        for way in ways:
            if isinstance(way, tuple):
                pl.when(way[0](place(0)[0]))(lambda rest=way[1]: go(rest))
            else:
                go(way)
        return 0

    lax.fori_loop(0, (slots[1] - slots[0]) * per // BESIDE, turn, 0)


def scores_of(q, keys, count):
    def scores(slot, r):
        rows = q[slot, :, pl.ds(r, TILE)]
        return [
            jnp.dot(keys[k : k + PIECE, :], rows, preferred_element_type=jnp.float32) * SCALE2
            for k in range(0, count, PIECE)
        ]

    return scores


def weigh(values, s, m, kept=None):
    total = None
    for k, one in enumerate(s):
        p = jnp.exp2(one - m[:1]).astype(jnp.bfloat16)
        o = jnp.dot(
            values[:, k * PIECE : (k + 1) * PIECE], p, preferred_element_type=jnp.float32
        )
        if kept is not None:
            o = jnp.where(kept[k], o, 0.0)
        total = o if total is None else total + o
    return total


def update(q, keys, values, count, m_in, acc_in, m_out, acc_out, kept):
    scores = scores_of(q, keys, count)
    squares = jnp.dot(
        keys[:count, :] * keys[:count, :], jnp.ones((DH, DH), jnp.bfloat16), preferred_element_type=jnp.float32
    )
    longest = jnp.sqrt(jnp.max(squares, axis=0, keepdims=True))[:, :1] * (1.02 * SCALE2)
    near = []
    for t in range(2):
        over = None
        for slot in range(t * QPK, (t + 1) * QPK):
            reach = m_in[slot, 1:2, :] * longest - m_in[slot, :1, :]
            over = reach if over is None else jnp.maximum(over, reach)
        near.append(jnp.max(over) < ROOM)
    near_at = lambda slot: jnp.where(slot < QPK, near[0], near[1])

    def stay(slot, r, s):
        rows = pl.ds(r, TILE)
        m = m_in[slot, :, rows]
        m_out[slot, :, rows] = m
        acc_out[slot, :, rows] = acc_in[slot, :, rows] + weigh(values, s, m, kept)

    def move(slot, r, s):
        rows = pl.ds(r, TILE)
        m_old = m_in[slot, :, rows]
        m = m_old[:1]
        for one, keep in zip(s, kept):
            m = jnp.maximum(m, jnp.where(keep, jnp.max(one, axis=0, keepdims=True), NEG))
        shrink = jnp.exp2(m_old[:1] - m)
        m_out[slot, :, rows] = jnp.concatenate([m, m_old[1:]], axis=0)
        acc_out[slot, :, rows] = acc_in[slot, :, rows] * shrink + weigh(values, s, m, kept)

    sweep(
        (0, 2 * QPK), q.shape[2], scores, (near_at, stay), (lambda slot: jnp.logical_not(near_at(slot)), move)
    )


def own_kernel(info, q, own, m_out, acc_out, keys, values):
    n = own.shape[0]
    count = load_kv((own,), keys, values)
    plain = scores_of(q, keys, count)

    def masked(slot, r):
        s = plain(slot, r)
        i = r + lax.broadcasted_iota(jnp.int32, (PIECE, TILE), 1)
        j = lax.broadcasted_iota(jnp.int32, (PIECE, TILE), 0)
        return [jnp.where(j + k * PIECE <= i, one, NEG) for k, one in enumerate(s)]

    def rest(slot, r, s):
        rows = pl.ds(r, TILE)
        m = jnp.max(s[0], axis=0, keepdims=True)
        for one in s[1:]:
            m = jnp.maximum(m, jnp.max(one, axis=0, keepdims=True))
        m_out[slot, :1, rows] = m
        acc_out[slot, :, rows] = weigh(values, s, m)

    sweep((0, QPK), n, masked, rest)

    @pl.when(info[0] == 0)
    def _():
        sweep((QPK, 2 * QPK), n, plain, rest)

    @pl.when(info[0] != 0)
    def _():
        m_out[QPK:, :1, :] = jnp.full((QPK, 1, n), NEG, jnp.float32)
        acc_out[QPK:] = jnp.zeros((QPK, DH + ONES, n), jnp.float32)

    for slot in range(2 * QPK):
        rows = q[slot].astype(jnp.float32)
        length = jnp.sqrt(jnp.sum(rows * rows, axis=0, keepdims=True))
        m_out[slot, 1:, :] = jnp.broadcast_to(length, (7, n))


def row_kernel(info, q, one_ref, other_ref, across_ref, m_in, acc_in, m_out, acc_out, keys, values):
    y = info[1]
    n = one_ref.shape[0]

    @pl.when(y == 0)
    def _():
        m_out[...] = m_in[...]
        acc_out[...] = acc_in[...]

    @pl.when(y != 0)
    def _():
        count = load_kv((one_ref, other_ref, across_ref), keys, values)
        before = ((y == 1) | (y == 3), y >= 2, y >= 2)
        kept = [before[k * PIECE // n] for k in range(count // PIECE)]
        update(q, keys, values, count, m_in, acc_in, m_out, acc_out, kept)


def plane_kernel(lowest, info, q, *refs):
    blocks, (m_in, acc_in, m_out, acc_out, keys, values) = refs[:-6], refs[-6:]
    z = info[2]
    least = min(min(lows) for lows in lowest)

    @pl.when(z < least)
    def _():
        m_out[...] = m_in[...]
        acc_out[...] = acc_in[...]

    @pl.when(z >= least)
    def _():
        count = load_kv(blocks, keys, values)
        kept = []
        for block, lows in zip(blocks, lowest):
            rows = block.shape[0]
            kept += [z >= lows[k * len(lows) // rows] for k in range(0, rows, PIECE)]
        update(q, keys, values, count, m_in, acc_in, m_out, acc_out, kept)


def share_kernel(m, acc, own_out, own_log, send):
    rows = own_out.shape[1]
    parts = []
    for slot in range(2 * QPK):
        t, h = slot // QPK, slot % QPK
        total = acc[slot, DH : DH + 1, :]
        some = total > 0.0
        total = jnp.where(some, total, 1.0)
        o = acc[slot, :DH, :] / total
        log_total = jnp.where(some, m[slot, :1, :] + jnp.log2(total), NEG)
        columns = slice(h * DH, (h + 1) * DH)
        if t == 0:
            own_out[columns, :] = o
            own_log[h : h + 1, :] = log_total
        else:
            send[columns, :] = o.astype(jnp.bfloat16)
            for _ in range(3):
                parts.append(log_total.astype(jnp.bfloat16).astype(jnp.float32))
                log_total = log_total - parts[-1]
    parts += [jnp.zeros((1, rows), jnp.float32)] * (ONES - len(parts))
    send[QPK * DH :, :] = jnp.concatenate(parts, axis=0).astype(jnp.bfloat16)


def join_kernel(own_in, own_log, got, top_out, low_out):
    theirs = got[QPK * DH :, :].astype(jnp.float32)
    for h in range(QPK):
        a = own_log[h : h + 1, :]
        b = theirs[3 * h : 3 * h + 1, :] + theirs[3 * h + 1 : 3 * h + 2, :] + theirs[3 * h + 2 : 3 * h + 3, :]
        top = jnp.maximum(a, b)
        a, b = jnp.exp2(a - top), jnp.exp2(b - top)
        share = 1.0 / (a + b)
        columns = slice(h * DH, (h + 1) * DH)
        o = own_in[columns, :] * (a * share) + got[columns, :].astype(jnp.float32) * (b * share)
        o = o.T.astype(jnp.bfloat16)
        half = top_out.shape[0]
        top_out[:, columns] = o[:half]
        low_out[:, columns] = o[half:]


VM = pl.BlockSpec(memory_space=pltpu.VMEM)
SM = pl.BlockSpec(memory_space=pltpu.SMEM)


def call(kernel, out_shape, *args, info=None, flops=0, scratch=()):
    size = sum(a.size * a.dtype.itemsize for a in args)
    many = isinstance(out_shape, tuple)
    first = [] if info is None else [info]
    return pl.pallas_call(
        kernel,
        out_shape=out_shape,
        in_specs=[SM] * len(first) + [VM] * len(args),
        out_specs=tuple(VM for _ in out_shape) if many else VM,
        scratch_shapes=scratch,
        cost_estimate=pl.CostEstimate(flops=flops, bytes_accessed=size, transcendentals=0),
        compiler_params=pltpu.CompilerParams(vmem_limit_bytes=22 * 2**20),
    )(*first, *args)


def arrange(order, out_weight, depth):
    count = out_weight.shape[0] // depth

    def kernel(order_ref, w_ref, out, sems):
        copies = []
        for k in range(count):
            start = pl.multiple_of(order_ref[k] * depth, depth)
            copies.append(
                pltpu.make_async_copy(
                    w_ref.at[pl.ds(start, depth), :], out.at[pl.ds(k * depth, depth), :], sems.at[k]
                )
            )
            copies[-1].start()
        for copy in copies:
            copy.wait()

    return pl.pallas_call(
        kernel,
        out_shape=jax.ShapeDtypeStruct(out_weight.shape, out_weight.dtype),
        in_specs=[SM, pl.BlockSpec(memory_space=pltpu.HBM)],
        out_specs=VM,
        scratch_shapes=[pltpu.SemaphoreType.DMA((count,))],
        compiler_params=pltpu.CompilerParams(vmem_limit_bytes=22 * 2**20),
    )(order, out_weight)


def project(first, pieces, weights, so_far, out_type):
    refs = [block for piece in pieces for block in piece]
    counts = [len(piece) for piece in pieces]
    rows, depth = sum(b.shape[0] for b in pieces[0]), pieces[0][0].shape[1]
    columns = weights.shape[1]

    def kernel(*args):
        parts, w_ref = args[: len(refs)], args[len(refs)]
        before = args[len(refs) + 1] if so_far is not None else None
        out, total = args[-2:]
        at_ref = 0
        for k, count in enumerate(counts):
            start = 0
            for block in parts[at_ref : at_ref + count]:
                at = slice(start, start + block.shape[0])
                start += block.shape[0]
                w = w_ref[(first + k) * depth : (first + k + 1) * depth, :]
                o = jnp.dot(block[...], w, preferred_element_type=jnp.float32)
                if k > 0:
                    o = total[at, :] + o
                elif before is not None:
                    o = before[at, :] + o
                if k == len(counts) - 1:
                    out[at, :] = o.astype(out_type)
                else:
                    total[at, :] = o
            at_ref += count

    inputs = refs + [weights] + ([so_far] if so_far is not None else [])
    return pl.pallas_call(
        kernel,
        out_shape=jax.ShapeDtypeStruct((rows, columns), out_type),
        in_specs=[VM] * len(inputs),
        out_specs=VM,
        scratch_shapes=[pltpu.VMEM((rows, columns), jnp.float32)],
        cost_estimate=pl.CostEstimate(
            flops=2 * rows * depth * columns * len(pieces),
            bytes_accessed=len(pieces) * depth * (columns + rows) * 2,
            transcendentals=0,
        ),
        compiler_params=pltpu.CompilerParams(vmem_limit_bytes=22 * 2**20),
    )(*inputs)


def swap_y(x, partner, low=0):
    return ctx_permute(x, lambda z, y, c: (z, partner(y), c) if z >= low else None)


def ring_y(x, low):
    return [swap_y(x, partner, low) for partner in (ONE, OTHER, ACROSS)]


def per_device(queries, keys, values, out_weight):
    rows = queries.shape[0]
    ctx = lax.axis_index("ctx")
    head = lax.axis_index("head")
    z, y, c = ctx // (NY * NC), ctx // NC % NY, ctx % NC
    i32 = lambda *v: jnp.stack([jnp.asarray(x, jnp.int32) for x in v])
    info = i32(c, y, z)
    swap = lambda z, y, c: (z, y, 1 - c)

    squares = values.reshape(rows // DH, DH, DH).transpose(0, 2, 1).reshape(rows, DH)
    kv, queries = lax.optimization_barrier((jnp.concatenate([keys, squares], axis=1), queries))
    q_own = queries.T.reshape(QPK, DH, rows)
    q = jnp.concatenate([q_own, ctx_permute(q_own, swap)], axis=0)
    lift = lambda x, d: ctx_permute(x, lambda z, y, c: (z + d, y, c) if z + d < NZ else None)
    unit = 2 * 2 * 2 * QPK * rows * rows * DH
    state = (
        jax.ShapeDtypeStruct((2 * QPK, 8, rows), jnp.float32),
        jax.ShapeDtypeStruct((2 * QPK, DH + ONES, rows), jnp.float32),
    )

    def attend(kernel, chunks, *args):
        return call(
            kernel,
            state,
            *args,
            info=info,
            flops=chunks * unit,
            scratch=[
                pltpu.VMEM((chunks * rows, DH), jnp.bfloat16),
                pltpu.VMEM((DH + ONES, chunks * rows), jnp.bfloat16),
            ],
        )

    def planes(lowest, blocks, m, acc):
        chunks = sum(b.shape[0] for b in blocks) // rows
        return attend(lambda *refs: plane_kernel(lowest, *refs), chunks, q, *blocks, m, acc)

    hz, hx = head // NX, head % NX
    along = (hx, hx + 1 - hx % 2 * 2, 3 - hx, (hx + 2) % NX)
    order = [h * NX + i for h in (hz, 1 - hz) for i in along]
    below = lift(kv, 1)
    row = ring_y(kv, 0)
    m, acc = attend(own_kernel, 1, q, kv)
    lower = [lift(below, 1), lift(below, 2)]
    near, m, *row[:2] = lax.optimization_barrier((below, m, *row[:2]))
    near = [near, *ring_y(near, 1)]
    m, acc = attend(row_kernel, 3, q, *row, m, acc)
    m, *lower = lax.optimization_barrier((m, *lower))
    both = jnp.concatenate(lower, axis=0)
    one, other, across = ring_y(both, 2)
    near[0], both = lax.optimization_barrier((near[0], both))
    m, acc = planes([(1,)] * 4 + [(2, 3)], [*near, both], m, acc)
    m, order = lax.optimization_barrier((m, i32(*order)))
    weights = arrange(order, out_weight, QPK * DH)
    m, weights = lax.optimization_barrier((m, weights))
    m, acc = planes([(2, 3)] * 3, [one, other, across], m, acc)
    own, own_log, send = call(
        share_kernel,
        (
            jax.ShapeDtypeStruct((QPK * DH, rows), jnp.float32),
            jax.ShapeDtypeStruct((8, rows), jnp.float32),
            jax.ShapeDtypeStruct((QPK * DH + ONES, rows), jnp.bfloat16),
        ),
        m, acc,
    )
    attended = call(
        join_kernel,
        (jax.ShapeDtypeStruct((rows // 2, QPK * DH), jnp.bfloat16),) * 2,
        own, own_log, ctx_permute(send, swap),
    )

    far = [head_permute(a, 1, lambda i: i) for a in attended]

    def ring_x(halves):
        one = [head_permute(a, 0, ONE) for a in halves]
        other = [head_permute(a, 0, OTHER) for a in halves]
        return one, other, [head_permute(one[0], 0, OTHER), head_permute(other[1], 0, ONE)]

    one, other, across = ring_x(attended)
    far_one, far_other, far_across = ring_x(far)
    total = project(0, [attended, one, other], weights, None, jnp.float32)
    far_one[1], far_other[0], total = lax.optimization_barrier((far_one[1], far_other[0], total))
    total = project(3, [across, far, far_one, far_other], weights, total, jnp.float32)
    return project(7, [far_across], weights, total, jnp.bfloat16)


def solution(mesh):
    return jax.shard_map(
        per_device,
        mesh=mesh,
        in_specs=(P("ctx", "head"), P("ctx", "head"), P("ctx", "head"), P(None, "head")),
        out_specs=P("ctx", "head"),
        check_vma=False,
    )
```

```python
import math

import jax
import jax.numpy as jnp
from jax import lax
from jax.experimental import pallas as pl
from jax.experimental.pallas import tpu as pltpu
from jax.sharding import PartitionSpec as P

DH = 128
QPK = 4
SCALE2 = math.log2(math.e) * DH ** (-0.5)
NEG = -1e30

NZ, NY, NC = 4, 4, 2
NH, NX = 2, 4

TILE = 256
BESIDE = 4
PIECE = 512
ONES = 16
ROOM = 100.0


def ctx_id(z, y, c):
    return (z * NY + y) * NC + c


def ctx_permute(x, target):
    pairs = []
    for z in range(NZ):
        for y in range(NY):
            for c in range(NC):
                to = target(z, y, c)
                if to is not None:
                    pairs.append((ctx_id(z, y, c), ctx_id(*to)))
    return lax.ppermute(x, "ctx", pairs)


def head_permute(x, dz, partner):
    pairs = [(h * NX + i, (h + dz) % NH * NX + partner(i)) for h in range(NH) for i in range(NX)]
    return lax.ppermute(x, "head", pairs)


ONE = lambda i: i ^ 1
OTHER = lambda i: 3 - i
ACROSS = lambda i: (i + 2) % 4


def load_kv(blocks, keys, values):
    at = 0
    for block in blocks:
        for i in range(0, block.shape[0], DH):
            keys[at : at + DH, :] = block[i : i + DH, :DH]
            values[:DH, at : at + DH] = block[i : i + DH, DH:]
            at += DH
    values[DH:, :at] = jnp.ones((ONES, at), jnp.bfloat16)
    return at


def sweep(slots, length, scores, *ways):
    per = length // TILE

    def turn(i, _):
        def place(u):
            j = i * BESIDE + u
            return slots[0] + j // per, pl.multiple_of(j % per * TILE, TILE)

        def go(rest):
            s = scores(*place(0))
            for u in range(BESIDE):
                after = scores(*place(u + 1)) if u + 1 < BESIDE else None
                rest(*place(u), s)
                s = after

        for way in ways:
            if isinstance(way, tuple):
                pl.when(way[0](place(0)[0]))(lambda rest=way[1]: go(rest))
            else:
                go(way)
        return 0

    lax.fori_loop(0, (slots[1] - slots[0]) * per // BESIDE, turn, 0)


def scores_of(q, keys, count, piece=PIECE):
    def scores(slot, r):
        rows = q[slot, :, pl.ds(r, TILE)]
        return [
            jnp.dot(keys[k : k + piece, :], rows, preferred_element_type=jnp.float32) * SCALE2
            for k in range(0, count, piece)
        ]

    return scores


def weigh(values, s, m, kept=None):
    total = None
    for k, one in enumerate(s):
        n = one.shape[0]
        p = jnp.exp2(one - m[:1]).astype(jnp.bfloat16)
        o = jnp.dot(values[:, k * n : (k + 1) * n], p, preferred_element_type=jnp.float32)
        if kept is not None:
            o = jnp.where(kept[k], o, 0.0)
        total = o if total is None else total + o
    return total


def update(q, keys, values, count, m_in, acc_in, m_out, acc_out, kept):
    scores = scores_of(q, keys, count, count // len(kept))
    squares = jnp.dot(
        keys[:count, :] * keys[:count, :], jnp.ones((DH, DH), jnp.bfloat16), preferred_element_type=jnp.float32
    )
    longest = jnp.sqrt(jnp.max(squares, axis=0, keepdims=True))[:, :1] * (1.02 * SCALE2)
    near = []
    for t in range(2):
        over = None
        for slot in range(t * QPK, (t + 1) * QPK):
            reach = m_in[slot, 1:2, :] * longest - m_in[slot, :1, :]
            over = reach if over is None else jnp.maximum(over, reach)
        near.append(jnp.max(over) < ROOM)
    near_at = lambda slot: jnp.where(slot < QPK, near[0], near[1])

    def stay(slot, r, s):
        rows = pl.ds(r, TILE)
        m = m_in[slot, :, rows]
        m_out[slot, :, rows] = m
        acc_out[slot, :, rows] = acc_in[slot, :, rows] + weigh(values, s, m, kept)

    def move(slot, r, s):
        rows = pl.ds(r, TILE)
        m_old = m_in[slot, :, rows]
        m = m_old[:1]
        for one, keep in zip(s, kept):
            m = jnp.maximum(m, jnp.where(keep, jnp.max(one, axis=0, keepdims=True), NEG))
        shrink = jnp.exp2(m_old[:1] - m)
        m_out[slot, :, rows] = jnp.concatenate([m, m_old[1:]], axis=0)
        acc_out[slot, :, rows] = acc_in[slot, :, rows] * shrink + weigh(values, s, m, kept)

    sweep(
        (0, 2 * QPK), q.shape[2], scores, (near_at, stay), (lambda slot: jnp.logical_not(near_at(slot)), move)
    )


def own_kernel(info, q, own, m_out, acc_out, keys, values):
    n = own.shape[0]
    count = load_kv((own,), keys, values)
    plain = scores_of(q, keys, count)

    def masked(slot, r):
        s = plain(slot, r)
        i = r + lax.broadcasted_iota(jnp.int32, (PIECE, TILE), 1)
        j = lax.broadcasted_iota(jnp.int32, (PIECE, TILE), 0)
        return [jnp.where(j + k * PIECE <= i, one, NEG) for k, one in enumerate(s)]

    def rest(slot, r, s):
        rows = pl.ds(r, TILE)
        m = jnp.max(s[0], axis=0, keepdims=True)
        for one in s[1:]:
            m = jnp.maximum(m, jnp.max(one, axis=0, keepdims=True))
        m_out[slot, :1, rows] = m
        acc_out[slot, :, rows] = weigh(values, s, m)

    sweep((0, QPK), n, masked, rest)

    @pl.when(info[0] == 0)
    def _():
        sweep((QPK, 2 * QPK), n, plain, rest)

    @pl.when(info[0] != 0)
    def _():
        m_out[QPK:, :1, :] = jnp.full((QPK, 1, n), NEG, jnp.float32)
        acc_out[QPK:] = jnp.zeros((QPK, DH + ONES, n), jnp.float32)

    for slot in range(2 * QPK):
        rows = q[slot].astype(jnp.float32)
        length = jnp.sqrt(jnp.sum(rows * rows, axis=0, keepdims=True))
        m_out[slot, 1:, :] = jnp.broadcast_to(length, (7, n))


def add_kernel(flags, q, *refs):
    blocks, (m_in, acc_in, m_out, acc_out, keys, values) = refs[:-6], refs[-6:]

    @pl.when(flags[0] == 0)
    def _():
        m_out[...] = m_in[...]
        acc_out[...] = acc_in[...]

    @pl.when(flags[0] != 0)
    def _():
        count = load_kv(blocks, keys, values)
        kept = [flags[1 + k] != 0 for k in range(flags.shape[0] - 1)]
        update(q, keys, values, count, m_in, acc_in, m_out, acc_out, kept)


def share_kernel(m, acc, own_out, own_log, send):
    rows = own_out.shape[1]
    parts = []
    for slot in range(2 * QPK):
        t, h = slot // QPK, slot % QPK
        total = acc[slot, DH : DH + 1, :]
        some = total > 0.0
        total = jnp.where(some, total, 1.0)
        o = acc[slot, :DH, :] / total
        log_total = jnp.where(some, m[slot, :1, :] + jnp.log2(total), NEG)
        columns = slice(h * DH, (h + 1) * DH)
        if t == 0:
            own_out[columns, :] = o
            own_log[h : h + 1, :] = log_total
        else:
            send[columns, :] = o.astype(jnp.bfloat16)
            for _ in range(3):
                parts.append(log_total.astype(jnp.bfloat16).astype(jnp.float32))
                log_total = log_total - parts[-1]
    parts += [jnp.zeros((1, rows), jnp.float32)] * (ONES - len(parts))
    send[QPK * DH :, :] = jnp.concatenate(parts, axis=0).astype(jnp.bfloat16)


def join_kernel(own_in, own_log, got, top_out, low_out):
    theirs = got[QPK * DH :, :].astype(jnp.float32)
    for h in range(QPK):
        a = own_log[h : h + 1, :]
        b = theirs[3 * h : 3 * h + 1, :] + theirs[3 * h + 1 : 3 * h + 2, :] + theirs[3 * h + 2 : 3 * h + 3, :]
        top = jnp.maximum(a, b)
        a, b = jnp.exp2(a - top), jnp.exp2(b - top)
        share = 1.0 / (a + b)
        columns = slice(h * DH, (h + 1) * DH)
        o = own_in[columns, :] * (a * share) + got[columns, :].astype(jnp.float32) * (b * share)
        o = o.T.astype(jnp.bfloat16)
        half = top_out.shape[0]
        top_out[:, columns] = o[:half]
        low_out[:, columns] = o[half:]


VM = pl.BlockSpec(memory_space=pltpu.VMEM)
SM = pl.BlockSpec(memory_space=pltpu.SMEM)


def call(kernel, out_shape, *args, info=None, flops=0, scratch=()):
    size = sum(a.size * a.dtype.itemsize for a in args)
    many = isinstance(out_shape, tuple)
    first = [] if info is None else [info]
    return pl.pallas_call(
        kernel,
        out_shape=out_shape,
        in_specs=[SM] * len(first) + [VM] * len(args),
        out_specs=tuple(VM for _ in out_shape) if many else VM,
        scratch_shapes=scratch,
        cost_estimate=pl.CostEstimate(flops=flops, bytes_accessed=size, transcendentals=0),
        compiler_params=pltpu.CompilerParams(vmem_limit_bytes=22 * 2**20),
    )(*first, *args)


def arrange(order, out_weight, depth):
    count = out_weight.shape[0] // depth

    def kernel(order_ref, w_ref, out, sems):
        copies = []
        for k in range(count):
            start = pl.multiple_of(order_ref[k] * depth, depth)
            copies.append(
                pltpu.make_async_copy(
                    w_ref.at[pl.ds(start, depth), :], out.at[pl.ds(k * depth, depth), :], sems.at[k]
                )
            )
            copies[-1].start()
        for copy in copies:
            copy.wait()

    return pl.pallas_call(
        kernel,
        out_shape=jax.ShapeDtypeStruct(out_weight.shape, out_weight.dtype),
        in_specs=[SM, pl.BlockSpec(memory_space=pltpu.HBM)],
        out_specs=VM,
        scratch_shapes=[pltpu.SemaphoreType.DMA((count,))],
        compiler_params=pltpu.CompilerParams(vmem_limit_bytes=22 * 2**20),
    )(order, out_weight)


def project(first, pieces, weights, so_far, out_type):
    refs = [block for piece in pieces for block in piece]
    counts = [len(piece) for piece in pieces]
    rows, depth = sum(b.shape[0] for b in pieces[0]), pieces[0][0].shape[1]
    columns = weights.shape[1]

    def kernel(*args):
        parts, w_ref = args[: len(refs)], args[len(refs)]
        before = args[len(refs) + 1] if so_far is not None else None
        out, total = args[-2:]
        at_ref = 0
        for k, count in enumerate(counts):
            start = 0
            for block in parts[at_ref : at_ref + count]:
                at = slice(start, start + block.shape[0])
                start += block.shape[0]
                w = w_ref[(first + k) * depth : (first + k + 1) * depth, :]
                o = jnp.dot(block[...], w, preferred_element_type=jnp.float32)
                if k > 0:
                    o = total[at, :] + o
                elif before is not None:
                    o = before[at, :] + o
                if k == len(counts) - 1:
                    out[at, :] = o.astype(out_type)
                else:
                    total[at, :] = o
            at_ref += count

    inputs = refs + [weights] + ([so_far] if so_far is not None else [])
    return pl.pallas_call(
        kernel,
        out_shape=jax.ShapeDtypeStruct((rows, columns), out_type),
        in_specs=[VM] * len(inputs),
        out_specs=VM,
        scratch_shapes=[pltpu.VMEM((rows, columns), jnp.float32)],
        cost_estimate=pl.CostEstimate(
            flops=2 * rows * depth * columns * len(pieces),
            bytes_accessed=len(pieces) * depth * (columns + rows) * 2,
            transcendentals=0,
        ),
        compiler_params=pltpu.CompilerParams(vmem_limit_bytes=22 * 2**20),
    )(*inputs)


def swap_y(x, partner, low=0):
    return ctx_permute(x, lambda z, y, c: (z, partner(y), c) if z >= low else None)


def ring_y(x, low):
    return [swap_y(x, partner, low) for partner in (ONE, OTHER, ACROSS)]


def per_device(queries, keys, values, out_weight):
    rows = queries.shape[0]
    ctx = lax.axis_index("ctx")
    head = lax.axis_index("head")
    z, y, c = ctx // (NY * NC), ctx // NC % NY, ctx % NC
    i32 = lambda *v: jnp.stack([jnp.asarray(x, jnp.int32) for x in v])
    info = i32(c, y, z)
    swap = lambda z, y, c: (z, y, 1 - c)

    squares = values.reshape(rows // DH, DH, DH).transpose(0, 2, 1).reshape(rows, DH)
    kv, queries = lax.optimization_barrier((jnp.concatenate([keys, squares], axis=1), queries))
    q_own = queries.T.reshape(QPK, DH, rows)
    q = jnp.concatenate([q_own, ctx_permute(q_own, swap)], axis=0)
    lift = lambda x, d: ctx_permute(x, lambda z, y, c: (z + d, y, c) if z + d < NZ else None)
    unit = 2 * 2 * 2 * QPK * rows * rows * DH
    state = (
        jax.ShapeDtypeStruct((2 * QPK, 8, rows), jnp.float32),
        jax.ShapeDtypeStruct((2 * QPK, DH + ONES, rows), jnp.float32),
    )

    def attend(kernel, keys, info, *args):
        return call(
            kernel,
            state,
            *args,
            info=info,
            flops=keys // rows * unit,
            scratch=[
                pltpu.VMEM((keys, DH), jnp.bfloat16),
                pltpu.VMEM((DH + ONES, keys), jnp.bfloat16),
            ],
        )

    def add(blocks, m, acc, piece=PIECE):
        kept = [keep for _, chunks in blocks for n, keep in chunks for _ in range(n // piece)]
        some = kept[0]
        for keep in kept[1:]:
            some = some | keep
        arrays = [a for a, _ in blocks]
        return attend(add_kernel, sum(a.shape[0] for a in arrays), i32(some, *kept), q, *arrays, m, acc)

    hz, hx = head // NX, head % NX
    along = (hx, hx + 1 - hx % 2 * 2, 3 - hx, (hx + 2) % NX)
    order = [h * NX + i for h in (hz, 1 - hz) for i in along]
    lower = [lift(kv, d) for d in (1, 2, 3)]
    late, q = lax.optimization_barrier((kv, q))
    one, other, across = ring_y(late, 0)
    m, acc = attend(own_kernel, rows, info, q, kv)
    m, acc = add([(one, [(rows, y % 2 == 1)]), (other, [(rows, y >= 2)])], m, acc)
    m, across, *lower = lax.optimization_barrier((m, across, *lower))
    lower = jnp.concatenate(lower, axis=0)
    chunks = [(rows, z >= d) for d in (1, 2, 3)]
    lower_one, lower_other = swap_y(lower, ONE, 1), swap_y(lower, OTHER, 1)
    m, acc = add([(lower, chunks), (across, [(rows, y >= 2)])], m, acc)
    half = lower.shape[0] // 2
    first, second = swap_y(lower_one[:half], OTHER, 1), swap_y(lower_other[half:], ONE, 1)
    m, order = lax.optimization_barrier((m, i32(*order)))
    weights = arrange(order, out_weight, QPK * DH)
    m, weights = lax.optimization_barrier((m, weights))
    m, acc = add([(lower_one, chunks), (lower_other, chunks)], m, acc)
    middle = (half - rows, z >= 2)
    m, acc = add([(first, [chunks[0], middle]), (second, [middle, chunks[2]])], m, acc, half - rows)
    own, own_log, send = call(
        share_kernel,
        (
            jax.ShapeDtypeStruct((QPK * DH, rows), jnp.float32),
            jax.ShapeDtypeStruct((8, rows), jnp.float32),
            jax.ShapeDtypeStruct((QPK * DH + ONES, rows), jnp.bfloat16),
        ),
        m, acc,
    )
    attended = call(
        join_kernel,
        (jax.ShapeDtypeStruct((rows // 2, QPK * DH), jnp.bfloat16),) * 2,
        own, own_log, ctx_permute(send, swap),
    )

    far = [head_permute(a, 1, lambda i: i) for a in attended]

    def ring_x(halves):
        one = [head_permute(a, 0, ONE) for a in halves]
        other = [head_permute(a, 0, OTHER) for a in halves]
        return one, other, [head_permute(one[0], 0, OTHER), head_permute(other[1], 0, ONE)]

    one, other, across = ring_x(attended)
    far_one, far_other, far_across = ring_x(far)
    total = project(0, [attended, one, other], weights, None, jnp.float32)
    far_one[1], far_other[0], total = lax.optimization_barrier((far_one[1], far_other[0], total))
    total = project(3, [across, far, far_one, far_other], weights, total, jnp.float32)
    return project(7, [far_across], weights, total, jnp.bfloat16)


def solution(mesh):
    return jax.shard_map(
        per_device,
        mesh=mesh,
        in_specs=(P("ctx", "head"), P("ctx", "head"), P("ctx", "head"), P(None, "head")),
        out_specs=P("ctx", "head"),
        check_vma=False,
    )
```

```python
import math

import jax
import jax.numpy as jnp
from jax import lax
from jax.experimental import pallas as pl
from jax.experimental.pallas import tpu as pltpu
from jax.sharding import PartitionSpec as P

DH = 128
QPK = 4
SCALE2 = math.log2(math.e) * DH ** (-0.5)
NEG = -1e30

NZ, NY, NC = 4, 4, 2
NH, NX = 2, 4

TILE = 512
BESIDE = 2
PIECE = 512
ONES = 16
ROOM = 100.0


def ctx_id(z, y, c):
    return (z * NY + y) * NC + c


def ctx_permute(x, target):
    pairs = []
    for z in range(NZ):
        for y in range(NY):
            for c in range(NC):
                to = target(z, y, c)
                if to is not None:
                    pairs.append((ctx_id(z, y, c), ctx_id(*to)))
    return lax.ppermute(x, "ctx", pairs)


def head_permute(x, dz, partner):
    pairs = [(h * NX + i, (h + dz) % NH * NX + partner(i)) for h in range(NH) for i in range(NX)]
    return lax.ppermute(x, "head", pairs)


ONE = lambda i: i ^ 1
OTHER = lambda i: 3 - i
ACROSS = lambda i: (i + 2) % 4


def load_kv(blocks, keys, values):
    at = 0
    for block in blocks:
        for i in range(0, block.shape[0], DH):
            keys[at : at + DH, :] = block[i : i + DH, :DH]
            values[:DH, at : at + DH] = block[i : i + DH, DH:]
            at += DH
    values[DH:, :at] = jnp.ones((ONES, at), jnp.bfloat16)
    return at


def sweep(slots, length, scores, *ways):
    per = length // TILE

    def turn(i, _):
        def place(u):
            j = i * BESIDE + u
            return slots[0] + j // per, pl.multiple_of(j % per * TILE, TILE)

        def go(rest):
            s = scores(*place(0))
            for u in range(BESIDE):
                after = scores(*place(u + 1)) if u + 1 < BESIDE else None
                rest(*place(u), s)
                s = after

        for way in ways:
            if isinstance(way, tuple):
                pl.when(way[0](place(0)[0]))(lambda rest=way[1]: go(rest))
            else:
                go(way)
        return 0

    lax.fori_loop(0, (slots[1] - slots[0]) * per // BESIDE, turn, 0)


def scores_of(q, keys, count):
    def scores(slot, r):
        rows = q[slot, :, pl.ds(r, TILE)]
        return [
            jnp.dot(keys[k : k + PIECE, :], rows, preferred_element_type=jnp.float32) * SCALE2
            for k in range(0, count, PIECE)
        ]

    return scores


def weigh(values, s, m, kept=None):
    total = None
    for k, one in enumerate(s):
        p = jnp.exp2(one - m[:1]).astype(jnp.bfloat16)
        o = jnp.dot(
            values[:, k * PIECE : (k + 1) * PIECE], p, preferred_element_type=jnp.float32
        )
        if kept is not None:
            o = jnp.where(kept[k], o, 0.0)
        total = o if total is None else total + o
    return total


def update(q, keys, values, count, m_in, acc_in, m_out, acc_out, kept=None):
    scores = scores_of(q, keys, count)
    squares = jnp.dot(
        keys[:count, :] * keys[:count, :], jnp.ones((DH, DH), jnp.bfloat16), preferred_element_type=jnp.float32
    )
    longest = jnp.sqrt(jnp.max(squares, axis=0, keepdims=True))[:, :1] * (1.02 * SCALE2)
    near = []
    for t in range(2):
        over = None
        for slot in range(t * QPK, (t + 1) * QPK):
            reach = m_in[slot, 1:2, :] * longest - m_in[slot, :1, :]
            over = reach if over is None else jnp.maximum(over, reach)
        near.append(jnp.max(over) < ROOM)
    near_at = lambda slot: jnp.where(slot < QPK, near[0], near[1])

    def stay(slot, r, s):
        rows = pl.ds(r, TILE)
        m = m_in[slot, :, rows]
        m_out[slot, :, rows] = m
        acc_out[slot, :, rows] = acc_in[slot, :, rows] + weigh(values, s, m, kept)

    def move(slot, r, s):
        rows = pl.ds(r, TILE)
        m_old = m_in[slot, :, rows]
        m = m_old[:1]
        for k, one in enumerate(s):
            top = jnp.max(one, axis=0, keepdims=True)
            m = jnp.maximum(m, top if kept is None else jnp.where(kept[k], top, NEG))
        shrink = jnp.exp2(m_old[:1] - m)
        m_out[slot, :, rows] = jnp.concatenate([m, m_old[1:]], axis=0)
        acc_out[slot, :, rows] = acc_in[slot, :, rows] * shrink + weigh(values, s, m, kept)

    sweep(
        (0, 2 * QPK), q.shape[2], scores, (near_at, stay), (lambda slot: jnp.logical_not(near_at(slot)), move)
    )


def own_kernel(info, q, own, m_out, acc_out, keys, values):
    n = own.shape[0]
    count = load_kv((own,), keys, values)
    plain = scores_of(q, keys, count)

    def masked(slot, r):
        s = plain(slot, r)
        i = r + lax.broadcasted_iota(jnp.int32, (PIECE, TILE), 1)
        j = lax.broadcasted_iota(jnp.int32, (PIECE, TILE), 0)
        return [jnp.where(j + k * PIECE <= i, one, NEG) for k, one in enumerate(s)]

    def rest(slot, r, s):
        rows = pl.ds(r, TILE)
        m = jnp.max(s[0], axis=0, keepdims=True)
        for one in s[1:]:
            m = jnp.maximum(m, jnp.max(one, axis=0, keepdims=True))
        m_out[slot, :1, rows] = m
        acc_out[slot, :, rows] = weigh(values, s, m)

    sweep((0, QPK), n, masked, rest)

    @pl.when(info[0] == 0)
    def _():
        sweep((QPK, 2 * QPK), n, plain, rest)

    @pl.when(info[0] != 0)
    def _():
        m_out[QPK:, :1, :] = jnp.full((QPK, 1, n), NEG, jnp.float32)
        acc_out[QPK:] = jnp.zeros((QPK, DH + ONES, n), jnp.float32)

    for slot in range(2 * QPK):
        rows = q[slot].astype(jnp.float32)
        length = jnp.sqrt(jnp.sum(rows * rows, axis=0, keepdims=True))
        m_out[slot, 1:, :] = jnp.broadcast_to(length, (7, n))


def row_kernel(info, q, one_ref, other_ref, across_ref, m_in, acc_in, m_out, acc_out, keys, values):
    y = info[1]
    n = one_ref.shape[0]

    @pl.when(y == 0)
    def _():
        m_out[...] = m_in[...]
        acc_out[...] = acc_in[...]

    @pl.when(y != 0)
    def _():
        count = load_kv((one_ref, other_ref, across_ref), keys, values)
        before = ((y == 1) | (y == 3), y >= 2, y >= 2)
        kept = [before[k * PIECE // n] for k in range(count // PIECE)]
        update(q, keys, values, count, m_in, acc_in, m_out, acc_out, kept)


def plane_kernel(least, parts, info, q, *refs):
    blocks, (m_in, acc_in, m_out, acc_out, keys, values) = refs[:-6], refs[-6:]
    z = info[2]

    @pl.when(z < least)
    def _():
        m_out[...] = m_in[...]
        acc_out[...] = acc_in[...]

    @pl.when(z >= least)
    def _():
        used = [b.at[start : start + n] for b, (start, n) in zip(blocks, parts)]
        count = load_kv(used, keys, values)
        update(q, keys, values, count, m_in, acc_in, m_out, acc_out)


def share_kernel(m, acc, own_out, own_log, send):
    rows = own_out.shape[1]
    parts = []
    for slot in range(2 * QPK):
        t, h = slot // QPK, slot % QPK
        total = acc[slot, DH : DH + 1, :]
        some = total > 0.0
        total = jnp.where(some, total, 1.0)
        o = acc[slot, :DH, :] / total
        log_total = jnp.where(some, m[slot, :1, :] + jnp.log2(total), NEG)
        columns = slice(h * DH, (h + 1) * DH)
        if t == 0:
            own_out[columns, :] = o
            own_log[h : h + 1, :] = log_total
        else:
            send[columns, :] = o.astype(jnp.bfloat16)
            for _ in range(3):
                parts.append(log_total.astype(jnp.bfloat16).astype(jnp.float32))
                log_total = log_total - parts[-1]
    parts += [jnp.zeros((1, rows), jnp.float32)] * (ONES - len(parts))
    send[QPK * DH :, :] = jnp.concatenate(parts, axis=0).astype(jnp.bfloat16)


def join_kernel(own_in, own_log, got, top_out, low_out):
    theirs = got[QPK * DH :, :].astype(jnp.float32)
    for h in range(QPK):
        a = own_log[h : h + 1, :]
        b = theirs[3 * h : 3 * h + 1, :] + theirs[3 * h + 1 : 3 * h + 2, :] + theirs[3 * h + 2 : 3 * h + 3, :]
        top = jnp.maximum(a, b)
        a, b = jnp.exp2(a - top), jnp.exp2(b - top)
        share = 1.0 / (a + b)
        columns = slice(h * DH, (h + 1) * DH)
        o = own_in[columns, :] * (a * share) + got[columns, :].astype(jnp.float32) * (b * share)
        o = o.T.astype(jnp.bfloat16)
        half = top_out.shape[0]
        top_out[:, columns] = o[:half]
        low_out[:, columns] = o[half:]


VM = pl.BlockSpec(memory_space=pltpu.VMEM)
SM = pl.BlockSpec(memory_space=pltpu.SMEM)


def call(kernel, out_shape, *args, info=None, flops=0, scratch=()):
    size = sum(a.size * a.dtype.itemsize for a in args)
    many = isinstance(out_shape, tuple)
    first = [] if info is None else [info]
    return pl.pallas_call(
        kernel,
        out_shape=out_shape,
        in_specs=[SM] * len(first) + [VM] * len(args),
        out_specs=tuple(VM for _ in out_shape) if many else VM,
        scratch_shapes=scratch,
        cost_estimate=pl.CostEstimate(flops=flops, bytes_accessed=size, transcendentals=0),
        compiler_params=pltpu.CompilerParams(vmem_limit_bytes=22 * 2**20),
    )(*first, *args)


def arrange(order, out_weight, depth):
    count = out_weight.shape[0] // depth

    def kernel(order_ref, w_ref, out, sems):
        copies = []
        for k in range(count):
            start = pl.multiple_of(order_ref[k] * depth, depth)
            copies.append(
                pltpu.make_async_copy(
                    w_ref.at[pl.ds(start, depth), :], out.at[pl.ds(k * depth, depth), :], sems.at[k]
                )
            )
            copies[-1].start()
        for copy in copies:
            copy.wait()

    return pl.pallas_call(
        kernel,
        out_shape=jax.ShapeDtypeStruct(out_weight.shape, out_weight.dtype),
        in_specs=[SM, pl.BlockSpec(memory_space=pltpu.HBM)],
        out_specs=VM,
        scratch_shapes=[pltpu.SemaphoreType.DMA((count,))],
        compiler_params=pltpu.CompilerParams(vmem_limit_bytes=22 * 2**20),
    )(order, out_weight)


def project(first, pieces, weights, so_far, out_type):
    refs = [block for piece in pieces for block in piece]
    counts = [len(piece) for piece in pieces]
    rows, depth = sum(b.shape[0] for b in pieces[0]), pieces[0][0].shape[1]
    columns = weights.shape[1]

    def kernel(*args):
        parts, w_ref = args[: len(refs)], args[len(refs)]
        before = args[len(refs) + 1] if so_far is not None else None
        out, total = args[-2:]
        at_ref = 0
        for k, count in enumerate(counts):
            start = 0
            for block in parts[at_ref : at_ref + count]:
                at = slice(start, start + block.shape[0])
                start += block.shape[0]
                w = w_ref[(first + k) * depth : (first + k + 1) * depth, :]
                o = jnp.dot(block[...], w, preferred_element_type=jnp.float32)
                if k > 0:
                    o = total[at, :] + o
                elif before is not None:
                    o = before[at, :] + o
                if k == len(counts) - 1:
                    out[at, :] = o.astype(out_type)
                else:
                    total[at, :] = o
            at_ref += count

    inputs = refs + [weights] + ([so_far] if so_far is not None else [])
    return pl.pallas_call(
        kernel,
        out_shape=jax.ShapeDtypeStruct((rows, columns), out_type),
        in_specs=[VM] * len(inputs),
        out_specs=VM,
        scratch_shapes=[pltpu.VMEM((rows, columns), jnp.float32)],
        cost_estimate=pl.CostEstimate(
            flops=2 * rows * depth * columns * len(pieces),
            bytes_accessed=len(pieces) * depth * (columns + rows) * 2,
            transcendentals=0,
        ),
        compiler_params=pltpu.CompilerParams(vmem_limit_bytes=22 * 2**20),
    )(*inputs)


def swap_y(x, partner, low=0):
    return ctx_permute(x, lambda z, y, c: (z, partner(y), c) if z >= low else None)


def ring_y(x, low):
    return [swap_y(x, partner, low) for partner in (ONE, OTHER, ACROSS)]


def per_device(queries, keys, values, out_weight):
    rows = queries.shape[0]
    ctx = lax.axis_index("ctx")
    head = lax.axis_index("head")
    z, y, c = ctx // (NY * NC), ctx // NC % NY, ctx % NC
    i32 = lambda *v: jnp.stack([jnp.asarray(x, jnp.int32) for x in v])
    info = i32(c, y, z)
    swap = lambda z, y, c: (z, y, 1 - c)

    squares = values.reshape(rows // DH, DH, DH).transpose(0, 2, 1).reshape(rows, DH)
    kv, queries = lax.optimization_barrier((jnp.concatenate([keys, squares], axis=1), queries))
    q_own = queries.T.reshape(QPK, DH, rows)
    q = jnp.concatenate([q_own, ctx_permute(q_own, swap)], axis=0)
    lift = lambda x, d: ctx_permute(x, lambda z, y, c: (z + d, y, c) if z + d < NZ else None)
    unit = 2 * 2 * 2 * QPK * rows * rows * DH
    state = (
        jax.ShapeDtypeStruct((2 * QPK, 8, rows), jnp.float32),
        jax.ShapeDtypeStruct((2 * QPK, DH + ONES, rows), jnp.float32),
    )

    def attend(kernel, chunks, *args):
        return call(
            kernel,
            state,
            *args,
            info=info,
            flops=chunks * unit,
            scratch=[
                pltpu.VMEM((chunks * rows, DH), jnp.bfloat16),
                pltpu.VMEM((DH + ONES, chunks * rows), jnp.bfloat16),
            ],
        )

    def planes(least, blocks, starts, m, acc):
        parts = [(start, rows) for start in starts]
        return attend(lambda *refs: plane_kernel(least, parts, *refs), len(parts), q, *blocks, m, acc)

    hz, hx = head // NX, head % NX
    along = (hx, hx + 1 - hx % 2 * 2, 3 - hx, (hx + 2) % NX)
    order = [h * NX + i for h in (hz, 1 - hz) for i in along]
    below = lift(kv, 1)
    row = ring_y(kv, 0)
    m, acc = attend(own_kernel, 1, q, kv)
    lower = [lift(below, 1), lift(below, 2)]
    near, m, *row[:2] = lax.optimization_barrier((below, m, *row[:2]))
    near = [near, *ring_y(near, 1)]
    m, acc = attend(row_kernel, 3, q, *row, m, acc)
    m, *lower = lax.optimization_barrier((m, *lower))
    both = jnp.concatenate(lower, axis=0)
    one, other, across = ring_y(both, 2)
    near[0], both = lax.optimization_barrier((near[0], both))
    m, acc = planes(1, near, [0] * 4, m, acc)
    m, acc = planes(2, [both], [0], m, acc)
    m, acc = planes(3, [both], [rows], m, acc)
    m, order = lax.optimization_barrier((m, i32(*order)))
    weights = arrange(order, out_weight, QPK * DH)
    m, weights = lax.optimization_barrier((m, weights))
    m, acc = planes(2, [one, other, across], [0] * 3, m, acc)
    m, acc = planes(3, [one, other, across], [rows] * 3, m, acc)
    own, own_log, send = call(
        share_kernel,
        (
            jax.ShapeDtypeStruct((QPK * DH, rows), jnp.float32),
            jax.ShapeDtypeStruct((8, rows), jnp.float32),
            jax.ShapeDtypeStruct((QPK * DH + ONES, rows), jnp.bfloat16),
        ),
        m, acc,
    )
    attended = call(
        join_kernel,
        (jax.ShapeDtypeStruct((rows // 2, QPK * DH), jnp.bfloat16),) * 2,
        own, own_log, ctx_permute(send, swap),
    )

    far = [head_permute(a, 1, lambda i: i) for a in attended]

    def ring_x(halves):
        one = [head_permute(a, 0, ONE) for a in halves]
        other = [head_permute(a, 0, OTHER) for a in halves]
        return one, other, [head_permute(one[0], 0, OTHER), head_permute(other[1], 0, ONE)]

    one, other, across = ring_x(attended)
    far_one, far_other, far_across = ring_x(far)
    total = project(0, [attended, one, other], weights, None, jnp.float32)
    far_one[1], far_other[0], total = lax.optimization_barrier((far_one[1], far_other[0], total))
    total = project(3, [across, far, far_one, far_other], weights, total, jnp.float32)
    return project(7, [far_across], weights, total, jnp.bfloat16)


def solution(mesh):
    return jax.shard_map(
        per_device,
        mesh=mesh,
        in_specs=(P("ctx", "head"), P("ctx", "head"), P("ctx", "head"), P(None, "head")),
        out_specs=P("ctx", "head"),
        check_vma=False,
    )
```

```python
import math

import jax
import jax.numpy as jnp
from jax import lax
from jax.experimental import pallas as pl
from jax.experimental.pallas import tpu as pltpu
from jax.sharding import PartitionSpec as P

DH = 128
QPK = 4
SCALE2 = math.log2(math.e) * DH ** (-0.5)
NEG = -1e30

NZ, NY, NC = 4, 4, 2
NH, NX = 2, 4

TILE = 512
BESIDE = 2
PIECE = 512
ONES = 16
LARGE = 1e37


def ctx_id(z, y, c):
    return (z * NY + y) * NC + c


def ctx_permute(x, target):
    pairs = []
    for z in range(NZ):
        for y in range(NY):
            for c in range(NC):
                to = target(z, y, c)
                if to is not None:
                    pairs.append((ctx_id(z, y, c), ctx_id(*to)))
    return lax.ppermute(x, "ctx", pairs)


def head_permute(x, dz, partner):
    pairs = [(h * NX + i, (h + dz) % NH * NX + partner(i)) for h in range(NH) for i in range(NX)]
    return lax.ppermute(x, "head", pairs)


ONE = lambda i: i ^ 1
OTHER = lambda i: 3 - i
ACROSS = lambda i: (i + 2) % 4


def load_kv(blocks, keys, values):
    at = 0
    for block in blocks:
        for i in range(0, block.shape[0], DH):
            keys[at : at + DH, :] = block[i : i + DH, :DH]
            values[:DH, at : at + DH] = block[i : i + DH, DH:]
            at += DH
    values[DH:, :at] = jnp.ones((ONES, at), jnp.bfloat16)
    return at


def sweep(slots, length, scores, rest):
    per = length // TILE

    def turn(i, _):
        def place(u):
            j = i * BESIDE + u
            return j // per, pl.multiple_of(j % per * TILE, TILE)

        s = scores(*place(0))
        for u in range(BESIDE):
            after = scores(*place(u + 1)) if u + 1 < BESIDE else None
            rest(*place(u), s)
            s = after
        return 0

    lax.fori_loop(slots[0] * per // BESIDE, slots[1] * per // BESIDE, turn, 0)


def scores_of(q, keys, count):
    def scores(slot, r):
        rows = q[slot, :, pl.ds(r, TILE)]
        return [
            jnp.dot(keys[k : k + PIECE, :], rows, preferred_element_type=jnp.float32) * SCALE2
            for k in range(0, count, PIECE)
        ]

    return scores


def weigh(values, s, m, kept=None):
    total = None
    for k, one in enumerate(s):
        p = jnp.exp2(one - m[:1]).astype(jnp.bfloat16)
        o = jnp.dot(
            values[:, k * PIECE : (k + 1) * PIECE], p, preferred_element_type=jnp.float32
        )
        if kept is not None:
            o = jnp.where(kept[k], o, 0.0)
        total = o if total is None else total + o
    return total


def update(q, keys, values, count, m_in, acc_in, m_out, acc_out, kept=None, cold=None):
    scores = scores_of(q, keys, count)

    def stay(slot, r, s):
        rows = pl.ds(r, TILE)
        m = m_in[slot, :, rows]
        m_out[slot, :, rows] = m
        acc_out[slot, :, rows] = acc_in[slot, :, rows] + weigh(values, s, m, kept)

    def move(slot, r, s):
        rows = pl.ds(r, TILE)
        m_old = m_in[slot, :, rows]
        m = m_old
        for k, one in enumerate(s):
            top = jnp.max(one, axis=0, keepdims=True)
            m = jnp.maximum(m, top if kept is None else jnp.where(kept[k], top, NEG))
        shrink = jnp.exp2(m_old[:1] - m[:1])
        m_out[slot, :, rows] = m
        acc_out[slot, :, rows] = acc_in[slot, :, rows] * shrink + weigh(values, s, m, kept)

    warm = 2 * QPK if cold is None else jnp.where(cold, QPK, 2 * QPK)
    sweep((0, warm), q.shape[2], scores, stay)
    worst = acc_out[0, DH : DH + 1, :]
    for slot in range(1, 2 * QPK):
        total = acc_out[slot, DH : DH + 1, :]
        if cold is not None and slot >= QPK:
            total = jnp.where(cold, 0.0, total)
        worst = jnp.maximum(worst, total)
    fine = jnp.max(worst) < LARGE
    sweep((jnp.where(fine, warm, 0), 2 * QPK), q.shape[2], scores, move)


def own_kernel(info, q, own, m_out, acc_out, keys, values):
    n = own.shape[0]
    count = load_kv((own,), keys, values)
    plain = scores_of(q, keys, count)

    def masked(slot, r):
        s = plain(slot, r)
        i = r + lax.broadcasted_iota(jnp.int32, (PIECE, TILE), 1)
        j = lax.broadcasted_iota(jnp.int32, (PIECE, TILE), 0)
        return [jnp.where(j + k * PIECE <= i, one, NEG) for k, one in enumerate(s)]

    def rest(slot, r, s):
        rows = pl.ds(r, TILE)
        m = jnp.full((8, TILE), NEG, jnp.float32)
        for one in s:
            m = jnp.maximum(m, jnp.max(one, axis=0, keepdims=True))
        m_out[slot, :, rows] = m
        acc_out[slot, :, rows] = weigh(values, s, m)

    sweep((0, QPK), n, masked, rest)

    @pl.when(info[0] == 0)
    def _():
        sweep((QPK, 2 * QPK), n, plain, rest)

    @pl.when(info[0] != 0)
    def _():
        m_out[QPK:] = jnp.full((QPK, 8, n), NEG, jnp.float32)
        acc_out[QPK:] = jnp.zeros((QPK, DH + ONES, n), jnp.float32)


def row_kernel(info, q, one_ref, other_ref, across_ref, m_in, acc_in, m_out, acc_out, keys, values):
    y = info[1]
    n = one_ref.shape[0]

    @pl.when(y == 0)
    def _():
        m_out[...] = m_in[...]
        acc_out[...] = acc_in[...]

    @pl.when(y != 0)
    def _():
        count = load_kv((one_ref, other_ref, across_ref), keys, values)
        before = ((y == 1) | (y == 3), y >= 2, y >= 2)
        kept = [before[k * PIECE // n] for k in range(count // PIECE)]
        update(q, keys, values, count, m_in, acc_in, m_out, acc_out, kept, info[0] == 1)


def plane_kernel(least, parts, info, q, *refs):
    blocks, (m_in, acc_in, m_out, acc_out, keys, values) = refs[:-6], refs[-6:]
    z = info[2]

    @pl.when(z < least)
    def _():
        m_out[...] = m_in[...]
        acc_out[...] = acc_in[...]

    @pl.when(z >= least)
    def _():
        used = [b.at[start : start + n] for b, (start, n) in zip(blocks, parts)]
        count = load_kv(used, keys, values)
        cold = (info[0] == 1) & (info[1] == 0) if least == 1 else None
        update(q, keys, values, count, m_in, acc_in, m_out, acc_out, None, cold)


def share_kernel(m, acc, own_out, own_log, send):
    rows = own_out.shape[1]
    parts = []
    for slot in range(2 * QPK):
        t, h = slot // QPK, slot % QPK
        total = acc[slot, DH : DH + 1, :]
        some = total > 0.0
        total = jnp.where(some, total, 1.0)
        o = acc[slot, :DH, :] / total
        log_total = jnp.where(some, m[slot, :1, :] + jnp.log2(total), NEG)
        columns = slice(h * DH, (h + 1) * DH)
        if t == 0:
            own_out[columns, :] = o
            own_log[h : h + 1, :] = log_total
        else:
            send[columns, :] = o.astype(jnp.bfloat16)
            for _ in range(3):
                parts.append(log_total.astype(jnp.bfloat16).astype(jnp.float32))
                log_total = log_total - parts[-1]
    parts += [jnp.zeros((1, rows), jnp.float32)] * (ONES - len(parts))
    send[QPK * DH :, :] = jnp.concatenate(parts, axis=0).astype(jnp.bfloat16)


def join_kernel(own_in, own_log, got, top_out, low_out):
    theirs = got[QPK * DH :, :].astype(jnp.float32)
    for h in range(QPK):
        a = own_log[h : h + 1, :]
        b = theirs[3 * h : 3 * h + 1, :] + theirs[3 * h + 1 : 3 * h + 2, :] + theirs[3 * h + 2 : 3 * h + 3, :]
        top = jnp.maximum(a, b)
        a, b = jnp.exp2(a - top), jnp.exp2(b - top)
        share = 1.0 / (a + b)
        columns = slice(h * DH, (h + 1) * DH)
        o = own_in[columns, :] * (a * share) + got[columns, :].astype(jnp.float32) * (b * share)
        o = o.T.astype(jnp.bfloat16)
        half = top_out.shape[0]
        top_out[:, columns] = o[:half]
        low_out[:, columns] = o[half:]


VM = pl.BlockSpec(memory_space=pltpu.VMEM)
SM = pl.BlockSpec(memory_space=pltpu.SMEM)


def call(kernel, out_shape, *args, info=None, flops=0, scratch=()):
    size = sum(a.size * a.dtype.itemsize for a in args)
    many = isinstance(out_shape, tuple)
    first = [] if info is None else [info]
    return pl.pallas_call(
        kernel,
        out_shape=out_shape,
        in_specs=[SM] * len(first) + [VM] * len(args),
        out_specs=tuple(VM for _ in out_shape) if many else VM,
        scratch_shapes=scratch,
        cost_estimate=pl.CostEstimate(flops=flops, bytes_accessed=size, transcendentals=0),
        compiler_params=pltpu.CompilerParams(vmem_limit_bytes=22 * 2**20),
    )(*first, *args)


def arrange(order, out_weight, depth):
    count = out_weight.shape[0] // depth

    def kernel(order_ref, w_ref, out, sems):
        copies = []
        for k in range(count):
            start = pl.multiple_of(order_ref[k] * depth, depth)
            copies.append(
                pltpu.make_async_copy(
                    w_ref.at[pl.ds(start, depth), :], out.at[pl.ds(k * depth, depth), :], sems.at[k]
                )
            )
            copies[-1].start()
        for copy in copies:
            copy.wait()

    return pl.pallas_call(
        kernel,
        out_shape=jax.ShapeDtypeStruct(out_weight.shape, out_weight.dtype),
        in_specs=[SM, pl.BlockSpec(memory_space=pltpu.HBM)],
        out_specs=VM,
        scratch_shapes=[pltpu.SemaphoreType.DMA((count,))],
        compiler_params=pltpu.CompilerParams(vmem_limit_bytes=22 * 2**20),
    )(order, out_weight)


def project(first, pieces, weights, so_far, out_type):
    refs = [block for piece in pieces for block in piece]
    counts = [len(piece) for piece in pieces]
    rows, depth = sum(b.shape[0] for b in pieces[0]), pieces[0][0].shape[1]
    columns = weights.shape[1]

    def kernel(*args):
        parts, w_ref = args[: len(refs)], args[len(refs)]
        before = args[len(refs) + 1] if so_far is not None else None
        out, total = args[-2:]
        at_ref = 0
        for k, count in enumerate(counts):
            start = 0
            for block in parts[at_ref : at_ref + count]:
                at = slice(start, start + block.shape[0])
                start += block.shape[0]
                w = w_ref[(first + k) * depth : (first + k + 1) * depth, :]
                o = jnp.dot(block[...], w, preferred_element_type=jnp.float32)
                if k > 0:
                    o = total[at, :] + o
                elif before is not None:
                    o = before[at, :] + o
                if k == len(counts) - 1:
                    out[at, :] = o.astype(out_type)
                else:
                    total[at, :] = o
            at_ref += count

    inputs = refs + [weights] + ([so_far] if so_far is not None else [])
    return pl.pallas_call(
        kernel,
        out_shape=jax.ShapeDtypeStruct((rows, columns), out_type),
        in_specs=[VM] * len(inputs),
        out_specs=VM,
        scratch_shapes=[pltpu.VMEM((rows, columns), jnp.float32)],
        cost_estimate=pl.CostEstimate(
            flops=2 * rows * depth * columns * len(pieces),
            bytes_accessed=len(pieces) * depth * (columns + rows) * 2,
            transcendentals=0,
        ),
        compiler_params=pltpu.CompilerParams(vmem_limit_bytes=22 * 2**20),
    )(*inputs)


def swap_y(x, partner, low=0):
    return ctx_permute(x, lambda z, y, c: (z, partner(y), c) if z >= low else None)


def ring_y(x, low):
    return [swap_y(x, partner, low) for partner in (ONE, OTHER, ACROSS)]


def per_device(queries, keys, values, out_weight):
    rows = queries.shape[0]
    ctx = lax.axis_index("ctx")
    head = lax.axis_index("head")
    z, y, c = ctx // (NY * NC), ctx // NC % NY, ctx % NC
    i32 = lambda *v: jnp.stack([jnp.asarray(x, jnp.int32) for x in v])
    info = i32(c, y, z)
    swap = lambda z, y, c: (z, y, 1 - c)

    squares = values.reshape(rows // DH, DH, DH).transpose(0, 2, 1).reshape(rows, DH)
    kv, queries = lax.optimization_barrier((jnp.concatenate([keys, squares], axis=1), queries))
    q_own = queries.T.reshape(QPK, DH, rows)
    q = jnp.concatenate([q_own, ctx_permute(q_own, swap)], axis=0)
    lift = lambda x, d: ctx_permute(x, lambda z, y, c: (z + d, y, c) if z + d < NZ else None)
    unit = 2 * 2 * 2 * QPK * rows * rows * DH
    state = (
        jax.ShapeDtypeStruct((2 * QPK, 8, rows), jnp.float32),
        jax.ShapeDtypeStruct((2 * QPK, DH + ONES, rows), jnp.float32),
    )

    def attend(kernel, chunks, *args):
        return call(
            kernel,
            state,
            *args,
            info=info,
            flops=chunks * unit,
            scratch=[
                pltpu.VMEM((chunks * rows, DH), jnp.bfloat16),
                pltpu.VMEM((DH + ONES, chunks * rows), jnp.bfloat16),
            ],
        )

    def planes(least, blocks, starts, m, acc):
        parts = [(start, rows) for start in starts]
        return attend(lambda *refs: plane_kernel(least, parts, *refs), len(parts), q, *blocks, m, acc)

    hz, hx = head // NX, head % NX
    along = (hx, hx + 1 - hx % 2 * 2, 3 - hx, (hx + 2) % NX)
    order = [h * NX + i for h in (hz, 1 - hz) for i in along]
    below = lift(kv, 1)
    row = ring_y(kv, 0)
    m, acc = attend(own_kernel, 1, q, kv)
    below, m, *row[:2] = lax.optimization_barrier((below, m, *row[:2]))
    lower = [lift(below, 1), lift(below, 2)]
    below, row[2] = lax.optimization_barrier((below, row[2]))
    near = [below, *ring_y(below, 1)]
    m, acc = attend(row_kernel, 3, q, *row, m, acc)
    m, *lower = lax.optimization_barrier((m, *lower))
    both = jnp.concatenate(lower, axis=0)
    one, other, across = ring_y(both, 2)
    near[0], both = lax.optimization_barrier((near[0], both))
    m, acc = planes(1, near, [0] * 4, m, acc)
    m, acc = planes(2, [both], [0], m, acc)
    m, acc = planes(3, [both], [rows], m, acc)
    m, order = lax.optimization_barrier((m, i32(*order)))
    weights = arrange(order, out_weight, QPK * DH)
    m, weights = lax.optimization_barrier((m, weights))
    m, acc = planes(2, [one, other, across], [0] * 3, m, acc)
    m, acc = planes(3, [one, other, across], [rows] * 3, m, acc)
    own, own_log, send = call(
        share_kernel,
        (
            jax.ShapeDtypeStruct((QPK * DH, rows), jnp.float32),
            jax.ShapeDtypeStruct((8, rows), jnp.float32),
            jax.ShapeDtypeStruct((QPK * DH + ONES, rows), jnp.bfloat16),
        ),
        m, acc,
    )
    attended = call(
        join_kernel,
        (jax.ShapeDtypeStruct((rows // 2, QPK * DH), jnp.bfloat16),) * 2,
        own, own_log, ctx_permute(send, swap),
    )

    far = [head_permute(a, 1, lambda i: i) for a in attended]

    def ring_x(halves):
        one = [head_permute(a, 0, ONE) for a in halves]
        other = [head_permute(a, 0, OTHER) for a in halves]
        return one, other, [head_permute(one[0], 0, OTHER), head_permute(other[1], 0, ONE)]

    one, other, across = ring_x(attended)
    far_one, far_other, far_across = ring_x(far)
    total = project(0, [attended, one, other], weights, None, jnp.float32)
    far_one[1], far_other[0], total = lax.optimization_barrier((far_one[1], far_other[0], total))
    total = project(3, [across, far, far_one, far_other], weights, total, jnp.float32)
    return project(7, [far_across], weights, total, jnp.bfloat16)


def solution(mesh):
    return jax.shard_map(
        per_device,
        mesh=mesh,
        in_specs=(P("ctx", "head"), P("ctx", "head"), P("ctx", "head"), P(None, "head")),
        out_specs=P("ctx", "head"),
        check_vma=False,
    )
```

```python
import math

import jax
import jax.numpy as jnp
from jax import lax
from jax.experimental import pallas as pl
from jax.experimental.pallas import tpu as pltpu
from jax.sharding import PartitionSpec as P

DH = 128
QPK = 4
SCALE2 = math.log2(math.e) * DH ** (-0.5)
NEG = -1e30

NZ, NY, NC = 4, 4, 2
NH, NX = 2, 4

TILE = 512
BESIDE = 2
PIECE = 512
ONES = 16
ROOM = 100.0


def ctx_id(z, y, c):
    return (z * NY + y) * NC + c


def ctx_permute(x, target):
    pairs = []
    for z in range(NZ):
        for y in range(NY):
            for c in range(NC):
                to = target(z, y, c)
                if to is not None:
                    pairs.append((ctx_id(z, y, c), ctx_id(*to)))
    return lax.ppermute(x, "ctx", pairs)


def head_permute(x, dz, partner):
    pairs = [(h * NX + i, (h + dz) % NH * NX + partner(i)) for h in range(NH) for i in range(NX)]
    return lax.ppermute(x, "head", pairs)


ONE = lambda i: i ^ 1
OTHER = lambda i: 3 - i
ACROSS = lambda i: (i + 2) % 4


def load_kv(blocks, keys, values):
    at = 0
    for block in blocks:
        for i in range(0, block.shape[0], DH):
            keys[at : at + DH, :] = block[i : i + DH, :DH]
            values[:DH, at : at + DH] = block[i : i + DH, DH:]
            at += DH
    values[DH:, :at] = jnp.ones((ONES, at), jnp.bfloat16)
    return at


def sweep(slots, length, scores, *ways):
    per = length // TILE

    def turn(i, _):
        def place(u):
            j = i * BESIDE + u
            return slots[0] + j // per, pl.multiple_of(j % per * TILE, TILE)

        def go(rest):
            s = scores(*place(0))
            for u in range(BESIDE):
                after = scores(*place(u + 1)) if u + 1 < BESIDE else None
                rest(*place(u), s)
                s = after

        for way in ways:
            if isinstance(way, tuple):
                pl.when(way[0](place(0)[0]))(lambda rest=way[1]: go(rest))
            else:
                go(way)
        return 0

    lax.fori_loop(0, (slots[1] - slots[0]) * per // BESIDE, turn, 0)


def scores_of(q, keys, count):
    def scores(slot, r):
        rows = q[slot, :, pl.ds(r, TILE)]
        return [
            jnp.dot(keys[k : k + PIECE, :], rows, preferred_element_type=jnp.float32) * SCALE2
            for k in range(0, count, PIECE)
        ]

    return scores


def weigh(values, s, m, kept=None):
    total = None
    for k, one in enumerate(s):
        p = jnp.exp2(one - m[:1]).astype(jnp.bfloat16)
        o = jnp.dot(
            values[:, k * PIECE : (k + 1) * PIECE], p, preferred_element_type=jnp.float32
        )
        if kept is not None:
            o = jnp.where(kept[k], o, 0.0)
        total = o if total is None else total + o
    return total


def update(q, keys, values, count, m_in, acc_in, m_out, acc_out, kept=None):
    scores = scores_of(q, keys, count)
    squares = jnp.dot(
        keys[:count, :] * keys[:count, :], jnp.ones((DH, DH), jnp.bfloat16), preferred_element_type=jnp.float32
    )
    longest = jnp.sqrt(jnp.max(squares, axis=0, keepdims=True))[:, :1] * (1.02 * SCALE2)
    near = []
    for t in range(2):
        over = None
        for slot in range(t * QPK, (t + 1) * QPK):
            reach = m_in[slot, 1:2, :] * longest - m_in[slot, :1, :]
            over = reach if over is None else jnp.maximum(over, reach)
        near.append(jnp.max(over) < ROOM)
    near_at = lambda slot: jnp.where(slot < QPK, near[0], near[1])

    def stay(slot, r, s):
        rows = pl.ds(r, TILE)
        m = m_in[slot, :, rows]
        m_out[slot, :, rows] = m
        acc_out[slot, :, rows] = acc_in[slot, :, rows] + weigh(values, s, m, kept)

    def move(slot, r, s):
        rows = pl.ds(r, TILE)
        m_old = m_in[slot, :, rows]
        m = m_old[:1]
        for k, one in enumerate(s):
            top = jnp.max(one, axis=0, keepdims=True)
            m = jnp.maximum(m, top if kept is None else jnp.where(kept[k], top, NEG))
        shrink = jnp.exp2(m_old[:1] - m)
        m_out[slot, :, rows] = jnp.concatenate([m, m_old[1:]], axis=0)
        acc_out[slot, :, rows] = acc_in[slot, :, rows] * shrink + weigh(values, s, m, kept)

    sweep(
        (0, 2 * QPK), q.shape[2], scores, (near_at, stay), (lambda slot: jnp.logical_not(near_at(slot)), move)
    )


def own_kernel(info, q, own, m_out, acc_out, keys, values):
    n = own.shape[0]
    count = load_kv((own,), keys, values)
    plain = scores_of(q, keys, count)

    def masked(slot, r):
        s = plain(slot, r)
        i = r + lax.broadcasted_iota(jnp.int32, (PIECE, TILE), 1)
        j = lax.broadcasted_iota(jnp.int32, (PIECE, TILE), 0)
        return [jnp.where(j + k * PIECE <= i, one, NEG) for k, one in enumerate(s)]

    def rest(slot, r, s):
        rows = pl.ds(r, TILE)
        m = jnp.max(s[0], axis=0, keepdims=True)
        for one in s[1:]:
            m = jnp.maximum(m, jnp.max(one, axis=0, keepdims=True))
        m_out[slot, :1, rows] = m
        acc_out[slot, :, rows] = weigh(values, s, m)

    sweep((0, QPK), n, masked, rest)

    @pl.when(info[0] == 0)
    def _():
        sweep((QPK, 2 * QPK), n, plain, rest)

    @pl.when(info[0] != 0)
    def _():
        m_out[QPK:, :1, :] = jnp.full((QPK, 1, n), NEG, jnp.float32)
        acc_out[QPK:] = jnp.zeros((QPK, DH + ONES, n), jnp.float32)

    for slot in range(2 * QPK):
        rows = q[slot].astype(jnp.float32)
        length = jnp.sqrt(jnp.sum(rows * rows, axis=0, keepdims=True))
        m_out[slot, 1:, :] = jnp.broadcast_to(length, (7, n))


def row_kernel(info, q, one_ref, other_ref, m_in, acc_in, m_out, acc_out, keys, values):
    y = info[1]

    @pl.when(y == 0)
    def _():
        m_out[...] = m_in[...]
        acc_out[...] = acc_in[...]

    @pl.when(y != 0)
    def _():
        count = load_kv((one_ref, other_ref), keys, values)
        per = one_ref.shape[0] // PIECE
        kept = [(y == 1) | (y == 3)] * per + [y >= 2] * per
        update(q, keys, values, count, m_in, acc_in, m_out, acc_out, kept)


def near_kernel(info, q, *refs):
    blocks, (m_in, acc_in, m_out, acc_out, keys, values) = refs[:-6], refs[-6:]
    below, before = info[2] >= 1, info[1] >= 2

    @pl.when(jnp.logical_not(below | before))
    def _():
        m_out[...] = m_in[...]
        acc_out[...] = acc_in[...]

    @pl.when(below | before)
    def _():
        count = load_kv(blocks, keys, values)
        per = blocks[0].shape[0] // PIECE
        kept = [below] * (4 * per) + [before] * per
        update(q, keys, values, count, m_in, acc_in, m_out, acc_out, kept)


def plane_kernel(least, parts, info, q, *refs):
    blocks, (m_in, acc_in, m_out, acc_out, keys, values) = refs[:-6], refs[-6:]
    z = info[2]

    @pl.when(z < least)
    def _():
        m_out[...] = m_in[...]
        acc_out[...] = acc_in[...]

    @pl.when(z >= least)
    def _():
        used = [b.at[start : start + n] for b, (start, n) in zip(blocks, parts)]
        count = load_kv(used, keys, values)
        update(q, keys, values, count, m_in, acc_in, m_out, acc_out)


def share_kernel(m, acc, own_out, own_log, send):
    rows = own_out.shape[1]
    parts = []
    for slot in range(2 * QPK):
        t, h = slot // QPK, slot % QPK
        total = acc[slot, DH : DH + 1, :]
        some = total > 0.0
        total = jnp.where(some, total, 1.0)
        o = acc[slot, :DH, :] / total
        log_total = jnp.where(some, m[slot, :1, :] + jnp.log2(total), NEG)
        columns = slice(h * DH, (h + 1) * DH)
        if t == 0:
            own_out[columns, :] = o
            own_log[h : h + 1, :] = log_total
        else:
            send[columns, :] = o.astype(jnp.bfloat16)
            for _ in range(3):
                parts.append(log_total.astype(jnp.bfloat16).astype(jnp.float32))
                log_total = log_total - parts[-1]
    parts += [jnp.zeros((1, rows), jnp.float32)] * (ONES - len(parts))
    send[QPK * DH :, :] = jnp.concatenate(parts, axis=0).astype(jnp.bfloat16)


def join_kernel(own_in, own_log, got, top_out, low_out):
    theirs = got[QPK * DH :, :].astype(jnp.float32)
    for h in range(QPK):
        a = own_log[h : h + 1, :]
        b = theirs[3 * h : 3 * h + 1, :] + theirs[3 * h + 1 : 3 * h + 2, :] + theirs[3 * h + 2 : 3 * h + 3, :]
        top = jnp.maximum(a, b)
        a, b = jnp.exp2(a - top), jnp.exp2(b - top)
        share = 1.0 / (a + b)
        columns = slice(h * DH, (h + 1) * DH)
        o = own_in[columns, :] * (a * share) + got[columns, :].astype(jnp.float32) * (b * share)
        o = o.T.astype(jnp.bfloat16)
        half = top_out.shape[0]
        top_out[:, columns] = o[:half]
        low_out[:, columns] = o[half:]


VM = pl.BlockSpec(memory_space=pltpu.VMEM)
SM = pl.BlockSpec(memory_space=pltpu.SMEM)


def call(kernel, out_shape, *args, info=None, flops=0, scratch=()):
    size = sum(a.size * a.dtype.itemsize for a in args)
    many = isinstance(out_shape, tuple)
    first = [] if info is None else [info]
    return pl.pallas_call(
        kernel,
        out_shape=out_shape,
        in_specs=[SM] * len(first) + [VM] * len(args),
        out_specs=tuple(VM for _ in out_shape) if many else VM,
        scratch_shapes=scratch,
        cost_estimate=pl.CostEstimate(flops=flops, bytes_accessed=size, transcendentals=0),
        compiler_params=pltpu.CompilerParams(vmem_limit_bytes=22 * 2**20),
    )(*first, *args)


def arrange(order, out_weight, depth):
    count = out_weight.shape[0] // depth

    def kernel(order_ref, w_ref, out, sems):
        copies = []
        for k in range(count):
            start = pl.multiple_of(order_ref[k] * depth, depth)
            copies.append(
                pltpu.make_async_copy(
                    w_ref.at[pl.ds(start, depth), :], out.at[pl.ds(k * depth, depth), :], sems.at[k]
                )
            )
            copies[-1].start()
        for copy in copies:
            copy.wait()

    return pl.pallas_call(
        kernel,
        out_shape=jax.ShapeDtypeStruct(out_weight.shape, out_weight.dtype),
        in_specs=[SM, pl.BlockSpec(memory_space=pltpu.HBM)],
        out_specs=VM,
        scratch_shapes=[pltpu.SemaphoreType.DMA((count,))],
        compiler_params=pltpu.CompilerParams(vmem_limit_bytes=22 * 2**20),
    )(order, out_weight)


def project(first, pieces, weights, so_far, out_type):
    refs = [block for piece in pieces for block in piece]
    counts = [len(piece) for piece in pieces]
    rows, depth = sum(b.shape[0] for b in pieces[0]), pieces[0][0].shape[1]
    columns = weights.shape[1]

    def kernel(*args):
        parts, w_ref = args[: len(refs)], args[len(refs)]
        before = args[len(refs) + 1] if so_far is not None else None
        out, total = args[-2:]
        at_ref = 0
        for k, count in enumerate(counts):
            start = 0
            for block in parts[at_ref : at_ref + count]:
                at = slice(start, start + block.shape[0])
                start += block.shape[0]
                w = w_ref[(first + k) * depth : (first + k + 1) * depth, :]
                o = jnp.dot(block[...], w, preferred_element_type=jnp.float32)
                if k > 0:
                    o = total[at, :] + o
                elif before is not None:
                    o = before[at, :] + o
                if k == len(counts) - 1:
                    out[at, :] = o.astype(out_type)
                else:
                    total[at, :] = o
            at_ref += count

    inputs = refs + [weights] + ([so_far] if so_far is not None else [])
    return pl.pallas_call(
        kernel,
        out_shape=jax.ShapeDtypeStruct((rows, columns), out_type),
        in_specs=[VM] * len(inputs),
        out_specs=VM,
        scratch_shapes=[pltpu.VMEM((rows, columns), jnp.float32)],
        cost_estimate=pl.CostEstimate(
            flops=2 * rows * depth * columns * len(pieces),
            bytes_accessed=len(pieces) * depth * (columns + rows) * 2,
            transcendentals=0,
        ),
        compiler_params=pltpu.CompilerParams(vmem_limit_bytes=22 * 2**20),
    )(*inputs)


def swap_y(x, partner, low=0):
    return ctx_permute(x, lambda z, y, c: (z, partner(y), c) if z >= low else None)


def ring_y(x, low):
    return [swap_y(x, partner, low) for partner in (ONE, OTHER, ACROSS)]


def per_device(queries, keys, values, out_weight):
    rows = queries.shape[0]
    ctx = lax.axis_index("ctx")
    head = lax.axis_index("head")
    z, y, c = ctx // (NY * NC), ctx // NC % NY, ctx % NC
    i32 = lambda *v: jnp.stack([jnp.asarray(x, jnp.int32) for x in v])
    info = i32(c, y, z)
    swap = lambda z, y, c: (z, y, 1 - c)

    squares = values.reshape(rows // DH, DH, DH).transpose(0, 2, 1).reshape(rows, DH)
    kv, queries = lax.optimization_barrier((jnp.concatenate([keys, squares], axis=1), queries))
    q_own = queries.T.reshape(QPK, DH, rows)
    q = jnp.concatenate([q_own, ctx_permute(q_own, swap)], axis=0)
    lift = lambda x, d: ctx_permute(x, lambda z, y, c: (z + d, y, c) if z + d < NZ else None)
    unit = 2 * 2 * 2 * QPK * rows * rows * DH
    state = (
        jax.ShapeDtypeStruct((2 * QPK, 8, rows), jnp.float32),
        jax.ShapeDtypeStruct((2 * QPK, DH + ONES, rows), jnp.float32),
    )

    def attend(kernel, chunks, *args):
        return call(
            kernel,
            state,
            *args,
            info=info,
            flops=chunks * unit,
            scratch=[
                pltpu.VMEM((chunks * rows, DH), jnp.bfloat16),
                pltpu.VMEM((DH + ONES, chunks * rows), jnp.bfloat16),
            ],
        )

    def planes(least, blocks, starts, m, acc):
        parts = [(start, rows) for start in starts]
        return attend(lambda *refs: plane_kernel(least, parts, *refs), len(parts), q, *blocks, m, acc)

    hz, hx = head // NX, head % NX
    along = (hx, hx + 1 - hx % 2 * 2, 3 - hx, (hx + 2) % NX)
    order = [h * NX + i for h in (hz, 1 - hz) for i in along]
    below = lift(kv, 1)
    row = ring_y(kv, 0)
    m, acc = attend(own_kernel, 1, q, kv)
    below, m = lax.optimization_barrier((below, m))
    lower = [lift(below, 1), lift(below, 2)]
    m, acc = attend(row_kernel, 2, q, *row[:2], m, acc)
    near, m, row[2] = lax.optimization_barrier((below, m, row[2]))
    near = [near, *ring_y(near, 1), row[2]]
    both = jnp.concatenate(lower, axis=0)
    one, other, across = ring_y(both, 2)
    near[0], both = lax.optimization_barrier((near[0], both))
    m, acc = attend(near_kernel, 5, q, *near, m, acc)
    m, acc = planes(2, [both], [0], m, acc)
    m, acc = planes(3, [both], [rows], m, acc)
    m, order = lax.optimization_barrier((m, i32(*order)))
    weights = arrange(order, out_weight, QPK * DH)
    m, weights = lax.optimization_barrier((m, weights))
    m, acc = planes(2, [one, other, across], [0] * 3, m, acc)
    m, acc = planes(3, [one, other, across], [rows] * 3, m, acc)
    own, own_log, send = call(
        share_kernel,
        (
            jax.ShapeDtypeStruct((QPK * DH, rows), jnp.float32),
            jax.ShapeDtypeStruct((8, rows), jnp.float32),
            jax.ShapeDtypeStruct((QPK * DH + ONES, rows), jnp.bfloat16),
        ),
        m, acc,
    )
    attended = call(
        join_kernel,
        (jax.ShapeDtypeStruct((rows // 2, QPK * DH), jnp.bfloat16),) * 2,
        own, own_log, ctx_permute(send, swap),
    )

    far = [head_permute(a, 1, lambda i: i) for a in attended]

    def ring_x(halves):
        one = [head_permute(a, 0, ONE) for a in halves]
        other = [head_permute(a, 0, OTHER) for a in halves]
        return one, other, [head_permute(one[0], 0, OTHER), head_permute(other[1], 0, ONE)]

    one, other, across = ring_x(attended)
    far_one, far_other, far_across = ring_x(far)
    total = project(0, [attended, one, other], weights, None, jnp.float32)
    far_one[1], far_other[0], total = lax.optimization_barrier((far_one[1], far_other[0], total))
    total = project(3, [across, far, far_one, far_other], weights, total, jnp.float32)
    return project(7, [far_across], weights, total, jnp.bfloat16)


def solution(mesh):
    return jax.shard_map(
        per_device,
        mesh=mesh,
        in_specs=(P("ctx", "head"), P("ctx", "head"), P("ctx", "head"), P(None, "head")),
        out_specs=P("ctx", "head"),
        check_vma=False,
    )
```

```python
import math

import jax
import jax.numpy as jnp
from jax import lax
from jax.experimental import pallas as pl
from jax.experimental.pallas import tpu as pltpu
from jax.sharding import PartitionSpec as P

DH = 128
QPK = 4
SCALE2 = math.log2(math.e) * DH ** (-0.5)
NEG = -1e30

NZ, NY, NC = 4, 4, 2
NH, NX = 2, 4

TILE = 512
BESIDE = 2
PIECE = 512
ONES = 16
ROOM = 100.0


def ctx_id(z, y, c):
    return (z * NY + y) * NC + c


def ctx_permute(x, target):
    pairs = []
    for z in range(NZ):
        for y in range(NY):
            for c in range(NC):
                to = target(z, y, c)
                if to is not None:
                    pairs.append((ctx_id(z, y, c), ctx_id(*to)))
    return lax.ppermute(x, "ctx", pairs)


def head_permute(x, dz, partner):
    pairs = [(h * NX + i, (h + dz) % NH * NX + partner(i)) for h in range(NH) for i in range(NX)]
    return lax.ppermute(x, "head", pairs)


ONE = lambda i: i ^ 1
OTHER = lambda i: 3 - i
ACROSS = lambda i: (i + 2) % 4


def load_kv(blocks, keys, values):
    at = 0
    for block in blocks:
        for i in range(0, block.shape[0], DH):
            keys[at : at + DH, :] = block[i : i + DH, :DH]
            values[:DH, at : at + DH] = block[i : i + DH, DH:]
            at += DH
    values[DH:, :at] = jnp.ones((ONES, at), jnp.bfloat16)
    return at


def sweep(slots, length, scores, *ways):
    per = length // TILE

    def turn(i, _):
        def place(u):
            j = i * BESIDE + u
            return slots[0] + j // per, pl.multiple_of(j % per * TILE, TILE)

        def go(rest):
            s = scores(*place(0))
            for u in range(BESIDE):
                after = scores(*place(u + 1)) if u + 1 < BESIDE else None
                rest(*place(u), s)
                s = after

        for way in ways:
            if isinstance(way, tuple):
                pl.when(way[0](place(0)[0]))(lambda rest=way[1]: go(rest))
            else:
                go(way)
        return 0

    lax.fori_loop(0, (slots[1] - slots[0]) * per // BESIDE, turn, 0)


def scores_of(q, keys, count):
    def scores(slot, r):
        rows = q[slot, :, pl.ds(r, TILE)]
        return [
            jnp.dot(keys[k : k + PIECE, :], rows, preferred_element_type=jnp.float32) * SCALE2
            for k in range(0, count, PIECE)
        ]

    return scores


def weigh(values, s, m, kept=None):
    total = None
    for k, one in enumerate(s):
        p = jnp.exp2(one - m[:1]).astype(jnp.bfloat16)
        o = jnp.dot(
            values[:, k * PIECE : (k + 1) * PIECE], p, preferred_element_type=jnp.float32
        )
        if kept is not None:
            o = jnp.where(kept[k], o, 0.0)
        total = o if total is None else total + o
    return total


def update(q, keys, values, count, m_in, acc_in, m_out, acc_out, kept=None):
    scores = scores_of(q, keys, count)
    squares = jnp.dot(
        keys[:count, :] * keys[:count, :], jnp.ones((DH, DH), jnp.bfloat16), preferred_element_type=jnp.float32
    )
    longest = jnp.sqrt(jnp.max(squares, axis=0, keepdims=True))[:, :1] * (1.02 * SCALE2)
    near = []
    for t in range(2):
        over = None
        for slot in range(t * QPK, (t + 1) * QPK):
            reach = m_in[slot, 1:2, :] * longest - m_in[slot, :1, :]
            over = reach if over is None else jnp.maximum(over, reach)
        near.append(jnp.max(over) < ROOM)
    near_at = lambda slot: jnp.where(slot < QPK, near[0], near[1])

    def stay(slot, r, s):
        rows = pl.ds(r, TILE)
        m = m_in[slot, :, rows]
        m_out[slot, :, rows] = m
        acc_out[slot, :, rows] = acc_in[slot, :, rows] + weigh(values, s, m, kept)

    def move(slot, r, s):
        rows = pl.ds(r, TILE)
        m_old = m_in[slot, :, rows]
        m = m_old[:1]
        for k, one in enumerate(s):
            top = jnp.max(one, axis=0, keepdims=True)
            m = jnp.maximum(m, top if kept is None else jnp.where(kept[k], top, NEG))
        shrink = jnp.exp2(m_old[:1] - m)
        m_out[slot, :, rows] = jnp.concatenate([m, m_old[1:]], axis=0)
        acc_out[slot, :, rows] = acc_in[slot, :, rows] * shrink + weigh(values, s, m, kept)

    sweep(
        (0, 2 * QPK), q.shape[2], scores, (near_at, stay), (lambda slot: jnp.logical_not(near_at(slot)), move)
    )


def own_kernel(info, q, own, m_out, acc_out, keys, values):
    n = own.shape[0]
    count = load_kv((own,), keys, values)
    plain = scores_of(q, keys, count)

    def masked(slot, r):
        s = plain(slot, r)
        i = r + lax.broadcasted_iota(jnp.int32, (PIECE, TILE), 1)
        j = lax.broadcasted_iota(jnp.int32, (PIECE, TILE), 0)
        return [jnp.where(j + k * PIECE <= i, one, NEG) for k, one in enumerate(s)]

    def rest(slot, r, s):
        rows = pl.ds(r, TILE)
        m = jnp.max(s[0], axis=0, keepdims=True)
        for one in s[1:]:
            m = jnp.maximum(m, jnp.max(one, axis=0, keepdims=True))
        m_out[slot, :1, rows] = m
        acc_out[slot, :, rows] = weigh(values, s, m)

    sweep((0, QPK), n, masked, rest)

    @pl.when(info[0] == 0)
    def _():
        sweep((QPK, 2 * QPK), n, plain, rest)

    @pl.when(info[0] != 0)
    def _():
        m_out[QPK:, :1, :] = jnp.full((QPK, 1, n), NEG, jnp.float32)
        acc_out[QPK:] = jnp.zeros((QPK, DH + ONES, n), jnp.float32)

    for slot in range(2 * QPK):
        rows = q[slot].astype(jnp.float32)
        length = jnp.sqrt(jnp.sum(rows * rows, axis=0, keepdims=True))
        m_out[slot, 1:, :] = jnp.broadcast_to(length, (7, n))


def row_kernel(info, q, one_ref, other_ref, m_in, acc_in, m_out, acc_out, keys, values):
    y = info[1]

    @pl.when(y == 0)
    def _():
        m_out[...] = m_in[...]
        acc_out[...] = acc_in[...]

    @pl.when(y != 0)
    def _():
        count = load_kv((one_ref, other_ref), keys, values)
        per = one_ref.shape[0] // PIECE
        kept = [(y == 1) | (y == 3)] * per + [y >= 2] * per
        update(q, keys, values, count, m_in, acc_in, m_out, acc_out, kept)


def near_kernel(info, q, *refs):
    blocks, (m_in, acc_in, m_out, acc_out, keys, values) = refs[:-6], refs[-6:]
    below, before = info[2] >= 1, info[1] >= 2

    @pl.when(jnp.logical_not(below | before))
    def _():
        m_out[...] = m_in[...]
        acc_out[...] = acc_in[...]

    @pl.when(below | before)
    def _():
        count = load_kv(blocks, keys, values)
        per = blocks[0].shape[0] // PIECE
        kept = [below] * (4 * per) + [before] * per
        update(q, keys, values, count, m_in, acc_in, m_out, acc_out, kept)


def plane_kernel(least, parts, info, q, *refs):
    blocks, (m_in, acc_in, m_out, acc_out, keys, values) = refs[:-6], refs[-6:]
    z = info[2]

    @pl.when(z < least)
    def _():
        m_out[...] = m_in[...]
        acc_out[...] = acc_in[...]

    @pl.when(z >= least)
    def _():
        used = [b.at[start : start + n] for b, (start, n) in zip(blocks, parts)]
        count = load_kv(used, keys, values)
        update(q, keys, values, count, m_in, acc_in, m_out, acc_out)


def share_kernel(m, acc, own_out, own_log, send):
    rows = own_out.shape[1]
    parts = []
    for slot in range(2 * QPK):
        t, h = slot // QPK, slot % QPK
        total = acc[slot, DH : DH + 1, :]
        some = total > 0.0
        total = jnp.where(some, total, 1.0)
        o = acc[slot, :DH, :] / total
        log_total = jnp.where(some, m[slot, :1, :] + jnp.log2(total), NEG)
        columns = slice(h * DH, (h + 1) * DH)
        if t == 0:
            own_out[columns, :] = o
            own_log[h : h + 1, :] = log_total
        else:
            send[columns, :] = o.astype(jnp.bfloat16)
            for _ in range(3):
                parts.append(log_total.astype(jnp.bfloat16).astype(jnp.float32))
                log_total = log_total - parts[-1]
    parts += [jnp.zeros((1, rows), jnp.float32)] * (ONES - len(parts))
    send[QPK * DH :, :] = jnp.concatenate(parts, axis=0).astype(jnp.bfloat16)


def join_kernel(own_in, own_log, got, top_out, low_out):
    theirs = got[QPK * DH :, :].astype(jnp.float32)
    for h in range(QPK):
        a = own_log[h : h + 1, :]
        b = theirs[3 * h : 3 * h + 1, :] + theirs[3 * h + 1 : 3 * h + 2, :] + theirs[3 * h + 2 : 3 * h + 3, :]
        top = jnp.maximum(a, b)
        a, b = jnp.exp2(a - top), jnp.exp2(b - top)
        share = 1.0 / (a + b)
        columns = slice(h * DH, (h + 1) * DH)
        o = own_in[columns, :] * (a * share) + got[columns, :].astype(jnp.float32) * (b * share)
        o = o.T.astype(jnp.bfloat16)
        half = top_out.shape[0]
        top_out[:, columns] = o[:half]
        low_out[:, columns] = o[half:]


VM = pl.BlockSpec(memory_space=pltpu.VMEM)
SM = pl.BlockSpec(memory_space=pltpu.SMEM)


def call(kernel, out_shape, *args, info=None, flops=0, scratch=()):
    size = sum(a.size * a.dtype.itemsize for a in args)
    many = isinstance(out_shape, tuple)
    first = [] if info is None else [info]
    return pl.pallas_call(
        kernel,
        out_shape=out_shape,
        in_specs=[SM] * len(first) + [VM] * len(args),
        out_specs=tuple(VM for _ in out_shape) if many else VM,
        scratch_shapes=scratch,
        cost_estimate=pl.CostEstimate(flops=flops, bytes_accessed=size, transcendentals=0),
        compiler_params=pltpu.CompilerParams(vmem_limit_bytes=22 * 2**20),
    )(*first, *args)


def arrange(order, out_weight, depth):
    count = out_weight.shape[0] // depth

    def kernel(order_ref, w_ref, out, sems):
        copies = []
        for k in range(count):
            start = pl.multiple_of(order_ref[k] * depth, depth)
            copies.append(
                pltpu.make_async_copy(
                    w_ref.at[pl.ds(start, depth), :], out.at[pl.ds(k * depth, depth), :], sems.at[k]
                )
            )
            copies[-1].start()
        for copy in copies:
            copy.wait()

    return pl.pallas_call(
        kernel,
        out_shape=jax.ShapeDtypeStruct(out_weight.shape, out_weight.dtype),
        in_specs=[SM, pl.BlockSpec(memory_space=pltpu.HBM)],
        out_specs=VM,
        scratch_shapes=[pltpu.SemaphoreType.DMA((count,))],
        compiler_params=pltpu.CompilerParams(vmem_limit_bytes=22 * 2**20),
    )(order, out_weight)


def project(first, pieces, weights, so_far, out_type):
    refs = [block for piece in pieces for block in piece]
    counts = [len(piece) for piece in pieces]
    rows, depth = sum(b.shape[0] for b in pieces[0]), pieces[0][0].shape[1]
    columns = weights.shape[1]

    def kernel(*args):
        parts, w_ref = args[: len(refs)], args[len(refs)]
        before = args[len(refs) + 1] if so_far is not None else None
        out, total = args[-2:]
        at_ref = 0
        for k, count in enumerate(counts):
            start = 0
            for block in parts[at_ref : at_ref + count]:
                at = slice(start, start + block.shape[0])
                start += block.shape[0]
                w = w_ref[(first + k) * depth : (first + k + 1) * depth, :]
                o = jnp.dot(block[...], w, preferred_element_type=jnp.float32)
                if k > 0:
                    o = total[at, :] + o
                elif before is not None:
                    o = before[at, :] + o
                if k == len(counts) - 1:
                    out[at, :] = o.astype(out_type)
                else:
                    total[at, :] = o
            at_ref += count

    inputs = refs + [weights] + ([so_far] if so_far is not None else [])
    return pl.pallas_call(
        kernel,
        out_shape=jax.ShapeDtypeStruct((rows, columns), out_type),
        in_specs=[VM] * len(inputs),
        out_specs=VM,
        scratch_shapes=[pltpu.VMEM((rows, columns), jnp.float32)],
        cost_estimate=pl.CostEstimate(
            flops=2 * rows * depth * columns * len(pieces),
            bytes_accessed=len(pieces) * depth * (columns + rows) * 2,
            transcendentals=0,
        ),
        compiler_params=pltpu.CompilerParams(vmem_limit_bytes=22 * 2**20),
    )(*inputs)


def swap_y(x, partner, low=0):
    return ctx_permute(x, lambda z, y, c: (z, partner(y), c) if z >= low else None)


def ring_y(x, low):
    return [swap_y(x, partner, low) for partner in (ONE, OTHER, ACROSS)]


def per_device(queries, keys, values, out_weight):
    rows = queries.shape[0]
    ctx = lax.axis_index("ctx")
    head = lax.axis_index("head")
    z, y, c = ctx // (NY * NC), ctx // NC % NY, ctx % NC
    i32 = lambda *v: jnp.stack([jnp.asarray(x, jnp.int32) for x in v])
    info = i32(c, y, z)
    swap = lambda z, y, c: (z, y, 1 - c)

    squares = values.reshape(rows // DH, DH, DH).transpose(0, 2, 1).reshape(rows, DH)
    kv, queries = lax.optimization_barrier((jnp.concatenate([keys, squares], axis=1), queries))
    q_own = queries.T.reshape(QPK, DH, rows)
    q = jnp.concatenate([q_own, ctx_permute(q_own, swap)], axis=0)
    lift = lambda x, d: ctx_permute(x, lambda z, y, c: (z + d, y, c) if z + d < NZ else None)
    unit = 2 * 2 * 2 * QPK * rows * rows * DH
    state = (
        jax.ShapeDtypeStruct((2 * QPK, 8, rows), jnp.float32),
        jax.ShapeDtypeStruct((2 * QPK, DH + ONES, rows), jnp.float32),
    )

    def attend(kernel, chunks, *args):
        return call(
            kernel,
            state,
            *args,
            info=info,
            flops=chunks * unit,
            scratch=[
                pltpu.VMEM((chunks * rows, DH), jnp.bfloat16),
                pltpu.VMEM((DH + ONES, chunks * rows), jnp.bfloat16),
            ],
        )

    def planes(least, blocks, starts, m, acc):
        parts = [(start, rows) for start in starts]
        return attend(lambda *refs: plane_kernel(least, parts, *refs), len(parts), q, *blocks, m, acc)

    hz, hx = head // NX, head % NX
    along = (hx, hx + 1 - hx % 2 * 2, 3 - hx, (hx + 2) % NX)
    order = [h * NX + i for h in (hz, 1 - hz) for i in along]
    below = lift(kv, 1)
    late, q = lax.optimization_barrier((kv, q))
    row = ring_y(late, 0)
    m, acc = attend(own_kernel, 1, q, kv)
    below, m = lax.optimization_barrier((below, m))
    lower = [lift(below, 1), lift(below, 2)]
    m, acc = attend(row_kernel, 2, q, *row[:2], m, acc)
    near, m, row[2] = lax.optimization_barrier((below, m, row[2]))
    near = [near, *ring_y(near, 1), row[2]]
    both = jnp.concatenate(lower, axis=0)
    one, other, across = ring_y(both, 2)
    near[0], both = lax.optimization_barrier((near[0], both))
    m, acc = attend(near_kernel, 5, q, *near, m, acc)
    m, acc = planes(2, [both], [0], m, acc)
    m, acc = planes(3, [both], [rows], m, acc)
    m, order = lax.optimization_barrier((m, i32(*order)))
    weights = arrange(order, out_weight, QPK * DH)
    m, weights = lax.optimization_barrier((m, weights))
    m, acc = planes(2, [one, other, across], [0] * 3, m, acc)
    m, acc = planes(3, [one, other, across], [rows] * 3, m, acc)
    own, own_log, send = call(
        share_kernel,
        (
            jax.ShapeDtypeStruct((QPK * DH, rows), jnp.float32),
            jax.ShapeDtypeStruct((8, rows), jnp.float32),
            jax.ShapeDtypeStruct((QPK * DH + ONES, rows), jnp.bfloat16),
        ),
        m, acc,
    )
    attended = call(
        join_kernel,
        (jax.ShapeDtypeStruct((rows // 2, QPK * DH), jnp.bfloat16),) * 2,
        own, own_log, ctx_permute(send, swap),
    )

    far = [head_permute(a, 1, lambda i: i) for a in attended]

    def ring_x(halves):
        one = [head_permute(a, 0, ONE) for a in halves]
        other = [head_permute(a, 0, OTHER) for a in halves]
        return one, other, [head_permute(one[0], 0, OTHER), head_permute(other[1], 0, ONE)]

    one, other, across = ring_x(attended)
    far_one, far_other, far_across = ring_x(far)
    total = project(0, [attended, one, other], weights, None, jnp.float32)
    far_one[1], far_other[0], total = lax.optimization_barrier((far_one[1], far_other[0], total))
    total = project(3, [across, far, far_one, far_other], weights, total, jnp.float32)
    return project(7, [far_across], weights, total, jnp.bfloat16)


def solution(mesh):
    return jax.shard_map(
        per_device,
        mesh=mesh,
        in_specs=(P("ctx", "head"), P("ctx", "head"), P("ctx", "head"), P(None, "head")),
        out_specs=P("ctx", "head"),
        check_vma=False,
    )
```

```python
import math

import jax
import jax.numpy as jnp
from jax import lax
from jax.experimental import pallas as pl
from jax.experimental.pallas import tpu as pltpu
from jax.sharding import PartitionSpec as P

DH = 128
QPK = 4
SCALE2 = math.log2(math.e) * DH ** (-0.5)
NEG = -1e30

NZ, NY, NC = 4, 4, 2
NH, NX = 2, 4

TILE = 512
BESIDE = 2
PIECE = 512
ONES = 16
ROOM = 100.0


def ctx_id(z, y, c):
    return (z * NY + y) * NC + c


def ctx_permute(x, target):
    pairs = []
    for z in range(NZ):
        for y in range(NY):
            for c in range(NC):
                to = target(z, y, c)
                if to is not None:
                    pairs.append((ctx_id(z, y, c), ctx_id(*to)))
    return lax.ppermute(x, "ctx", pairs)


def head_permute(x, dz, partner):
    pairs = [(h * NX + i, (h + dz) % NH * NX + partner(i)) for h in range(NH) for i in range(NX)]
    return lax.ppermute(x, "head", pairs)


ONE = lambda i: i ^ 1
OTHER = lambda i: 3 - i
ACROSS = lambda i: (i + 2) % 4


def load_kv(blocks, keys, values):
    at = 0
    for block in blocks:
        for i in range(0, block.shape[0], DH):
            keys[at : at + DH, :] = block[i : i + DH, :DH]
            values[:DH, at : at + DH] = block[i : i + DH, DH:]
            at += DH
    values[DH:, :at] = jnp.ones((ONES, at), jnp.bfloat16)
    return at


def sweep(slots, length, scores, *ways):
    per = length // TILE

    def turn(i, _):
        def place(u):
            j = i * BESIDE + u
            return slots[0] + j // per, pl.multiple_of(j % per * TILE, TILE)

        def go(rest):
            s = scores(*place(0))
            for u in range(BESIDE):
                after = scores(*place(u + 1)) if u + 1 < BESIDE else None
                rest(*place(u), s)
                s = after

        for way in ways:
            if isinstance(way, tuple):
                pl.when(way[0](place(0)[0]))(lambda rest=way[1]: go(rest))
            else:
                go(way)
        return 0

    lax.fori_loop(0, (slots[1] - slots[0]) * per // BESIDE, turn, 0)


def scores_of(q, keys, count):
    def scores(slot, r):
        rows = q[slot, :, pl.ds(r, TILE)]
        return [
            jnp.dot(keys[k : k + PIECE, :], rows, preferred_element_type=jnp.float32) * SCALE2
            for k in range(0, count, PIECE)
        ]

    return scores


def weigh(values, s, m, kept=None):
    total = None
    for k, one in enumerate(s):
        p = jnp.exp2(one - m[:1]).astype(jnp.bfloat16)
        o = jnp.dot(
            values[:, k * PIECE : (k + 1) * PIECE], p, preferred_element_type=jnp.float32
        )
        if kept is not None:
            o = jnp.where(kept[k], o, 0.0)
        total = o if total is None else total + o
    return total


def update(q, keys, values, count, m_in, acc_in, m_out, acc_out, kept=None):
    scores = scores_of(q, keys, count)
    squares = jnp.dot(
        keys[:count, :] * keys[:count, :], jnp.ones((DH, DH), jnp.bfloat16), preferred_element_type=jnp.float32
    )
    longest = jnp.sqrt(jnp.max(squares, axis=0, keepdims=True))[:, :1] * (1.02 * SCALE2)
    near = []
    for t in range(2):
        over = None
        for slot in range(t * QPK, (t + 1) * QPK):
            reach = m_in[slot, 1:2, :] * longest - m_in[slot, :1, :]
            over = reach if over is None else jnp.maximum(over, reach)
        near.append(jnp.max(over) < ROOM)
    near_at = lambda slot: jnp.where(slot < QPK, near[0], near[1])

    def stay(slot, r, s):
        rows = pl.ds(r, TILE)
        m = m_in[slot, :, rows]
        m_out[slot, :, rows] = m
        acc_out[slot, :, rows] = acc_in[slot, :, rows] + weigh(values, s, m, kept)

    def move(slot, r, s):
        rows = pl.ds(r, TILE)
        m_old = m_in[slot, :, rows]
        m = m_old[:1]
        for k, one in enumerate(s):
            top = jnp.max(one, axis=0, keepdims=True)
            m = jnp.maximum(m, top if kept is None else jnp.where(kept[k], top, NEG))
        shrink = jnp.exp2(m_old[:1] - m)
        m_out[slot, :, rows] = jnp.concatenate([m, m_old[1:]], axis=0)
        acc_out[slot, :, rows] = acc_in[slot, :, rows] * shrink + weigh(values, s, m, kept)

    sweep(
        (0, 2 * QPK), q.shape[2], scores, (near_at, stay), (lambda slot: jnp.logical_not(near_at(slot)), move)
    )


def own_kernel(info, q, own, m_out, acc_out, keys, values):
    n = own.shape[0]
    count = load_kv((own,), keys, values)
    plain = scores_of(q, keys, count)

    def masked(slot, r):
        s = plain(slot, r)
        i = r + lax.broadcasted_iota(jnp.int32, (PIECE, TILE), 1)
        j = lax.broadcasted_iota(jnp.int32, (PIECE, TILE), 0)
        return [jnp.where(j + k * PIECE <= i, one, NEG) for k, one in enumerate(s)]

    def rest(slot, r, s):
        rows = pl.ds(r, TILE)
        m = jnp.max(s[0], axis=0, keepdims=True)
        for one in s[1:]:
            m = jnp.maximum(m, jnp.max(one, axis=0, keepdims=True))
        m_out[slot, :1, rows] = m
        acc_out[slot, :, rows] = weigh(values, s, m)

    sweep((0, QPK), n, masked, rest)

    @pl.when(info[0] == 0)
    def _():
        sweep((QPK, 2 * QPK), n, plain, rest)

    @pl.when(info[0] != 0)
    def _():
        m_out[QPK:, :1, :] = jnp.full((QPK, 1, n), NEG, jnp.float32)
        acc_out[QPK:] = jnp.zeros((QPK, DH + ONES, n), jnp.float32)

    for slot in range(2 * QPK):
        rows = q[slot].astype(jnp.float32)
        length = jnp.sqrt(jnp.sum(rows * rows, axis=0, keepdims=True))
        m_out[slot, 1:, :] = jnp.broadcast_to(length, (7, n))


def row_kernel(info, q, one_ref, other_ref, m_in, acc_in, m_out, acc_out, keys, values):
    y = info[1]

    @pl.when(y == 0)
    def _():
        m_out[...] = m_in[...]
        acc_out[...] = acc_in[...]

    @pl.when(y != 0)
    def _():
        count = load_kv((one_ref, other_ref), keys, values)
        per = one_ref.shape[0] // PIECE
        kept = [(y == 1) | (y == 3)] * per + [y >= 2] * per
        update(q, keys, values, count, m_in, acc_in, m_out, acc_out, kept)


def near_kernel(info, q, *refs):
    blocks, (m_in, acc_in, m_out, acc_out, keys, values) = refs[:-6], refs[-6:]
    below, before = info[2] >= 1, info[1] >= 2

    @pl.when(jnp.logical_not(below | before))
    def _():
        m_out[...] = m_in[...]
        acc_out[...] = acc_in[...]

    @pl.when(below | before)
    def _():
        count = load_kv(blocks, keys, values)
        per = blocks[0].shape[0] // PIECE
        kept = [below] * (4 * per) + [before] * per
        update(q, keys, values, count, m_in, acc_in, m_out, acc_out, kept)


def plane_kernel(least, parts, info, q, *refs):
    blocks, (m_in, acc_in, m_out, acc_out, keys, values) = refs[:-6], refs[-6:]
    z = info[2]

    @pl.when(z < least)
    def _():
        m_out[...] = m_in[...]
        acc_out[...] = acc_in[...]

    @pl.when(z >= least)
    def _():
        used = [b.at[start : start + n] for b, (start, n) in zip(blocks, parts)]
        count = load_kv(used, keys, values)
        update(q, keys, values, count, m_in, acc_in, m_out, acc_out)


def share_kernel(m, acc, own_out, own_log, send):
    rows = own_out.shape[1]
    parts = []
    for slot in range(2 * QPK):
        t, h = slot // QPK, slot % QPK
        total = acc[slot, DH : DH + 1, :]
        some = total > 0.0
        total = jnp.where(some, total, 1.0)
        o = acc[slot, :DH, :] / total
        log_total = jnp.where(some, m[slot, :1, :] + jnp.log2(total), NEG)
        columns = slice(h * DH, (h + 1) * DH)
        if t == 0:
            own_out[columns, :] = o
            own_log[h : h + 1, :] = log_total
        else:
            send[columns, :] = o.astype(jnp.bfloat16)
            for _ in range(3):
                parts.append(log_total.astype(jnp.bfloat16).astype(jnp.float32))
                log_total = log_total - parts[-1]
    parts += [jnp.zeros((1, rows), jnp.float32)] * (ONES - len(parts))
    send[QPK * DH :, :] = jnp.concatenate(parts, axis=0).astype(jnp.bfloat16)


def join_kernel(own_in, own_log, got, top_out, low_out):
    theirs = got[QPK * DH :, :].astype(jnp.float32)
    for h in range(QPK):
        a = own_log[h : h + 1, :]
        b = theirs[3 * h : 3 * h + 1, :] + theirs[3 * h + 1 : 3 * h + 2, :] + theirs[3 * h + 2 : 3 * h + 3, :]
        top = jnp.maximum(a, b)
        a, b = jnp.exp2(a - top), jnp.exp2(b - top)
        share = 1.0 / (a + b)
        columns = slice(h * DH, (h + 1) * DH)
        o = own_in[columns, :] * (a * share) + got[columns, :].astype(jnp.float32) * (b * share)
        o = o.T.astype(jnp.bfloat16)
        half = top_out.shape[0]
        top_out[:, columns] = o[:half]
        low_out[:, columns] = o[half:]


VM = pl.BlockSpec(memory_space=pltpu.VMEM)
SM = pl.BlockSpec(memory_space=pltpu.SMEM)


def call(kernel, out_shape, *args, info=None, flops=0, scratch=()):
    size = sum(a.size * a.dtype.itemsize for a in args)
    many = isinstance(out_shape, tuple)
    first = [] if info is None else [info]
    return pl.pallas_call(
        kernel,
        out_shape=out_shape,
        in_specs=[SM] * len(first) + [VM] * len(args),
        out_specs=tuple(VM for _ in out_shape) if many else VM,
        scratch_shapes=scratch,
        cost_estimate=pl.CostEstimate(flops=flops, bytes_accessed=size, transcendentals=0),
        compiler_params=pltpu.CompilerParams(vmem_limit_bytes=22 * 2**20),
    )(*first, *args)


def arrange(order, out_weight, depth):
    count = out_weight.shape[0] // depth

    def kernel(order_ref, w_ref, out, sems):
        copies = []
        for k in range(count):
            start = pl.multiple_of(order_ref[k] * depth, depth)
            copies.append(
                pltpu.make_async_copy(
                    w_ref.at[pl.ds(start, depth), :], out.at[pl.ds(k * depth, depth), :], sems.at[k]
                )
            )
            copies[-1].start()
        for copy in copies:
            copy.wait()

    return pl.pallas_call(
        kernel,
        out_shape=jax.ShapeDtypeStruct(out_weight.shape, out_weight.dtype),
        in_specs=[SM, pl.BlockSpec(memory_space=pltpu.HBM)],
        out_specs=VM,
        scratch_shapes=[pltpu.SemaphoreType.DMA((count,))],
        compiler_params=pltpu.CompilerParams(vmem_limit_bytes=22 * 2**20),
    )(order, out_weight)


def project(first, pieces, weights, so_far, out_type):
    refs = [block for piece in pieces for block in piece]
    counts = [len(piece) for piece in pieces]
    rows, depth = sum(b.shape[0] for b in pieces[0]), pieces[0][0].shape[1]
    columns = weights.shape[1]

    def kernel(*args):
        parts, w_ref = args[: len(refs)], args[len(refs)]
        before = args[len(refs) + 1] if so_far is not None else None
        out, total = args[-2:]
        at_ref = 0
        for k, count in enumerate(counts):
            start = 0
            for block in parts[at_ref : at_ref + count]:
                at = slice(start, start + block.shape[0])
                start += block.shape[0]
                w = w_ref[(first + k) * depth : (first + k + 1) * depth, :]
                o = jnp.dot(block[...], w, preferred_element_type=jnp.float32)
                if k > 0:
                    o = total[at, :] + o
                elif before is not None:
                    o = before[at, :] + o
                if k == len(counts) - 1:
                    out[at, :] = o.astype(out_type)
                else:
                    total[at, :] = o
            at_ref += count

    inputs = refs + [weights] + ([so_far] if so_far is not None else [])
    return pl.pallas_call(
        kernel,
        out_shape=jax.ShapeDtypeStruct((rows, columns), out_type),
        in_specs=[VM] * len(inputs),
        out_specs=VM,
        scratch_shapes=[pltpu.VMEM((rows, columns), jnp.float32)],
        cost_estimate=pl.CostEstimate(
            flops=2 * rows * depth * columns * len(pieces),
            bytes_accessed=len(pieces) * depth * (columns + rows) * 2,
            transcendentals=0,
        ),
        compiler_params=pltpu.CompilerParams(vmem_limit_bytes=22 * 2**20),
    )(*inputs)


def swap_y(x, partner, low=0):
    return ctx_permute(x, lambda z, y, c: (z, partner(y), c) if z >= low else None)


def ring_y(x, low):
    return [swap_y(x, partner, low) for partner in (ONE, OTHER, ACROSS)]


def per_device(queries, keys, values, out_weight):
    rows = queries.shape[0]
    ctx = lax.axis_index("ctx")
    head = lax.axis_index("head")
    z, y, c = ctx // (NY * NC), ctx // NC % NY, ctx % NC
    i32 = lambda *v: jnp.stack([jnp.asarray(x, jnp.int32) for x in v])
    info = i32(c, y, z)
    swap = lambda z, y, c: (z, y, 1 - c)

    squares = values.reshape(rows // DH, DH, DH).transpose(0, 2, 1).reshape(rows, DH)
    kv, queries = lax.optimization_barrier((jnp.concatenate([keys, squares], axis=1), queries))
    q_own = queries.T.reshape(QPK, DH, rows)
    q = jnp.concatenate([q_own, ctx_permute(q_own, swap)], axis=0)
    lift = lambda x, d: ctx_permute(x, lambda z, y, c: (z + d, y, c) if z + d < NZ else None)
    unit = 2 * 2 * 2 * QPK * rows * rows * DH
    state = (
        jax.ShapeDtypeStruct((2 * QPK, 8, rows), jnp.float32),
        jax.ShapeDtypeStruct((2 * QPK, DH + ONES, rows), jnp.float32),
    )

    def attend(kernel, chunks, *args):
        return call(
            kernel,
            state,
            *args,
            info=info,
            flops=chunks * unit,
            scratch=[
                pltpu.VMEM((chunks * rows, DH), jnp.bfloat16),
                pltpu.VMEM((DH + ONES, chunks * rows), jnp.bfloat16),
            ],
        )

    def planes(least, blocks, starts, m, acc):
        parts = [(start, rows) for start in starts]
        return attend(lambda *refs: plane_kernel(least, parts, *refs), len(parts), q, *blocks, m, acc)

    hz, hx = head // NX, head % NX
    along = (hx, hx + 1 - hx % 2 * 2, 3 - hx, (hx + 2) % NX)
    order = [h * NX + i for h in (hz, 1 - hz) for i in along]
    below = lift(kv, 1)
    late, q = lax.optimization_barrier((kv, q))
    row = ring_y(late, 0)
    m, acc = attend(own_kernel, 1, q, kv)
    below, m = lax.optimization_barrier((below, m))
    lower = [lift(below, 1), lift(below, 2)]
    m, acc = attend(row_kernel, 2, q, *row[:2], m, acc)
    near, m, row[2] = lax.optimization_barrier((below, m, row[2]))
    near = [near, *ring_y(near, 1), row[2]]
    both = jnp.concatenate(lower, axis=0)
    one, other, across = ring_y(both, 2)
    near[0], both = lax.optimization_barrier((near[0], both))
    m, acc = attend(near_kernel, 5, q, *near, m, acc)
    m, acc = planes(2, [both], [0], m, acc)
    m, acc = planes(3, [both], [rows], m, acc)
    m, order = lax.optimization_barrier((m, i32(*order)))
    weights = arrange(order, out_weight, QPK * DH)
    m, weights = lax.optimization_barrier((m, weights))
    m, acc = planes(2, [one, other, across], [0] * 3, m, acc)
    m, acc = planes(3, [one, other, across], [rows] * 3, m, acc)
    own, own_log, send = call(
        share_kernel,
        (
            jax.ShapeDtypeStruct((QPK * DH, rows), jnp.float32),
            jax.ShapeDtypeStruct((8, rows), jnp.float32),
            jax.ShapeDtypeStruct((QPK * DH + ONES, rows), jnp.bfloat16),
        ),
        m, acc,
    )
    attended = call(
        join_kernel,
        (jax.ShapeDtypeStruct((rows // 2, QPK * DH), jnp.bfloat16),) * 2,
        own, own_log, ctx_permute(send, swap),
    )

    def ring_x(halves):
        one = [head_permute(a, 0, ONE) for a in halves]
        other = [head_permute(a, 0, OTHER) for a in halves]
        return one, other, [head_permute(one[0], 0, OTHER), head_permute(other[1], 0, ONE)]

    one, other, across = ring_x(attended)
    low, one[1] = lax.optimization_barrier((attended[1], one[1]))
    far = [head_permute(a, 1, lambda i: i) for a in (attended[0], low)]
    far_one, far_other, far_across = ring_x(far)
    total = project(0, [attended, one, other], weights, None, jnp.float32)
    far_one[1], far_other[0], total = lax.optimization_barrier((far_one[1], far_other[0], total))
    total = project(3, [across, far, far_one, far_other], weights, total, jnp.float32)
    return project(7, [far_across], weights, total, jnp.bfloat16)


def solution(mesh):
    return jax.shard_map(
        per_device,
        mesh=mesh,
        in_specs=(P("ctx", "head"), P("ctx", "head"), P("ctx", "head"), P(None, "head")),
        out_specs=P("ctx", "head"),
        check_vma=False,
    )
```

```python
import math

import jax
import jax.numpy as jnp
from jax import lax
from jax.experimental import pallas as pl
from jax.experimental.pallas import tpu as pltpu
from jax.sharding import PartitionSpec as P

DH = 128
QPK = 4
SCALE2 = math.log2(math.e) * DH ** (-0.5)
NEG = -1e30

NZ, NY, NC = 4, 4, 2
NH, NX = 2, 4

TILE = 512
BESIDE = 2
PIECE = 512
ONES = 16
ROOM = 100.0


def ctx_id(z, y, c):
    return (z * NY + y) * NC + c


def ctx_permute(x, target):
    pairs = []
    for z in range(NZ):
        for y in range(NY):
            for c in range(NC):
                to = target(z, y, c)
                if to is not None:
                    pairs.append((ctx_id(z, y, c), ctx_id(*to)))
    return lax.ppermute(x, "ctx", pairs)


def head_permute(x, dz, partner):
    pairs = [(h * NX + i, (h + dz) % NH * NX + partner(i)) for h in range(NH) for i in range(NX)]
    return lax.ppermute(x, "head", pairs)


ONE = lambda i: i ^ 1
OTHER = lambda i: 3 - i
ACROSS = lambda i: (i + 2) % 4


def load_kv(blocks, keys, values):
    at = 0
    for block in blocks:
        for i in range(0, block.shape[0], DH):
            keys[at : at + DH, :] = block[i : i + DH, :DH]
            values[:DH, at : at + DH] = block[i : i + DH, DH:]
            at += DH
    values[DH:, :at] = jnp.ones((ONES, at), jnp.bfloat16)
    return at


def sweep(slots, length, scores, *ways):
    per = length // TILE

    def turn(i, _):
        def place(u):
            j = i * BESIDE + u
            return slots[0] + j // per, pl.multiple_of(j % per * TILE, TILE)

        def go(rest):
            s = scores(*place(0))
            for u in range(BESIDE):
                after = scores(*place(u + 1)) if u + 1 < BESIDE else None
                rest(*place(u), s)
                s = after

        for way in ways:
            if isinstance(way, tuple):
                pl.when(way[0](place(0)[0]))(lambda rest=way[1]: go(rest))
            else:
                go(way)
        return 0

    lax.fori_loop(0, (slots[1] - slots[0]) * per // BESIDE, turn, 0)


def scores_of(q, keys, count):
    def scores(slot, r):
        rows = q[slot, :, pl.ds(r, TILE)]
        return [
            jnp.dot(keys[k : k + PIECE, :], rows, preferred_element_type=jnp.float32) * SCALE2
            for k in range(0, count, PIECE)
        ]

    return scores


def weigh(values, s, m, kept=None):
    total = None
    for k, one in enumerate(s):
        p = jnp.exp2(one - m[:1]).astype(jnp.bfloat16)
        o = jnp.dot(
            values[:, k * PIECE : (k + 1) * PIECE], p, preferred_element_type=jnp.float32
        )
        if kept is not None:
            o = jnp.where(kept[k], o, 0.0)
        total = o if total is None else total + o
    return total


def update(q, keys, values, count, m_in, acc_in, m_out, acc_out, kept=None):
    scores = scores_of(q, keys, count)
    squares = jnp.dot(
        keys[:count, :] * keys[:count, :], jnp.ones((DH, DH), jnp.bfloat16), preferred_element_type=jnp.float32
    )
    longest = jnp.sqrt(jnp.max(squares, axis=0, keepdims=True))[:, :1] * (1.02 * SCALE2)
    near = []
    for t in range(2):
        over = None
        for slot in range(t * QPK, (t + 1) * QPK):
            reach = m_in[slot, 1:2, :] * longest - m_in[slot, :1, :]
            over = reach if over is None else jnp.maximum(over, reach)
        near.append(jnp.max(over) < ROOM)
    near_at = lambda slot: jnp.where(slot < QPK, near[0], near[1])

    def stay(slot, r, s):
        rows = pl.ds(r, TILE)
        m = m_in[slot, :, rows]
        m_out[slot, :, rows] = m
        acc_out[slot, :, rows] = acc_in[slot, :, rows] + weigh(values, s, m, kept)

    def move(slot, r, s):
        rows = pl.ds(r, TILE)
        m_old = m_in[slot, :, rows]
        m = m_old[:1]
        for k, one in enumerate(s):
            top = jnp.max(one, axis=0, keepdims=True)
            m = jnp.maximum(m, top if kept is None else jnp.where(kept[k], top, NEG))
        shrink = jnp.exp2(m_old[:1] - m)
        m_out[slot, :, rows] = jnp.concatenate([m, m_old[1:]], axis=0)
        acc_out[slot, :, rows] = acc_in[slot, :, rows] * shrink + weigh(values, s, m, kept)

    sweep(
        (0, 2 * QPK), q.shape[2], scores, (near_at, stay), (lambda slot: jnp.logical_not(near_at(slot)), move)
    )


def own_kernel(info, q, own, m_out, acc_out, keys, values):
    n = own.shape[0]
    count = load_kv((own,), keys, values)
    plain = scores_of(q, keys, count)

    def masked(slot, r):
        s = plain(slot, r)
        i = r + lax.broadcasted_iota(jnp.int32, (PIECE, TILE), 1)
        j = lax.broadcasted_iota(jnp.int32, (PIECE, TILE), 0)
        return [jnp.where(j + k * PIECE <= i, one, NEG) for k, one in enumerate(s)]

    def rest(slot, r, s):
        rows = pl.ds(r, TILE)
        m = jnp.max(s[0], axis=0, keepdims=True)
        for one in s[1:]:
            m = jnp.maximum(m, jnp.max(one, axis=0, keepdims=True))
        m_out[slot, :1, rows] = m
        acc_out[slot, :, rows] = weigh(values, s, m)

    sweep((0, QPK), n, masked, rest)

    @pl.when(info[0] == 0)
    def _():
        sweep((QPK, 2 * QPK), n, plain, rest)

    @pl.when(info[0] != 0)
    def _():
        m_out[QPK:, :1, :] = jnp.full((QPK, 1, n), NEG, jnp.float32)
        acc_out[QPK:] = jnp.zeros((QPK, DH + ONES, n), jnp.float32)

    for slot in range(2 * QPK):
        rows = q[slot].astype(jnp.float32)
        length = jnp.sqrt(jnp.sum(rows * rows, axis=0, keepdims=True))
        m_out[slot, 1:, :] = jnp.broadcast_to(length, (7, n))


def row_kernel(info, q, one_ref, other_ref, m_in, acc_in, m_out, acc_out, keys, values):
    y = info[1]

    @pl.when(y == 0)
    def _():
        m_out[...] = m_in[...]
        acc_out[...] = acc_in[...]

    @pl.when(y != 0)
    def _():
        count = load_kv((one_ref, other_ref), keys, values)
        per = one_ref.shape[0] // PIECE
        kept = [(y == 1) | (y == 3)] * per + [y >= 2] * per
        update(q, keys, values, count, m_in, acc_in, m_out, acc_out, kept)


def near_kernel(info, q, *refs):
    blocks, (m_in, acc_in, m_out, acc_out, keys, values) = refs[:-6], refs[-6:]
    below, before = info[2] >= 1, info[1] >= 2

    @pl.when(jnp.logical_not(below | before))
    def _():
        m_out[...] = m_in[...]
        acc_out[...] = acc_in[...]

    @pl.when(below | before)
    def _():
        count = load_kv(blocks, keys, values)
        per = blocks[0].shape[0] // PIECE
        kept = [below] * (4 * per) + [before] * per
        update(q, keys, values, count, m_in, acc_in, m_out, acc_out, kept)


def plane_kernel(least, parts, info, q, *refs):
    blocks, (m_in, acc_in, m_out, acc_out, keys, values) = refs[:-6], refs[-6:]
    z = info[2]

    @pl.when(z < least)
    def _():
        m_out[...] = m_in[...]
        acc_out[...] = acc_in[...]

    @pl.when(z >= least)
    def _():
        used = [b.at[start : start + n] for b, (start, n) in zip(blocks, parts)]
        count = load_kv(used, keys, values)
        update(q, keys, values, count, m_in, acc_in, m_out, acc_out)


def share_kernel(m, acc, own_out, own_log, send):
    rows = own_out.shape[1]
    parts = []
    for slot in range(2 * QPK):
        t, h = slot // QPK, slot % QPK
        total = acc[slot, DH : DH + 1, :]
        some = total > 0.0
        total = jnp.where(some, total, 1.0)
        o = acc[slot, :DH, :] / total
        log_total = jnp.where(some, m[slot, :1, :] + jnp.log2(total), NEG)
        columns = slice(h * DH, (h + 1) * DH)
        if t == 0:
            own_out[columns, :] = o
            own_log[h : h + 1, :] = log_total
        else:
            send[columns, :] = o.astype(jnp.bfloat16)
            for _ in range(3):
                parts.append(log_total.astype(jnp.bfloat16).astype(jnp.float32))
                log_total = log_total - parts[-1]
    parts += [jnp.zeros((1, rows), jnp.float32)] * (ONES - len(parts))
    send[QPK * DH :, :] = jnp.concatenate(parts, axis=0).astype(jnp.bfloat16)


def join_kernel(own_in, own_log, got, top_out, low_out):
    theirs = got[QPK * DH :, :].astype(jnp.float32)
    for h in range(QPK):
        a = own_log[h : h + 1, :]
        b = theirs[3 * h : 3 * h + 1, :] + theirs[3 * h + 1 : 3 * h + 2, :] + theirs[3 * h + 2 : 3 * h + 3, :]
        top = jnp.maximum(a, b)
        a, b = jnp.exp2(a - top), jnp.exp2(b - top)
        share = 1.0 / (a + b)
        columns = slice(h * DH, (h + 1) * DH)
        o = own_in[columns, :] * (a * share) + got[columns, :].astype(jnp.float32) * (b * share)
        o = o.T.astype(jnp.bfloat16)
        half = top_out.shape[0]
        top_out[:, columns] = o[:half]
        low_out[:, columns] = o[half:]


VM = pl.BlockSpec(memory_space=pltpu.VMEM)
SM = pl.BlockSpec(memory_space=pltpu.SMEM)


def call(kernel, out_shape, *args, info=None, flops=0, scratch=()):
    size = sum(a.size * a.dtype.itemsize for a in args)
    many = isinstance(out_shape, tuple)
    first = [] if info is None else [info]
    return pl.pallas_call(
        kernel,
        out_shape=out_shape,
        in_specs=[SM] * len(first) + [VM] * len(args),
        out_specs=tuple(VM for _ in out_shape) if many else VM,
        scratch_shapes=scratch,
        cost_estimate=pl.CostEstimate(flops=flops, bytes_accessed=size, transcendentals=0),
        compiler_params=pltpu.CompilerParams(vmem_limit_bytes=22 * 2**20),
    )(*first, *args)


def arrange(order, out_weight, depth):
    count = out_weight.shape[0] // depth

    def kernel(order_ref, w_ref, out, sems):
        copies = []
        for k in range(count):
            start = pl.multiple_of(order_ref[k] * depth, depth)
            copies.append(
                pltpu.make_async_copy(
                    w_ref.at[pl.ds(start, depth), :], out.at[pl.ds(k * depth, depth), :], sems.at[k]
                )
            )
            copies[-1].start()
        for copy in copies:
            copy.wait()

    return pl.pallas_call(
        kernel,
        out_shape=jax.ShapeDtypeStruct(out_weight.shape, out_weight.dtype),
        in_specs=[SM, pl.BlockSpec(memory_space=pltpu.HBM)],
        out_specs=VM,
        scratch_shapes=[pltpu.SemaphoreType.DMA((count,))],
        compiler_params=pltpu.CompilerParams(vmem_limit_bytes=22 * 2**20),
    )(order, out_weight)


def project(first, pieces, weights, so_far, out_type):
    refs = [block for piece in pieces for block in piece]
    counts = [len(piece) for piece in pieces]
    rows, depth = sum(b.shape[0] for b in pieces[0]), pieces[0][0].shape[1]
    columns = weights.shape[1]

    def kernel(*args):
        parts, w_ref = args[: len(refs)], args[len(refs)]
        before = args[len(refs) + 1] if so_far is not None else None
        out, total = args[-2:]
        at_ref = 0
        for k, count in enumerate(counts):
            start = 0
            for block in parts[at_ref : at_ref + count]:
                at = slice(start, start + block.shape[0])
                start += block.shape[0]
                w = w_ref[(first + k) * depth : (first + k + 1) * depth, :]
                o = jnp.dot(block[...], w, preferred_element_type=jnp.float32)
                if k > 0:
                    o = total[at, :] + o
                elif before is not None:
                    o = before[at, :] + o
                if k == len(counts) - 1:
                    out[at, :] = o.astype(out_type)
                else:
                    total[at, :] = o
            at_ref += count

    inputs = refs + [weights] + ([so_far] if so_far is not None else [])
    return pl.pallas_call(
        kernel,
        out_shape=jax.ShapeDtypeStruct((rows, columns), out_type),
        in_specs=[VM] * len(inputs),
        out_specs=VM,
        scratch_shapes=[pltpu.VMEM((rows, columns), jnp.float32)],
        cost_estimate=pl.CostEstimate(
            flops=2 * rows * depth * columns * len(pieces),
            bytes_accessed=len(pieces) * depth * (columns + rows) * 2,
            transcendentals=0,
        ),
        compiler_params=pltpu.CompilerParams(vmem_limit_bytes=22 * 2**20),
    )(*inputs)


def swap_y(x, partner, low=0):
    return ctx_permute(x, lambda z, y, c: (z, partner(y), c) if z >= low else None)


def ring_y(x, low):
    return [swap_y(x, partner, low) for partner in (ONE, OTHER, ACROSS)]


def per_device(queries, keys, values, out_weight):
    rows = queries.shape[0]
    ctx = lax.axis_index("ctx")
    head = lax.axis_index("head")
    z, y, c = ctx // (NY * NC), ctx // NC % NY, ctx % NC
    i32 = lambda *v: jnp.stack([jnp.asarray(x, jnp.int32) for x in v])
    info = i32(c, y, z)
    swap = lambda z, y, c: (z, y, 1 - c)

    squares = values.reshape(rows // DH, DH, DH).transpose(0, 2, 1).reshape(rows, DH)
    kv, queries = lax.optimization_barrier((jnp.concatenate([keys, squares], axis=1), queries))
    q_own = queries.T.reshape(QPK, DH, rows)
    q = jnp.concatenate([q_own, ctx_permute(q_own, swap)], axis=0)
    lift = lambda x, d: ctx_permute(x, lambda z, y, c: (z + d, y, c) if z + d < NZ else None)
    unit = 2 * 2 * 2 * QPK * rows * rows * DH
    state = (
        jax.ShapeDtypeStruct((2 * QPK, 8, rows), jnp.float32),
        jax.ShapeDtypeStruct((2 * QPK, DH + ONES, rows), jnp.float32),
    )

    def attend(kernel, chunks, *args):
        return call(
            kernel,
            state,
            *args,
            info=info,
            flops=chunks * unit,
            scratch=[
                pltpu.VMEM((chunks * rows, DH), jnp.bfloat16),
                pltpu.VMEM((DH + ONES, chunks * rows), jnp.bfloat16),
            ],
        )

    def planes(least, blocks, starts, m, acc):
        parts = [(start, rows) for start in starts]
        return attend(lambda *refs: plane_kernel(least, parts, *refs), len(parts), q, *blocks, m, acc)

    hz, hx = head // NX, head % NX
    along = (hx, hx + 1 - hx % 2 * 2, 3 - hx, (hx + 2) % NX)
    order = [h * NX + i for h in (hz, 1 - hz) for i in along]
    below = lift(kv, 1)
    late, q = lax.optimization_barrier((kv, q))
    row = ring_y(late, 0)
    m, acc = attend(own_kernel, 1, q, kv)
    below, m = lax.optimization_barrier((below, m))
    lower = [lift(below, 1), lift(below, 2)]
    m, acc = attend(row_kernel, 2, q, *row[:2], m, acc)
    near, m, row[2] = lax.optimization_barrier((below, m, row[2]))
    near = [near, *ring_y(near, 1), row[2]]
    both = jnp.concatenate(lower, axis=0)
    one, other, across = ring_y(both, 2)
    near[0], both = lax.optimization_barrier((near[0], both))
    m, acc = attend(near_kernel, 5, q, *near, m, acc)
    m, acc = planes(2, [both], [0], m, acc)
    m, order = lax.optimization_barrier((m, i32(*order)))
    weights = arrange(order, out_weight, QPK * DH)
    m, weights = lax.optimization_barrier((m, weights))
    m, acc = planes(2, [one, other, across], [0] * 3, m, acc)
    m, acc = planes(3, [both, one, other, across], [rows] * 4, m, acc)
    own, own_log, send = call(
        share_kernel,
        (
            jax.ShapeDtypeStruct((QPK * DH, rows), jnp.float32),
            jax.ShapeDtypeStruct((8, rows), jnp.float32),
            jax.ShapeDtypeStruct((QPK * DH + ONES, rows), jnp.bfloat16),
        ),
        m, acc,
    )
    attended = call(
        join_kernel,
        (jax.ShapeDtypeStruct((rows // 2, QPK * DH), jnp.bfloat16),) * 2,
        own, own_log, ctx_permute(send, swap),
    )

    far = [head_permute(a, 1, lambda i: i) for a in attended]

    def ring_x(halves):
        one = [head_permute(a, 0, ONE) for a in halves]
        other = [head_permute(a, 0, OTHER) for a in halves]
        return one, other, [head_permute(one[0], 0, OTHER), head_permute(other[1], 0, ONE)]

    one, other, across = ring_x(attended)
    far_one, far_other, far_across = ring_x(far)
    total = project(0, [attended, one, other], weights, None, jnp.float32)
    far_one[1], far_other[0], total = lax.optimization_barrier((far_one[1], far_other[0], total))
    total = project(3, [across, far, far_one, far_other], weights, total, jnp.float32)
    return project(7, [far_across], weights, total, jnp.bfloat16)


def solution(mesh):
    return jax.shard_map(
        per_device,
        mesh=mesh,
        in_specs=(P("ctx", "head"), P("ctx", "head"), P("ctx", "head"), P(None, "head")),
        out_specs=P("ctx", "head"),
        check_vma=False,
    )
```
